128 devices in a mesh: wide: 16 (over z, y_hi, core), narrow: 8 (over x, y_lo).
Axes of the slice: x: 4, y: 4 (y_hi: 2, y_lo: 2; y = y_hi * 2 + y_lo), z: 4, core: 2. Of those that a mesh axis runs over, the one named last changes fastest.
Arguments:
- layer_input: bfloat16 [8192, 2560], P('wide', 'narrow'), may hold values from -6 to 6
- gain_attn: float32 [2560], P('narrow'), may hold values from 0.1 to 1.9
- w_query: bfloat16 [2560, 2560], P('wide', 'narrow'), may hold values from -0.125 to 0.125
- w_key: bfloat16 [2560, 640], P('wide', 'narrow'), may hold values from -0.125 to 0.125
- w_value: bfloat16 [2560, 640], P('wide', 'narrow'), may hold values from -0.125 to 0.125
- w_out: bfloat16 [2560, 2560], P('narrow', 'wide'), may hold values from -1.5 to 1.5
- gain_mlp: float32 [2560], P('narrow'), may hold values from 0.1 to 1.9
- w_gate: bfloat16 [2560, 7168], P('wide', 'narrow'), may hold values from -0.125 to 0.125
- w_up: bfloat16 [2560, 7168], P('wide', 'narrow'), may hold values from -0.125 to 0.125
- w_down: bfloat16 [7168, 2560], P('narrow', 'wide'), may hold values from -0.0625 to 0.0625
- doc_lengths: int32 [8], replicated, may hold values from 1 to 7968, as said below
- cotangent: bfloat16 [8192, 2560], P('wide', 'narrow'), may hold values from -6 to 6
Outputs:
- layer_output: bfloat16 [8192, 2560], P('wide', 'narrow')
- grad_input: float32 [8192, 2560], P('wide', 'narrow')
- grad_gain_attn: float32 [2560], P('narrow')
- grad_query: float32 [2560, 2560], P('wide', 'narrow')
- grad_key: float32 [2560, 640], P('wide', 'narrow')
- grad_value: float32 [2560, 640], P('wide', 'narrow')
- grad_out: float32 [2560, 2560], P('narrow', 'wide')
- grad_gain_mlp: float32 [2560], P('narrow')
- grad_gate: float32 [2560, 7168], P('wide', 'narrow')
- grad_up: float32 [2560, 7168], P('wide', 'narrow')
- grad_down: float32 [7168, 2560], P('narrow', 'wide')
The draws below stay inside these ranges and needn't reach their ends.
Inputs may be any that keep to these rules, and one draw needn't show every extreme that they name: `doc_lengths`: the 8 lengths sum to 8192. One document, at a place drawn from the seed, has exactly 7968 tokens; the others together have (7) * 32 tokens, each between 1 and 63, and one of them exactly 1.
All inputs are finite; a program needn't handle non-finite values.
Results may differ from the reference program's by a relative error of at most 0.019.
Values may be sent and summed in bfloat16 or wider, within the bound.
A program may use at most 192 MiB of HBM per device.

```python
import math
import jax
import jax.numpy as jnp
from jax import lax

D = 2560
HEADS = 32
KV_HEADS = 8
HEAD = 80
FF = 7168
WINDOW = 1024
DOCS = 8
TOKENS = 8192
SHORT_MEAN = 32


def draw_doc_lengths(key, part):
    key = jax.random.fold_in(key, 7)
    shift_key, place_key = jax.random.split(key)
    short_count = DOCS - 1
    shifts = jax.random.randint(shift_key, (short_count,), 0, SHORT_MEAN)
    slots = jnp.arange(short_count)
    shifts = jnp.where(slots == 0, SHORT_MEAN - 1, jnp.where(slots == short_count - 1, 0, shifts))
    shorts = SHORT_MEAN + shifts - jnp.roll(shifts, -1)
    longest = TOKENS - short_count * SHORT_MEAN
    placed = jax.random.randint(place_key, (), 0, DOCS)
    doc_slots = jnp.arange(DOCS)
    early_ones = shorts[jnp.clip(doc_slots, 0, DOCS - 2)]
    later_ones = shorts[jnp.clip(doc_slots - 1, 0, DOCS - 2)]
    chosen = jnp.where(doc_slots < placed, early_ones, jnp.where(doc_slots == placed, longest, later_ones))
    return chosen.astype(jnp.int32)


def raised(entries, rng, source, target, parts, factor):
    owner, partner = [(jnp.arange(entries.shape[dim]) // (entries.shape[dim] // parts)).reshape([-1 if axis == dim else 1 for axis in range(entries.ndim)]) for dim in (source, target)]
    chosen = jax.random.permutation(rng, parts)[partner]
    strong = (owner == chosen) | (owner == (partner + parts // 2) % parts)
    return jnp.where(strong, factor * entries, entries)


def block_scale(key, extent, cuts, least, high):
    factor_of, own = 1.0, jax.random.fold_in(key, 6)
    for dim, shards_of in cuts:
        steps = jnp.exp(jax.random.uniform(jax.random.fold_in(own, dim), (shards_of,), jnp.float32, least / len(cuts), high / len(cuts)))
        factor_of = factor_of * jnp.repeat(steps, extent[dim] // shards_of).reshape([-1 if axis == dim else 1 for axis in range(len(extent))])
    return factor_of


def scatter_about(rng, dims, scale, bound, cuts=(), kind=jnp.bfloat16):
    values = scale * jax.random.normal(rng, dims, jnp.float32)
    if cuts:
        values = values * block_scale(rng, dims, cuts, -0.22, 0.18)
    return jnp.clip(values, -bound, bound).astype(kind)


def heavy_noise(key, shape, width, limit, shards, heavy, held_as=jnp.bfloat16):
    values = width * jax.random.normal(key, shape, jnp.float32)
    if shards:
        values = values * block_scale(key, shape, shards, -0.22, 0.18)
    return jnp.clip(raised(values, jax.random.fold_in(key, 3), *heavy), -limit, limit).astype(held_as)


def setup_inputs(seed: int = 0) -> dict:
    arg_keys = jax.random.split(jax.random.key(seed), 13)
    return {
        "layer_input": scatter_about(arg_keys[0], (TOKENS, D), 1.0, 6.0, ((0, 16), (1, 8))),
        "gain_attn": jnp.clip(1.0 + 0.18 * jax.random.normal(arg_keys[1], (D,), jnp.float32), 0.1, 1.9),
        "w_query": scatter_about(arg_keys[2], (D, HEADS * HEAD), D ** -0.5, 0.125, ((0, 16), (1, 8))),
        "w_key": scatter_about(arg_keys[3], (D, KV_HEADS * HEAD), D ** -0.5, 0.125, ((0, 16), (1, 8))),
        "w_value": scatter_about(arg_keys[4], (D, KV_HEADS * HEAD), D ** -0.5, 0.125, ((0, 16), (1, 8))),
        "w_out": scatter_about(arg_keys[5], (HEADS * HEAD, D), 16 ** -0.5, 1.5, ((0, 8), (1, 16))),
        "gain_mlp": jnp.clip(1.0 + 0.18 * jax.random.normal(arg_keys[6], (D,), jnp.float32), 0.1, 1.9),
        "w_gate": scatter_about(arg_keys[7], (D, FF), D ** -0.5, 0.125, ((0, 16), (1, 8))),
        "w_up": scatter_about(arg_keys[8], (D, FF), D ** -0.5, 0.125, ((0, 16), (1, 8))),
        "w_down": scatter_about(arg_keys[9], (FF, D), FF ** -0.5, 0.0625, ((0, 8), (1, 16))),
        "doc_lengths": draw_doc_lengths(jax.random.fold_in(arg_keys[12], 71), 0),
        "cotangent": heavy_noise(arg_keys[11], (TOKENS, D), 1.0, 6.0, ((0, 16), (1, 8)), (0, 1, 16, 2.0)),
    }


highest = lax.Precision.HIGHEST
epsilon = 1e-05
rope_base = 1000000.0
rope_factor = 8.0
long_wave = 8192.0
short_wave = 2048.0
masked = -1e+30

@jax.custom_vjp
def low(v):
    return lax.optimization_barrier(v.astype(jnp.bfloat16)).astype(jnp.float32)

@jax.custom_vjp
def low_back(v):
    return v

def low_keep(v):
    return (low(v), None)

def low_pass(kept, grad):
    return (grad,)

def back_keep(v):
    return (v, None)

def back_low(kept, grad):
    return (low(grad),)
low.defvjp(low_keep, low_pass)
low_back.defvjp(back_keep, back_low)

def documents(doc_lengths, places):
    ends_at = jnp.cumsum(doc_lengths).astype(jnp.int32)
    passed = places[:, None] >= ends_at[None, :]
    segment = lax.optimization_barrier(jnp.sum(passed.astype(jnp.int32), axis=1)).astype(jnp.int32)
    begins = lax.optimization_barrier(jnp.sum(jnp.where(passed, doc_lengths[None, :], 0), axis=1)).astype(jnp.int32)
    return (segment, (places - begins).astype(jnp.int32))

def scaled_freqs():
    half_width = HEAD // 2
    freqs = rope_base ** (-2.0 * jnp.arange(half_width, dtype=jnp.float32) / HEAD)
    wavelen = 2.0 * math.pi / freqs
    smooth = (long_wave / wavelen - 1.0) / 3.0
    blended = (1.0 - smooth) * freqs / rope_factor + smooth * freqs
    return jnp.where(wavelen < short_wave, freqs, jnp.where(wavelen > long_wave, freqs / rope_factor, blended))

def rope_tables(position):
    freqs = scaled_freqs()
    angles = position.astype(jnp.float32)[:, None] * freqs[None, :]
    return (jnp.cos(angles), jnp.sin(angles))

def rotate(stacked, cosine, sine_table):
    half_width = stacked.shape[-1] // 2
    front_half = stacked[..., :half_width]
    back_half = stacked[..., half_width:]
    cos_rows = cosine[:, None, :]
    sin_rows = sine_table[:, None, :]
    return jnp.concatenate([front_half * cos_rows - back_half * sin_rows, back_half * cos_rows + front_half * sin_rows], axis=-1)

def rms_norm(stream, gain):
    inverse_rms = lax.rsqrt(lax.optimization_barrier(jnp.mean(stream * stream, axis=-1, keepdims=True)) + epsilon)
    return stream * inverse_rms * gain

def product(left, right):
    return jnp.dot(left, right, precision=highest)

def attention(queries, keys_all, values_all, segment):
    block_rows = math.gcd(TOKENS, 512)
    span = min(TOKENS, WINDOW + block_rows)
    per_group = HEADS // KV_HEADS
    blocks = queries.reshape(TOKENS // block_rows, block_rows, KV_HEADS, per_group, HEAD)
    starts = jnp.arange(TOKENS // block_rows, dtype=jnp.int32) * block_rows

    def one_block(packed):
        row_start, query_block = packed
        key_start = jnp.clip(row_start - WINDOW, 0, TOKENS - span).astype(jnp.int32)
        key_block = lax.dynamic_slice_in_dim(keys_all, key_start, span, 0)
        value_block = lax.dynamic_slice_in_dim(values_all, key_start, span, 0)
        query_index = row_start + jnp.arange(block_rows, dtype=jnp.int32)
        key_index = key_start + jnp.arange(span, dtype=jnp.int32)
        query_seg = lax.dynamic_slice_in_dim(segment, row_start, block_rows, 0)
        key_seg = lax.dynamic_slice_in_dim(segment, key_start, span, 0)
        visible = (query_seg[:, None] == key_seg[None, :]) & (key_index[None, :] <= query_index[:, None]) & (query_index[:, None] - key_index[None, :] < WINDOW)
        scores = low_back(jnp.einsum('tkgd,skd->kgts', query_block, key_block, precision=highest) * (1.0 / math.sqrt(HEAD)))
        scores = jnp.where(visible[None, None], scores, masked)
        largest = lax.optimization_barrier(jnp.max(scores, axis=-1, keepdims=True))
        powers = jnp.exp(scores - largest)
        weights = low(powers / lax.optimization_barrier(jnp.sum(powers, axis=-1, keepdims=True)))
        mixed = jnp.einsum('kgts,skd->tkgd', weights, value_block, precision=highest)
        return mixed.reshape(block_rows, HEADS * HEAD)
    results = lax.map(jax.checkpoint(one_block), (starts, blocks))
    return results.reshape(TOKENS, HEADS * HEAD)

def reference(layer_input, gain_attn, w_query, w_key, w_value, w_out, gain_mlp, w_gate, w_up, w_down, doc_lengths, cotangent):
    places = jnp.arange(TOKENS, dtype=jnp.int32)
    segment, position = documents(doc_lengths, places)
    cosine, sine_table = rope_tables(position)

    def layer(stream, gain_one, query_w, key_w, value_w, out_w, gain_two, gate_w, up_w, down_w):
        normed_one = low(rms_norm(stream, gain_one))
        query_pre = low_back(product(normed_one, query_w)).reshape(TOKENS, HEADS, HEAD)
        key_pre = low_back(product(normed_one, key_w)).reshape(TOKENS, KV_HEADS, HEAD)
        value_pre = low_back(product(normed_one, value_w)).reshape(TOKENS, KV_HEADS, HEAD)
        queries = low(rotate(query_pre, cosine, sine_table))
        keys_all = low(rotate(key_pre, cosine, sine_table))
        values_all = low(value_pre)
        attended = low(low_back(attention(queries, keys_all, values_all, segment)))
        midstream = stream + low_back(product(attended, out_w))
        normed_two = low(rms_norm(midstream, gain_two))
        gate_val = low_back(product(normed_two, gate_w))
        up_val = low_back(product(normed_two, up_w))
        hidden_act = low(jax.nn.silu(gate_val) * up_val)
        return midstream + low_back(product(hidden_act, down_w))
    params = tuple((item.astype(jnp.float32) for item in (layer_input, gain_attn, w_query, w_key, w_value, w_out, gain_mlp, w_gate, w_up, w_down)))
    result, pullback = jax.vjp(layer, *params)
    grads = pullback(cotangent.astype(jnp.float32))
    return (result.astype(jnp.bfloat16), grads[0], grads[1], grads[2], grads[3], grads[4], grads[5], grads[6], grads[7], grads[8], grads[9])
```

```python
import functools
import math

import jax
import jax.numpy as jnp
from jax import lax
from jax.experimental import pallas as pl
from jax.experimental.pallas import tpu as pltpu
from jax.sharding import PartitionSpec as P

D = 2560
HEADS = 32
KV_HEADS = 8
HEAD = 80
WINDOW = 1024
TOK = 512
OWN = 64
ROWS = 160
PANEL = 896

epsilon = 1e-05
rope_base = 1000000.0
rope_factor = 8.0
long_wave = 8192.0
short_wave = 2048.0
masked = -1e30

MESH = pl.DeviceIdType.MESH
BF = jnp.bfloat16
F32 = jnp.float32


class Place:
    def __init__(self):
        self.w = lax.axis_index("wide")
        self.n = lax.axis_index("narrow")
        self.z, self.h, self.c = self.w // 4, (self.w // 2) % 2, self.w % 2
        self.x, self.l = self.n // 2, self.n % 2

    def wide(self, dz, dh, dc):
        return ((self.z + dz) % 4) * 4 + ((self.h + dh) % 2) * 2 + (self.c + dc) % 2

    def narrow(self, dx, dl):
        return ((self.x + dx) % 4) * 2 + (self.l + dl) % 2

    def narrow_peers(self):
        return [(self.w, self.narrow(k // 2, k % 2)) for k in (2, 6, 1, 3, 7, 4, 5)]

    def wide_peers(self):
        return [(self.wide(*d), self.n) for d in ((0, 1, 0), (1, 0, 0), (3, 0, 0), (2, 0, 0), (0, 0, 1))]


class Net:
    def __init__(self, place, send_sems, recv_sems, local_sems):
        self.at = place
        self.sems = (send_sems, recv_sems, local_sems)
        self.sent, self.kept = [], []

    def barrier(self, givers, takers):
        bar = pltpu.get_barrier_semaphore()
        for device in givers:
            pl.semaphore_signal(bar, inc=1, device_id=device, device_id_type=MESH)
        pl.semaphore_wait(bar, takers)

    def send(self, src, dst, device):
        i = len(self.sent)
        copy = pltpu.make_async_remote_copy(
            src_ref=src,
            dst_ref=dst,
            send_sem=self.sems[0].at[i],
            recv_sem=self.sems[1].at[i],
            device_id=device,
            device_id_type=MESH,
        )
        copy.start()
        self.sent.append(copy)
        return copy

    def keep(self, src, dst):
        copy = pltpu.make_async_copy(src, dst, self.sems[2].at[len(self.kept)])
        copy.start()
        self.kept.append(copy)
        return copy

    def run(self, tasks):
        tasks = list(tasks)
        while tasks:
            left = []
            for task in tasks:
                try:
                    next(task)
                    left.append(task)
                except StopIteration:
                    pass
            tasks = left
        for copy in self.sent:
            copy.wait_send()
        for copy in self.kept:
            copy.wait()


def narrow_gather(net, src, dst):
    me = net.at.n
    copies = [net.send(src, dst.at[me], peer) for peer in net.at.narrow_peers()]
    net.keep(src, dst.at[me])
    yield
    yield
    yield
    for copy in copies:
        copy.wait_recv()


def narrow_swap(net, src, dst):
    me = net.at.n
    copies = [net.send(src.at[peer[1]], dst.at[me], peer) for peer in net.at.narrow_peers()]
    net.keep(src.at[me], dst.at[me])
    yield
    yield
    yield
    for copy in copies:
        copy.wait_recv()


def narrow_sum(net, src, slots, out):
    me = net.at.n
    copies = [
        net.send(src.at[peer[1]], slots.at[k], peer) for k, peer in enumerate(net.at.narrow_peers())
    ]
    yield
    yield
    yield
    for copy in copies:
        copy.wait_recv()

    @pl.loop(0, OWN // 16)
    def _(i):
        rows = pl.ds(pl.multiple_of(i * 16, 16), 16)
        total = src[me, rows, :].astype(F32)
        for k in range(7):
            total += slots[k, rows, :].astype(F32)
        out[rows, :] = total


def wide_gather(net, src, dst):
    at = net.at
    me, far = at.w, at.wide(0, 1, 0)
    net.keep(src, dst.at[me])
    from_far = net.send(src, dst.at[me], (far, at.n))
    turns = [(d, 0, net.send(src, dst.at[me], (at.wide(d, 0, 0), at.n))) for d in (1, 3, 2)]
    other = (at.wide(0, 0, 1), at.n)
    over = [net.send(src, dst.at[me], other)]
    yield
    from_far.wait_recv()
    turns += [(d, 1, net.send(dst.at[far], dst.at[far], (at.wide(d, 0, 0), at.n))) for d in (1, 3, 2)]
    over.append(net.send(dst.at[far], dst.at[far], other))
    yield
    for d, e, copy in turns:
        copy.wait_recv()
        block = at.wide(-d, e, 0)
        over.append(net.send(dst.at[block], dst.at[block], other))
    yield
    for copy in over:
        copy.wait_recv()


def wide_sum(net, src, half, turned, last, out):
    at = net.at
    other = (at.wide(0, 0, 1), at.n)
    over = [
        net.send(src.at[at.wide(d, e, 1)], half.at[d, e], other) for d in (1, 3, 2, 0) for e in (0, 1)
    ]
    yield
    turns = []
    k = 0
    for d in (1, 3, 2, 0):
        for e in (0, 1):
            over[k].wait_recv()
            k += 1
            block = at.wide(d, e, 0)

            @pl.loop(0, src.shape[1] // 32)
            def _(i):
                rows = pl.ds(pl.multiple_of(i * 32, 32), 32)
                src[block, rows, :] = (
                    src[block, rows, :].astype(F32) + half[d, e, rows, :].astype(F32)
                ).astype(BF)

            if d:
                turns.append(
                    (e, net.send(src.at[block], turned.at[d - 1, e], (at.wide(d, 0, 0), at.n)))
                )
    yield
    mine, far = at.w, at.wide(0, 1, 0)
    for _, copy in turns:
        copy.wait_recv()

    @pl.loop(0, src.shape[1] // 32)
    def _(i):
        rows = pl.ds(pl.multiple_of(i * 32, 32), 32)
        total = src[far, rows, :].astype(F32)
        for d in range(3):
            total += turned[d, 1, rows, :].astype(F32)
        src[far, rows, :] = total.astype(BF)

    final = net.send(src.at[far], last, (far, at.n))
    yield
    final.wait_recv()

    @pl.loop(0, src.shape[1] // 32)
    def _(i):
        rows = pl.ds(pl.multiple_of(i * 32, 32), 32)
        total = src[mine, rows, :].astype(F32) + last[rows, :].astype(F32)
        for d in range(3):
            total += turned[d, 0, rows, :].astype(F32)
        out[rows, :] = total


def wide_sum_scratch(columns):
    return [
        pltpu.VMEM((16, ROWS, columns), BF),
        pltpu.VMEM((4, 2, ROWS, columns), BF),
        pltpu.VMEM((3, 2, ROWS, columns), BF),
        pltpu.VMEM((ROWS, columns), BF),
    ]


def vmem():
    return pl.BlockSpec(memory_space=pltpu.VMEM)


def hbm():
    return pl.BlockSpec(memory_space=pl.ANY)


def exchange(name, number, body, ins, outs, scratch=(), sends=96, keeps=32):
    def kernel(*refs):
        a, b = len(ins), len(ins) + len(outs)
        net = Net(Place(), *refs[-3:])
        body(net, refs[:a], refs[a:b], refs[b:-3])

    return pl.pallas_call(
        kernel,
        out_shape=[jax.ShapeDtypeStruct(shape, dtype) for shape, dtype, _ in outs],
        in_specs=[spec for _, spec in ins],
        out_specs=[spec for _, _, spec in outs],
        scratch_shapes=[
            *scratch,
            pltpu.SemaphoreType.DMA((sends,)),
            pltpu.SemaphoreType.DMA((sends,)),
            pltpu.SemaphoreType.DMA((keeps,)),
        ],
        compiler_params=pltpu.CompilerParams(
            collective_id=number, has_side_effects=True, vmem_limit_bytes=56 * 2**20
        ),
        name=name,
    )(*[array for array, _ in ins])


def documents(doc_lengths, places):
    ends_at = jnp.cumsum(doc_lengths)
    passed = places[:, None] >= ends_at[None, :]
    segment = jnp.sum(passed.astype(jnp.int32), axis=1)
    begins = jnp.sum(jnp.where(passed, doc_lengths[None, :], 0), axis=1)
    return (segment, places - begins)


def scaled_freqs():
    half_width = HEAD // 2
    freqs = rope_base ** (-2.0 * jnp.arange(half_width, dtype=jnp.float32) / HEAD)
    wavelen = 2.0 * math.pi / freqs
    smooth = (long_wave / wavelen - 1.0) / 3.0
    blended = (1.0 - smooth) * freqs / rope_factor + smooth * freqs
    return jnp.where(
        wavelen < short_wave, freqs, jnp.where(wavelen > long_wave, freqs / rope_factor, blended)
    )


def rope_tables(position):
    freqs = scaled_freqs()
    angles = position.astype(jnp.float32)[:, None] * freqs[None, :]
    return (jnp.cos(angles), jnp.sin(angles))


def rotate(stacked, cosine, sine_table):
    half_width = stacked.shape[-1] // 2
    front_half = stacked[..., :half_width]
    back_half = stacked[..., half_width:]
    cos_rows = cosine[:, None, :]
    sin_rows = sine_table[:, None, :]
    return jnp.concatenate(
        [
            front_half * cos_rows - back_half * sin_rows,
            back_half * cos_rows + front_half * sin_rows,
        ],
        axis=-1,
    )


def unrotate(stacked, cosine, sine_table):
    return rotate(stacked, cosine, -sine_table)


def norm_rows(stream, gain):
    inverse_rms = lax.rsqrt(jnp.mean(stream * stream, axis=1, keepdims=True) + epsilon)
    return stream * inverse_rms * gain[None, :], inverse_rms


def norm_back(stream, inverse_rms, gain, upstream):
    weighted = upstream * gain[None, :]
    inner = jnp.sum(weighted * stream, axis=1, keepdims=True)
    through = inverse_rms * weighted - stream * (
        inverse_rms * inverse_rms * inverse_rms * inner / D
    )
    return (through, jnp.sum(upstream * stream * inverse_rms, axis=0))


def scores_of(queries, keys_here, visible):
    raw_scores = jnp.einsum(
        "tkgd,skd->kgts", queries, keys_here, preferred_element_type=jnp.float32
    ) * (1.0 / math.sqrt(HEAD))
    return jnp.where(visible[None, None], raw_scores, masked)


def attend(queries, keys_here, values_here, visible):
    scores = scores_of(queries, keys_here, visible)
    largest = jnp.max(scores, axis=-1, keepdims=True)
    powers = jnp.exp(scores - largest)
    totals = jnp.sum(powers, axis=-1, keepdims=True)
    weights = (powers / totals).astype(jnp.bfloat16)
    mixed = jnp.einsum("kgts,skd->tkgd", weights, values_here, preferred_element_type=jnp.float32)
    return (mixed, largest + jnp.log(totals))


def attend_back(queries, keys_here, values_here, visible, log_totals, upstream):
    weights = jnp.exp(scores_of(queries, keys_here, visible) - log_totals)
    upstream_prob = jnp.einsum(
        "tkgd,skd->kgts", upstream, values_here, preferred_element_type=jnp.float32
    )
    grad_scores = (
        weights * (upstream_prob - jnp.sum(weights * upstream_prob, axis=-1, keepdims=True))
    ).astype(jnp.bfloat16)
    factor = 1.0 / math.sqrt(HEAD)
    grad_queries = (
        jnp.einsum("kgts,skd->tkgd", grad_scores, keys_here, preferred_element_type=jnp.float32)
        * factor
    )
    grad_keys = (
        jnp.einsum("kgts,tkgd->skd", grad_scores, queries, preferred_element_type=jnp.float32)
        * factor
    )
    grad_values = jnp.einsum(
        "kgts,tkgd->skd", weights.astype(jnp.bfloat16), upstream, preferred_element_type=jnp.float32
    )
    return (grad_queries, grad_keys, grad_values)


def packed(block):
    return jnp.concatenate([block[: TOK // 2], block[TOK // 2 :]], axis=1)


def unpacked(pieces):
    return (
        pieces.reshape(8, TOK // 2, 2, D // 8).transpose(2, 1, 0, 3).reshape(TOK, D)
    )


def dot(a, b):
    return jnp.dot(a, b, preferred_element_type=F32)


def dot_t(a, b):
    return lax.dot_general(a, b, (((1,), (1,)), ((), ())), preferred_element_type=F32)


def t_dot(a, b):
    return lax.dot_general(a, b, (((0,), (0,)), ((), ())), preferred_element_type=F32)


def body(
    layer_input,
    gain_attn,
    w_query,
    w_key,
    w_value,
    w_out,
    gain_mlp,
    w_gate,
    w_up,
    w_down,
    doc_lengths,
    cotangent,
):
    q_width, kv_width, ff_width = 320, 80, 896
    per_group = HEADS // KV_HEADS
    me_n = lax.axis_index("narrow")
    me_w = lax.axis_index("wide")
    shard_a = jnp.concatenate(
        [w_query, w_key, w_value, jnp.zeros((ROWS, 32), BF), w_out.T, jnp.zeros((ROWS, 64), BF)],
        axis=1,
    )
    shard_d = w_down.T
    gains = jnp.zeros((8, 384), F32).at[0, :320].set(gain_attn).at[1, :320].set(gain_mlp)
    full = ((16, ROWS, PANEL), BF, hbm())

    def k1(net, ins, outs, scratch):
        at = net.at
        net.barrier(at.narrow_peers() + at.wide_peers(), 12)
        net.run(
            [
                narrow_gather(net, ins[2], outs[2]),
                narrow_gather(net, ins[0], outs[0]),
                wide_gather(net, ins[3], outs[3]),
                narrow_gather(net, ins[1], outs[1]),
                wide_gather(net, ins[4], outs[4]),
            ]
        )

    piece = ((8, TOK // 2, 640), BF, hbm())
    x_pieces, cot_pieces, gain_pieces, full_a, full_g = exchange(
        "gather_input",
        1,
        k1,
        [
            (packed(layer_input), hbm()),
            (packed(cotangent), hbm()),
            (gains, hbm()),
            (shard_a, hbm()),
            (w_gate, hbm()),
        ],
        [piece, piece, ((8, 8, 384), F32, hbm()), full, full],
    )
    full_a = full_a.reshape(D, PANEL)
    full_g = full_g.reshape(D, PANEL)
    gain_one = gain_pieces[:, 0, :320].reshape(D)
    gain_two = gain_pieces[:, 1, :320].reshape(D)
    w_qkv = full_a[:, :480]
    w_outt = full_a[:, 512:832]

    query_index = me_w * TOK + jnp.arange(TOK, dtype=jnp.int32)
    query_seg, query_pos = documents(doc_lengths, query_index)
    cosine, sine_table = rope_tables(query_pos)
    x_full = unpacked(x_pieces)
    cot_full = unpacked(cot_pieces)
    x_mine = lax.dynamic_slice_in_dim(x_full, me_n * OWN, OWN, 0).astype(F32)
    cot_mine = lax.dynamic_slice_in_dim(cot_full, me_n * OWN, OWN, 0).astype(F32)
    normed_one = norm_rows(x_full.astype(F32), gain_one)[0].astype(BF)
    qkv_raw = dot(normed_one, w_qkv)
    queries = rotate(qkv_raw[:, :q_width].reshape(TOK, -1, HEAD), cosine, sine_table).astype(BF)
    keys_mine = rotate(
        qkv_raw[:, q_width : q_width + kv_width].reshape(TOK, 1, HEAD), cosine, sine_table
    )
    kv_mine = jnp.concatenate(
        [
            keys_mine.reshape(TOK, HEAD),
            jnp.zeros((TOK, 48), F32),
            qkv_raw[:, q_width + kv_width :],
            jnp.zeros((TOK, 48), F32),
        ],
        axis=1,
    ).astype(BF)

    def k2(net, ins, outs, scratch):
        at = net.at
        net.barrier([((at.w + 15) % 16, at.n), ((at.w + 14) % 16, at.n)], 2)
        net.keep(ins[0], outs[0].at[2])
        copies = [
            net.send(ins[0], outs[0].at[1], ((at.w + 1) % 16, at.n)),
            net.send(ins[0], outs[0].at[0], ((at.w + 2) % 16, at.n)),
        ]
        for copy in copies:
            copy.wait_recv()
        net.run([])

    (kv_seen,) = exchange(
        "keys_values", 2, k2, [(kv_mine, hbm())], [((3, TOK, 256), BF, hbm())]
    )
    kv_seen = kv_seen.reshape(3 * TOK, 256)
    key_start = (me_w - 2) * TOK
    key_index = key_start + jnp.arange(3 * TOK, dtype=jnp.int32)
    key_seg = documents(doc_lengths, key_index)[0]
    visible = (
        (query_seg[:, None] == key_seg[None, :])
        & (key_index[None, :] <= query_index[:, None])
        & (query_index[:, None] - key_index[None, :] < WINDOW)
        & (key_index[None, :] >= 0)
    )
    keys_here = kv_seen[:, :HEAD].reshape(3 * TOK, 1, HEAD)
    values_here = kv_seen[:, 128 : 128 + HEAD].reshape(3 * TOK, 1, HEAD)
    grouped = queries.reshape(TOK, 1, per_group, HEAD)
    mixed, log_totals = attend(grouped, keys_here, values_here, visible)
    attended = mixed.reshape(TOK, q_width).astype(BF)
    out_part = dot_t(attended, w_outt).astype(BF).reshape(8, OWN, D)

    def k3(net, ins, outs, scratch):
        at = net.at
        net.barrier(at.narrow_peers() + at.wide_peers(), 12)
        net.run(
            [narrow_sum(net, ins[0], scratch[0], outs[0]), wide_gather(net, ins[1], outs[1])]
        )

    mine = ((OWN, D), F32, vmem())
    slots = pltpu.VMEM((7, OWN, D), BF)
    out_sum, full_u = exchange(
        "sum_out", 3, k3, [(out_part, vmem()), (w_up, hbm())], [mine, full], [slots]
    )
    full_u = full_u.reshape(D, PANEL)
    mid_mine = x_mine + out_sum
    normed_mine, inverse_two = norm_rows(mid_mine, gain_two)

    def k4(net, ins, outs, scratch):
        at = net.at
        net.barrier(at.narrow_peers() + at.wide_peers(), 12)
        net.run([narrow_gather(net, ins[0], outs[0]), wide_gather(net, ins[1], outs[1])])

    tokens = ((8, OWN, D), BF, hbm())
    normed_two, full_d = exchange(
        "gather_normed", 4, k4, [(normed_mine.astype(BF), hbm()), (shard_d, hbm())], [tokens, full]
    )
    normed_two = normed_two.reshape(TOK, D)
    full_d = full_d.reshape(D, PANEL)
    gate_val = dot(normed_two, full_g)
    up_val = dot(normed_two, full_u)
    sigmoid_gate = jax.nn.sigmoid(gate_val)
    activated = gate_val * sigmoid_gate
    hidden_act = (activated * up_val).astype(BF)
    down_part = dot_t(hidden_act, full_d).astype(BF).reshape(8, OWN, D)
    grad_hidden = dot(cot_full, full_d)
    grad_gate_pre = (
        grad_hidden * up_val * sigmoid_gate * (1.0 + gate_val * (1.0 - sigmoid_gate))
    ).astype(BF)
    grad_up_pre = (grad_hidden * activated).astype(BF)
    gn2_part = (
        (dot_t(grad_gate_pre, full_g) + dot_t(grad_up_pre, full_u)).astype(BF).reshape(8, OWN, D)
    )
    grad_d = t_dot(cot_full, hidden_act).astype(BF).reshape(16, ROWS, PANEL)
    grad_g = t_dot(normed_two, grad_gate_pre).astype(BF).reshape(16, ROWS, PANEL)
    grad_u = t_dot(normed_two, grad_up_pre).astype(BF).reshape(16, ROWS, PANEL)

    def k5(net, ins, outs, scratch):
        at = net.at
        net.barrier(at.narrow_peers() + at.wide_peers(), 12)
        loads = [net.keep(ins[2], scratch[2]), net.keep(ins[3], scratch[6])]
        for copy in loads:
            copy.wait()
        net.kept.clear()
        net.run(
            [
                narrow_sum(net, ins[0], scratch[0], outs[0]),
                wide_sum(net, *scratch[2:6], outs[2]),
                narrow_sum(net, ins[1], scratch[1], outs[1]),
                wide_sum(net, *scratch[6:10], outs[3]),
            ]
        )

    def summed(columns):
        return ((ROWS, columns), F32, vmem())

    gn2_sum, down_sum, grad_d_mine, grad_g_mine = exchange(
        "sum_mlp",
        5,
        k5,
        [(gn2_part, vmem()), (down_part, vmem()), (grad_d, hbm()), (grad_g, hbm())],
        [mine, mine, summed(PANEL), summed(PANEL)],
        [slots, slots, *wide_sum_scratch(PANEL), *wide_sum_scratch(PANEL)],
    )
    output_mine = (mid_mine + down_sum).astype(BF)
    through_two, gain_two_part = norm_back(mid_mine, inverse_two, gain_two, gn2_sum)
    grad_mid_mine = cot_mine + through_two

    def by_feature(rows):
        return rows.reshape(OWN, 8, 320).transpose(1, 0, 2)

    def k6(net, ins, outs, scratch):
        at = net.at
        net.barrier(at.narrow_peers() + at.wide_peers(), 12)
        net.keep(ins[2], scratch[0]).wait()
        net.kept.clear()
        net.run(
            [
                narrow_gather(net, ins[0], outs[0]),
                narrow_swap(net, ins[1], outs[1]),
                wide_sum(net, *scratch, outs[2]),
            ]
        )

    grad_mid_full, output_rows, grad_u_mine = exchange(
        "gather_grad_mid",
        6,
        k6,
        [
            (grad_mid_mine.astype(BF), hbm()),
            (by_feature(output_mine), hbm()),
            (grad_u, hbm()),
        ],
        [tokens, ((8, OWN, 320), BF, hbm()), summed(PANEL)],
        wide_sum_scratch(PANEL),
    )
    layer_output = output_rows.reshape(TOK, 320)
    grad_mid_full = grad_mid_full.reshape(TOK, D)
    grad_out = t_dot(grad_mid_full, attended).astype(BF)
    grad_out = jnp.pad(grad_out, ((0, 0), (0, 64))).reshape(16, ROWS, 384)
    grad_attended = dot(grad_mid_full, w_outt).astype(BF)
    grad_grouped, grad_keys, grad_values = attend_back(
        grouped,
        keys_here,
        values_here,
        visible,
        log_totals,
        grad_attended.reshape(TOK, 1, per_group, HEAD),
    )
    pad = jnp.zeros((3 * TOK, 48), F32)
    grad_seen = jnp.concatenate(
        [grad_keys.reshape(3 * TOK, HEAD), pad, grad_values.reshape(3 * TOK, HEAD), pad], axis=1
    ).reshape(3, TOK, 256)

    def k7(net, ins, outs, scratch):
        at = net.at
        net.barrier([((at.w + 1) % 16, at.n), ((at.w + 2) % 16, at.n)], 2)
        copies = [
            net.send(ins[0].at[1], outs[0].at[1], ((at.w + 15) % 16, at.n)),
            net.send(ins[0].at[0], outs[0].at[0], ((at.w + 14) % 16, at.n)),
        ]
        for copy in copies:
            copy.wait_recv()
        net.run([])

    (grad_later,) = exchange(
        "grad_keys_values", 7, k7, [(grad_seen[:2].astype(BF), hbm())], [((2, TOK, 256), BF, hbm())]
    )
    grad_kv_mine = (
        grad_seen[2]
        + jnp.where(me_w < 15, grad_later[1], 0).astype(F32)
        + jnp.where(me_w < 14, grad_later[0], 0).astype(F32)
    )
    grad_query_raw = unrotate(grad_grouped.reshape(TOK, 4, HEAD), cosine, sine_table).reshape(
        TOK, q_width
    )
    grad_key_raw = unrotate(
        grad_kv_mine[:, :HEAD].reshape(TOK, 1, HEAD), cosine, sine_table
    ).reshape(TOK, kv_width)
    grad_qkv = jnp.concatenate(
        [grad_query_raw, grad_key_raw, grad_kv_mine[:, 128 : 128 + HEAD]], axis=1
    ).astype(BF)
    gn1_part = dot_t(grad_qkv, w_qkv).astype(BF).reshape(8, OWN, D)
    grad_qkv_full = jnp.pad(t_dot(normed_one, grad_qkv).astype(BF), ((0, 0), (0, 32))).reshape(
        16, ROWS, 512
    )

    def k8(net, ins, outs, scratch):
        at = net.at
        net.barrier(at.narrow_peers() + at.wide_peers(), 12)
        loads = [net.keep(ins[1], scratch[1]), net.keep(ins[2], scratch[5])]
        for copy in loads:
            copy.wait()
        net.kept.clear()
        net.run(
            [
                narrow_sum(net, ins[0], scratch[0], outs[0]),
                wide_sum(net, *scratch[1:5], outs[1]),
                wide_sum(net, *scratch[5:9], outs[2]),
            ]
        )

    gn1_sum, grad_out_mine, grad_qkv_mine = exchange(
        "sum_attn",
        8,
        k8,
        [(gn1_part, vmem()), (grad_out, hbm()), (grad_qkv_full, hbm())],
        [mine, summed(384), summed(512)],
        [slots, *wide_sum_scratch(384), *wide_sum_scratch(512)],
    )
    inverse_one = lax.rsqrt(jnp.mean(x_mine * x_mine, axis=1, keepdims=True) + epsilon)
    through_one, gain_one_part = norm_back(x_mine, inverse_one, gain_one, gn1_sum)
    grad_input_mine = (grad_mid_mine + through_one).astype(BF)
    gain_parts = jnp.stack([gain_one_part.reshape(8, 320), gain_two_part.reshape(8, 320)], axis=1)
    gain_parts = jnp.pad(gain_parts, ((0, 0), (0, 6), (0, 64)))

    def k9(net, ins, outs, scratch):
        at = net.at
        everyone = [((at.w + k) % 16, at.n) for k in range(1, 16)]
        net.barrier(at.narrow_peers() + everyone, 22)
        me = at.n
        copies = [net.send(ins[1].at[p[1]], scratch[0].at[me], p) for p in at.narrow_peers()]
        task = narrow_swap(net, ins[0], outs[0])
        next(task)
        scratch[0][me] = ins[1][me]
        for copy in copies:
            copy.wait_recv()
        total = scratch[0][0]
        for k in range(1, 8):
            total += scratch[0][k]
        scratch[1][0] = total
        copies = [net.send(scratch[1].at[0], scratch[1].at[k + 1], p) for k, p in enumerate(everyone)]
        for copy in copies:
            copy.wait_recv()
        total = scratch[1][0]
        for k in range(1, 16):
            total += scratch[1][k]
        outs[1][...] = total
        net.run([task])

    grad_rows, gain_sums = exchange(
        "swap_grad_input",
        9,
        k9,
        [(by_feature(grad_input_mine), hbm()), (gain_parts, vmem())],
        [((8, OWN, 320), BF, hbm()), ((8, 384), F32, vmem())],
        [pltpu.VMEM((8, 8, 384), F32), pltpu.VMEM((16, 8, 384), F32)],
    )
    return (
        layer_output,
        grad_rows.reshape(TOK, 320).astype(F32),
        gain_sums[0, :320],
        grad_qkv_mine[:, :320],
        grad_qkv_mine[:, 320:400],
        grad_qkv_mine[:, 400:480],
        grad_out_mine[:, :320].T,
        gain_sums[1, :320],
        grad_g_mine,
        grad_u_mine,
        grad_d_mine.T,
    )


def solution(mesh):
    rows, columns = P("wide", "narrow"), P("narrow", "wide")
    return jax.shard_map(
        body,
        mesh=mesh,
        in_specs=(
            rows,
            P("narrow"),
            rows,
            rows,
            rows,
            columns,
            P("narrow"),
            rows,
            rows,
            columns,
            P(),
            rows,
        ),
        out_specs=(
            rows,
            rows,
            P("narrow"),
            rows,
            rows,
            rows,
            columns,
            P("narrow"),
            rows,
            rows,
            columns,
        ),
        check_vma=False,
    )
```

```python
import functools
import math

import jax
import jax.numpy as jnp
from jax import lax
from jax.experimental import pallas as pl
from jax.experimental.pallas import tpu as pltpu
from jax.sharding import PartitionSpec as P

D = 2560
HEADS = 32
KV_HEADS = 8
HEAD = 80
WINDOW = 1024
TOK = 512
OWN = 64
ROWS = 160
PANEL = 896

epsilon = 1e-05
rope_base = 1000000.0
rope_factor = 8.0
long_wave = 8192.0
short_wave = 2048.0
masked = -1e30

MESH = pl.DeviceIdType.MESH
BF = jnp.bfloat16
F32 = jnp.float32


class Place:
    def __init__(self):
        self.w = lax.axis_index("wide")
        self.n = lax.axis_index("narrow")
        self.z, self.h, self.c = self.w // 4, (self.w // 2) % 2, self.w % 2
        self.x, self.l = self.n // 2, self.n % 2

    def wide(self, dz, dh, dc):
        return ((self.z + dz) % 4) * 4 + ((self.h + dh) % 2) * 2 + (self.c + dc) % 2

    def narrow(self, dx, dl):
        return ((self.x + dx) % 4) * 2 + (self.l + dl) % 2

    def narrow_peers(self):
        return [(self.w, self.narrow(k // 2, k % 2)) for k in (2, 6, 1, 3, 7, 4, 5)]

    def wide_peers(self):
        return [(self.wide(*d), self.n) for d in ((0, 1, 0), (1, 0, 0), (3, 0, 0), (2, 0, 0), (0, 0, 1))]


class Net:
    def __init__(self, place, send_sems, recv_sems, local_sems):
        self.at = place
        self.sems = (send_sems, recv_sems, local_sems)
        self.sent, self.kept = [], []

    def barrier(self, givers, takers):
        bar = pltpu.get_barrier_semaphore()
        for device in givers:
            pl.semaphore_signal(bar, inc=1, device_id=device, device_id_type=MESH)
        pl.semaphore_wait(bar, takers)

    def send(self, src, dst, device):
        i = len(self.sent)
        copy = pltpu.make_async_remote_copy(
            src_ref=src,
            dst_ref=dst,
            send_sem=self.sems[0].at[i],
            recv_sem=self.sems[1].at[i],
            device_id=device,
            device_id_type=MESH,
        )
        copy.start()
        self.sent.append(copy)
        return copy

    def keep(self, src, dst):
        copy = pltpu.make_async_copy(src, dst, self.sems[2].at[len(self.kept)])
        copy.start()
        self.kept.append(copy)
        return copy

    def run(self, tasks):
        tasks = list(tasks)
        while tasks:
            left = []
            for task in tasks:
                try:
                    next(task)
                    left.append(task)
                except StopIteration:
                    pass
            tasks = left
        for copy in self.sent:
            copy.wait_send()
        for copy in self.kept:
            copy.wait()


def narrow_gather(net, src, dst, cut):
    at = net.at
    me, near = at.n, at.narrow(0, 1)
    net.keep(src, dst.at[me])
    late = net.send(src.at[cut:], dst.at[me, cut:], (at.w, near))
    turns = [(d, net.send(src, dst.at[me], (at.w, at.narrow(d, 0)))) for d in (1, 3, 2)]
    early = net.send(src.at[:cut], dst.at[me, :cut], (at.w, near))
    yield
    late.wait_recv()
    rest = [
        net.send(dst.at[near, cut:], dst.at[near, cut:], (at.w, at.narrow(d, 0))) for d in (1, 3, 2)
    ]
    yield
    for d, copy in turns:
        copy.wait_recv()
        block = at.narrow(-d, 0)
        rest.append(net.send(dst.at[block, :cut], dst.at[block, :cut], (at.w, near)))
    yield
    early.wait_recv()
    for copy in rest:
        copy.wait_recv()


def narrow_share(net, src, dst):
    me = net.at.n
    copies = [net.send(src, dst.at[me], peer) for peer in net.at.narrow_peers()]
    net.keep(src, dst.at[me])
    yield
    yield
    for copy in copies:
        copy.wait_recv()


def narrow_swap(net, src, dst):
    me = net.at.n
    copies = [net.send(src.at[peer[1]], dst.at[me], peer) for peer in net.at.narrow_peers()]
    net.keep(src.at[me], dst.at[me])
    yield
    yield
    yield
    for copy in copies:
        copy.wait_recv()


def add_rows(rows, step, dst, terms):
    @pl.loop(0, rows // step)
    def _(i):
        part = pl.ds(pl.multiple_of(i * step, step), step)
        total = terms[0][part, :].astype(F32)
        for term in terms[1:]:
            total += term[part, :].astype(F32)
        dst[part, :] = total.astype(dst.dtype)


def narrow_sum(net, src, slots, out, cut):
    at = net.at
    me, near = at.n, at.narrow(0, 1)
    rows = src.shape[1]
    over = {
        d: net.send(
            src.at[at.narrow(d, 1), :cut], slots.at[d - 1, :cut], (at.w, near)
        )
        for d in (1, 3, 2)
    }
    across = {
        d: net.send(
            src.at[at.narrow(d, 1), cut:], slots.at[d - 1, cut:], (at.w, at.narrow(d, 0))
        )
        for d in (1, 3, 2)
    }
    late = [
        net.send(src.at[at.narrow(d, 0), cut:], slots.at[2 + d, cut:], (at.w, at.narrow(d, 0)))
        for d in (1, 3, 2)
    ]
    final = [net.send(src.at[near, :cut], slots.at[6, :cut], (at.w, near))]
    yield
    early = []
    for d in (1, 3, 2):
        over[d].wait_recv()
        block = at.narrow(d, 0)
        term = src.at[block, :cut]
        add_rows(cut, 16, term, [term, slots.at[d - 1, :cut]])
        early.append(net.send(term, slots.at[2 + d, :cut], (at.w, at.narrow(d, 0))))
    yield
    for d in (1, 3, 2):
        across[d].wait_recv()
    term = src.at[near, cut:]
    add_rows(rows - cut, 16, term, [term, *(slots.at[k, cut:] for k in range(3))])
    final.append(net.send(term, slots.at[6, cut:], (at.w, near)))
    yield
    for copy in late + early + final:
        copy.wait_recv()
    add_rows(rows, 16, out, [src.at[me], *(slots.at[k] for k in range(3, 7))])


def wide_gather(net, src, dst):
    at = net.at
    half = ROWS // 2
    me, far = at.w, at.wide(0, 1, 0)
    up, down = (at.wide(1, 0, 0), at.n), (at.wide(3, 0, 0), at.n)
    other = (at.wide(0, 0, 1), at.n)
    net.keep(src, dst.at[me])
    from_far = net.send(src, dst.at[me], (far, at.n))
    turns = [[net.send(src, dst.at[me], up), net.send(src, dst.at[me], down)]]
    over = [net.send(src, dst.at[me], other)]
    yield
    from_far.wait_recv()
    turns.append([net.send(dst.at[far], dst.at[far], up), net.send(dst.at[far], dst.at[far], down)])
    over.append(net.send(dst.at[far], dst.at[far], other))
    yield
    further = []
    for e in (0, 1):
        for d, part, ahead, copy in ((3, slice(0, half), up, turns[e][0]), (1, slice(half, ROWS), down, turns[e][1])):
            copy.wait_recv()
            block = at.wide(d, e, 0)
            further.append((e, part, net.send(dst.at[block, part], dst.at[block, part], ahead)))
            over.append(net.send(dst.at[block], dst.at[block], other))
        yield
    for e, part, copy in further:
        copy.wait_recv()
        block = at.wide(2, e, 0)
        over.append(net.send(dst.at[block, part], dst.at[block, part], other))
    yield
    for copy in over:
        copy.wait_recv()


def wide_sum(net, src, core, turned, last, out):
    at = net.at
    rows = src.shape[1]
    half = rows // 2
    up, down = (at.wide(1, 0, 0), at.n), (at.wide(3, 0, 0), at.n)
    other = (at.wide(0, 0, 1), at.n)
    order = [(d, e) for d in (2, 1, 3, 0) for e in (1, 0)]
    over = {(d, e): net.send(src.at[at.wide(d, e, 1)], core.at[d, e], other) for d, e in order}
    yield
    further = []
    for d, e in order:
        over[d, e].wait_recv()
        block = src.at[at.wide(d, e, 0)]
        add_rows(rows, 32, block, [block, core.at[d, e]])
        if d == 2:
            further.append(
                (
                    e,
                    net.send(block.at[:half], turned.at[2, e, :half], up),
                    net.send(block.at[half:], turned.at[2, e, half:], down),
                )
            )
    yield
    turns = []
    for e, first, second in further:
        first.wait_recv()
        block = src.at[at.wide(1, e, 0)]
        part = block.at[:half]
        add_rows(half, 16, part, [part, turned.at[2, e, :half]])
        turns.append((e, net.send(block, turned.at[0, e], up)))
        second.wait_recv()
        block = src.at[at.wide(3, e, 0)]
        part = block.at[half:]
        add_rows(half, 16, part, [part, turned.at[2, e, half:]])
        turns.append((e, net.send(block, turned.at[1, e], down)))
        yield
    for e, copy in turns:
        if e:
            copy.wait_recv()
    block = src.at[at.wide(0, 1, 0)]
    add_rows(rows, 32, block, [block, turned.at[0, 1], turned.at[1, 1]])
    final = net.send(block, last, (at.wide(0, 1, 0), at.n))
    yield
    for e, copy in turns:
        if not e:
            copy.wait_recv()
    final.wait_recv()
    add_rows(rows, 32, out, [src.at[at.w], last, turned.at[0, 0], turned.at[1, 0]])


def wide_sum_scratch(columns):
    return [
        pltpu.VMEM((16, ROWS, columns), BF),
        pltpu.VMEM((4, 2, ROWS, columns), BF),
        pltpu.VMEM((3, 2, ROWS, columns), BF),
        pltpu.VMEM((ROWS, columns), BF),
    ]


def vmem():
    return pl.BlockSpec(memory_space=pltpu.VMEM)


def hbm():
    return pl.BlockSpec(memory_space=pl.ANY)


def exchange(name, number, body, ins, outs, scratch=(), sends=96, keeps=32):
    def kernel(*refs):
        a, b = len(ins), len(ins) + len(outs)
        net = Net(Place(), *refs[-3:])
        body(net, refs[:a], refs[a:b], refs[b:-3])

    return pl.pallas_call(
        kernel,
        out_shape=[jax.ShapeDtypeStruct(shape, dtype) for shape, dtype, _ in outs],
        in_specs=[spec for _, spec in ins],
        out_specs=[spec for _, _, spec in outs],
        scratch_shapes=[
            *scratch,
            pltpu.SemaphoreType.DMA((sends,)),
            pltpu.SemaphoreType.DMA((sends,)),
            pltpu.SemaphoreType.DMA((keeps,)),
        ],
        compiler_params=pltpu.CompilerParams(
            collective_id=number, has_side_effects=True, vmem_limit_bytes=56 * 2**20
        ),
        name=name,
    )(*[array for array, _ in ins])


def documents(doc_lengths, places):
    ends_at = jnp.cumsum(doc_lengths)
    passed = places[:, None] >= ends_at[None, :]
    segment = jnp.sum(passed.astype(jnp.int32), axis=1)
    begins = jnp.sum(jnp.where(passed, doc_lengths[None, :], 0), axis=1)
    return (segment, places - begins)


def scaled_freqs():
    half_width = HEAD // 2
    freqs = rope_base ** (-2.0 * jnp.arange(half_width, dtype=jnp.float32) / HEAD)
    wavelen = 2.0 * math.pi / freqs
    smooth = (long_wave / wavelen - 1.0) / 3.0
    blended = (1.0 - smooth) * freqs / rope_factor + smooth * freqs
    return jnp.where(
        wavelen < short_wave, freqs, jnp.where(wavelen > long_wave, freqs / rope_factor, blended)
    )


def rope_tables(position):
    freqs = scaled_freqs()
    angles = position.astype(jnp.float32)[:, None] * freqs[None, :]
    return (jnp.cos(angles), jnp.sin(angles))


def rotate(stacked, cosine, sine_table):
    half_width = stacked.shape[-1] // 2
    front_half = stacked[..., :half_width]
    back_half = stacked[..., half_width:]
    cos_rows = cosine[:, None, :]
    sin_rows = sine_table[:, None, :]
    return jnp.concatenate(
        [
            front_half * cos_rows - back_half * sin_rows,
            back_half * cos_rows + front_half * sin_rows,
        ],
        axis=-1,
    )


def unrotate(stacked, cosine, sine_table):
    return rotate(stacked, cosine, -sine_table)


def norm_rows(stream, gain):
    inverse_rms = lax.rsqrt(jnp.mean(stream * stream, axis=1, keepdims=True) + epsilon)
    return stream * inverse_rms * gain[None, :], inverse_rms


def norm_back(stream, inverse_rms, gain, upstream):
    weighted = upstream * gain[None, :]
    inner = jnp.sum(weighted * stream, axis=1, keepdims=True)
    through = inverse_rms * weighted - stream * (
        inverse_rms * inverse_rms * inverse_rms * inner / D
    )
    return (through, jnp.sum(upstream * stream * inverse_rms, axis=0))


def scores_of(queries, keys_here, visible):
    raw_scores = jnp.einsum(
        "tkgd,skd->kgts", queries, keys_here, preferred_element_type=jnp.float32
    ) * (1.0 / math.sqrt(HEAD))
    return jnp.where(visible[None, None], raw_scores, masked)


def attend(queries, keys_here, values_here, visible):
    scores = scores_of(queries, keys_here, visible)
    largest = jnp.max(scores, axis=-1, keepdims=True)
    powers = jnp.exp(scores - largest)
    totals = jnp.sum(powers, axis=-1, keepdims=True)
    weights = (powers / totals).astype(jnp.bfloat16)
    mixed = jnp.einsum("kgts,skd->tkgd", weights, values_here, preferred_element_type=jnp.float32)
    return (mixed, largest + jnp.log(totals))


def attend_back(queries, keys_here, values_here, visible, log_totals, upstream):
    weights = jnp.exp(scores_of(queries, keys_here, visible) - log_totals)
    upstream_prob = jnp.einsum(
        "tkgd,skd->kgts", upstream, values_here, preferred_element_type=jnp.float32
    )
    grad_scores = (
        weights * (upstream_prob - jnp.sum(weights * upstream_prob, axis=-1, keepdims=True))
    ).astype(jnp.bfloat16)
    factor = 1.0 / math.sqrt(HEAD)
    grad_queries = (
        jnp.einsum("kgts,skd->tkgd", grad_scores, keys_here, preferred_element_type=jnp.float32)
        * factor
    )
    grad_keys = (
        jnp.einsum("kgts,tkgd->skd", grad_scores, queries, preferred_element_type=jnp.float32)
        * factor
    )
    grad_values = jnp.einsum(
        "kgts,tkgd->skd", weights.astype(jnp.bfloat16), upstream, preferred_element_type=jnp.float32
    )
    return (grad_queries, grad_keys, grad_values)


def packed(block):
    return jnp.concatenate([block[: TOK // 2], block[TOK // 2 :]], axis=1)


def unpacked(pieces):
    return (
        pieces.reshape(8, TOK // 2, 2, D // 8).transpose(2, 1, 0, 3).reshape(TOK, D)
    )


def dot(a, b):
    return jnp.dot(a, b, preferred_element_type=F32)


def dot_t(a, b):
    return lax.dot_general(a, b, (((1,), (1,)), ((), ())), preferred_element_type=F32)


def t_dot(a, b):
    return lax.dot_general(a, b, (((0,), (0,)), ((), ())), preferred_element_type=F32)


def body(
    layer_input,
    gain_attn,
    w_query,
    w_key,
    w_value,
    w_out,
    gain_mlp,
    w_gate,
    w_up,
    w_down,
    doc_lengths,
    cotangent,
):
    q_width, kv_width, ff_width = 320, 80, 896
    per_group = HEADS // KV_HEADS
    me_n = lax.axis_index("narrow")
    me_w = lax.axis_index("wide")
    shard_a = jnp.concatenate(
        [w_query, w_key, w_value, jnp.zeros((ROWS, 32), BF), w_out.T, jnp.zeros((ROWS, 64), BF)],
        axis=1,
    )
    shard_d = w_down.T
    gains = jnp.zeros((8, 384), F32).at[0, :320].set(gain_attn).at[1, :320].set(gain_mlp)
    full = ((16, ROWS, PANEL), BF, hbm())

    def k1(net, ins, outs, scratch):
        at = net.at
        net.barrier(at.narrow_peers() + at.wide_peers(), 12)
        net.run(
            [
                wide_gather(net, ins[3], outs[3]),
                narrow_share(net, ins[2], outs[2]),
                narrow_gather(net, ins[0], outs[0], 128),
                wide_gather(net, ins[4], outs[4]),
                narrow_gather(net, ins[1], outs[1], 128),
            ]
        )

    piece = ((8, TOK // 2, 640), BF, hbm())
    x_pieces, cot_pieces, gain_pieces, full_a, full_g = exchange(
        "gather_input",
        1,
        k1,
        [
            (packed(layer_input), hbm()),
            (packed(cotangent), hbm()),
            (gains, hbm()),
            (shard_a, hbm()),
            (w_gate, hbm()),
        ],
        [piece, piece, ((8, 8, 384), F32, hbm()), full, full],
    )
    full_a = full_a.reshape(D, PANEL)
    full_g = full_g.reshape(D, PANEL)
    gain_one = gain_pieces[:, 0, :320].reshape(D)
    gain_two = gain_pieces[:, 1, :320].reshape(D)
    w_qkv = full_a[:, :480]
    w_outt = full_a[:, 512:832]

    query_index = me_w * TOK + jnp.arange(TOK, dtype=jnp.int32)
    query_seg, query_pos = documents(doc_lengths, query_index)
    cosine, sine_table = rope_tables(query_pos)
    x_full = unpacked(x_pieces)
    cot_full = unpacked(cot_pieces)
    x_mine = lax.dynamic_slice_in_dim(x_full, me_n * OWN, OWN, 0).astype(F32)
    cot_mine = lax.dynamic_slice_in_dim(cot_full, me_n * OWN, OWN, 0).astype(F32)
    normed_one = norm_rows(x_full.astype(F32), gain_one)[0].astype(BF)
    qkv_raw = dot(normed_one, w_qkv)
    queries = rotate(qkv_raw[:, :q_width].reshape(TOK, -1, HEAD), cosine, sine_table).astype(BF)
    keys_mine = rotate(
        qkv_raw[:, q_width : q_width + kv_width].reshape(TOK, 1, HEAD), cosine, sine_table
    )
    kv_mine = jnp.concatenate(
        [
            keys_mine.reshape(TOK, HEAD),
            jnp.zeros((TOK, 48), F32),
            qkv_raw[:, q_width + kv_width :],
            jnp.zeros((TOK, 48), F32),
        ],
        axis=1,
    ).astype(BF)

    def k2(net, ins, outs, scratch):
        at = net.at
        net.barrier([((at.w + 15) % 16, at.n), ((at.w + 14) % 16, at.n)], 2)
        net.keep(ins[0], outs[0].at[2])
        copies = [
            net.send(ins[0], outs[0].at[1], ((at.w + 1) % 16, at.n)),
            net.send(ins[0], outs[0].at[0], ((at.w + 2) % 16, at.n)),
        ]
        for copy in copies:
            copy.wait_recv()
        net.run([])

    (kv_seen,) = exchange(
        "keys_values", 2, k2, [(kv_mine, hbm())], [((3, TOK, 256), BF, hbm())]
    )
    kv_seen = kv_seen.reshape(3 * TOK, 256)
    key_start = (me_w - 2) * TOK
    key_index = key_start + jnp.arange(3 * TOK, dtype=jnp.int32)
    key_seg = documents(doc_lengths, key_index)[0]
    visible = (
        (query_seg[:, None] == key_seg[None, :])
        & (key_index[None, :] <= query_index[:, None])
        & (query_index[:, None] - key_index[None, :] < WINDOW)
        & (key_index[None, :] >= 0)
    )
    keys_here = kv_seen[:, :HEAD].reshape(3 * TOK, 1, HEAD)
    values_here = kv_seen[:, 128 : 128 + HEAD].reshape(3 * TOK, 1, HEAD)
    grouped = queries.reshape(TOK, 1, per_group, HEAD)
    mixed, log_totals = attend(grouped, keys_here, values_here, visible)
    attended = mixed.reshape(TOK, q_width).astype(BF)
    out_part = dot_t(attended, w_outt).astype(BF).reshape(8, OWN, D)

    def k3(net, ins, outs, scratch):
        at = net.at
        net.barrier(at.narrow_peers() + at.wide_peers(), 12)
        net.run(
            [wide_gather(net, ins[1], outs[1]), narrow_sum(net, ins[0], scratch[0], outs[0], 32)]
        )

    mine = ((OWN, D), F32, vmem())
    slots = pltpu.VMEM((7, OWN, D), BF)
    out_sum, full_u = exchange(
        "sum_out", 3, k3, [(out_part, vmem()), (w_up, hbm())], [mine, full], [slots]
    )
    full_u = full_u.reshape(D, PANEL)
    mid_mine = x_mine + out_sum
    normed_mine, inverse_two = norm_rows(mid_mine, gain_two)

    def k4(net, ins, outs, scratch):
        at = net.at
        net.barrier(at.narrow_peers() + at.wide_peers(), 12)
        net.run([wide_gather(net, ins[1], outs[1]), narrow_gather(net, ins[0], outs[0], 32)])

    tokens = ((8, OWN, D), BF, hbm())
    normed_two, full_d = exchange(
        "gather_normed", 4, k4, [(normed_mine.astype(BF), hbm()), (shard_d, hbm())], [tokens, full]
    )
    normed_two = normed_two.reshape(TOK, D)
    full_d = full_d.reshape(D, PANEL)
    gate_val = dot(normed_two, full_g)
    up_val = dot(normed_two, full_u)
    sigmoid_gate = jax.nn.sigmoid(gate_val)
    activated = gate_val * sigmoid_gate
    hidden_act = (activated * up_val).astype(BF)
    down_part = dot_t(hidden_act, full_d).astype(BF).reshape(8, OWN, D)
    grad_hidden = dot(cot_full, full_d)
    grad_gate_pre = (
        grad_hidden * up_val * sigmoid_gate * (1.0 + gate_val * (1.0 - sigmoid_gate))
    ).astype(BF)
    grad_up_pre = (grad_hidden * activated).astype(BF)
    gn2_part = (
        (dot_t(grad_gate_pre, full_g) + dot_t(grad_up_pre, full_u)).astype(BF).reshape(8, OWN, D)
    )
    grad_d = t_dot(cot_full, hidden_act).astype(BF).reshape(16, ROWS, PANEL)
    grad_g = t_dot(normed_two, grad_gate_pre).astype(BF).reshape(16, ROWS, PANEL)
    grad_u = t_dot(normed_two, grad_up_pre).astype(BF).reshape(16, ROWS, PANEL)

    def k5(net, ins, outs, scratch):
        at = net.at
        net.barrier(at.narrow_peers() + at.wide_peers(), 12)
        loads = [net.keep(ins[2], scratch[2]), net.keep(ins[3], scratch[6])]
        for copy in loads:
            copy.wait()
        net.kept.clear()
        net.run(
            [
                wide_sum(net, *scratch[2:6], outs[2]),
                narrow_sum(net, ins[0], scratch[0], outs[0], 32),
                wide_sum(net, *scratch[6:10], outs[3]),
                narrow_sum(net, ins[1], scratch[1], outs[1], 32),
            ]
        )

    def summed(columns):
        return ((ROWS, columns), F32, vmem())

    gn2_sum, down_sum, grad_d_mine, grad_g_mine = exchange(
        "sum_mlp",
        5,
        k5,
        [(gn2_part, vmem()), (down_part, vmem()), (grad_d, hbm()), (grad_g, hbm())],
        [mine, mine, summed(PANEL), summed(PANEL)],
        [slots, slots, *wide_sum_scratch(PANEL), *wide_sum_scratch(PANEL)],
    )
    output_mine = (mid_mine + down_sum).astype(BF)
    through_two, gain_two_part = norm_back(mid_mine, inverse_two, gain_two, gn2_sum)
    grad_mid_mine = cot_mine + through_two

    def by_feature(rows):
        return rows.reshape(OWN, 8, 320).transpose(1, 0, 2)

    def k6(net, ins, outs, scratch):
        at = net.at
        net.barrier(at.narrow_peers() + at.wide_peers(), 12)
        net.keep(ins[2], scratch[0]).wait()
        net.kept.clear()
        net.run(
            [
                wide_sum(net, *scratch, outs[2]),
                narrow_gather(net, ins[0], outs[0], 32),
                narrow_swap(net, ins[1], outs[1]),
            ]
        )

    grad_mid_full, output_rows, grad_u_mine = exchange(
        "gather_grad_mid",
        6,
        k6,
        [
            (grad_mid_mine.astype(BF), hbm()),
            (by_feature(output_mine), hbm()),
            (grad_u, hbm()),
        ],
        [tokens, ((8, OWN, 320), BF, hbm()), summed(PANEL)],
        wide_sum_scratch(PANEL),
    )
    layer_output = output_rows.reshape(TOK, 320)
    grad_mid_full = grad_mid_full.reshape(TOK, D)
    grad_out = t_dot(grad_mid_full, attended).astype(BF)
    grad_out = jnp.pad(grad_out, ((0, 0), (0, 64))).reshape(16, ROWS, 384)
    grad_attended = dot(grad_mid_full, w_outt).astype(BF)
    grad_grouped, grad_keys, grad_values = attend_back(
        grouped,
        keys_here,
        values_here,
        visible,
        log_totals,
        grad_attended.reshape(TOK, 1, per_group, HEAD),
    )
    pad = jnp.zeros((3 * TOK, 48), F32)
    grad_seen = jnp.concatenate(
        [grad_keys.reshape(3 * TOK, HEAD), pad, grad_values.reshape(3 * TOK, HEAD), pad], axis=1
    ).reshape(3, TOK, 256)

    def k7(net, ins, outs, scratch):
        at = net.at
        net.barrier([((at.w + 1) % 16, at.n), ((at.w + 2) % 16, at.n)], 2)
        copies = [
            net.send(ins[0].at[1], outs[0].at[1], ((at.w + 15) % 16, at.n)),
            net.send(ins[0].at[0], outs[0].at[0], ((at.w + 14) % 16, at.n)),
        ]
        for copy in copies:
            copy.wait_recv()
        net.run([])

    (grad_later,) = exchange(
        "grad_keys_values", 7, k7, [(grad_seen[:2].astype(BF), hbm())], [((2, TOK, 256), BF, hbm())]
    )
    grad_kv_mine = (
        grad_seen[2]
        + jnp.where(me_w < 15, grad_later[1], 0).astype(F32)
        + jnp.where(me_w < 14, grad_later[0], 0).astype(F32)
    )
    grad_query_raw = unrotate(grad_grouped.reshape(TOK, 4, HEAD), cosine, sine_table).reshape(
        TOK, q_width
    )
    grad_key_raw = unrotate(
        grad_kv_mine[:, :HEAD].reshape(TOK, 1, HEAD), cosine, sine_table
    ).reshape(TOK, kv_width)
    grad_qkv = jnp.concatenate(
        [grad_query_raw, grad_key_raw, grad_kv_mine[:, 128 : 128 + HEAD]], axis=1
    ).astype(BF)
    gn1_part = dot_t(grad_qkv, w_qkv).astype(BF).reshape(8, OWN, D)
    grad_qkv_full = jnp.pad(t_dot(normed_one, grad_qkv).astype(BF), ((0, 0), (0, 32))).reshape(
        16, ROWS, 512
    )

    def k8(net, ins, outs, scratch):
        at = net.at
        net.barrier(at.narrow_peers() + at.wide_peers(), 12)
        loads = [net.keep(ins[1], scratch[1]), net.keep(ins[2], scratch[5])]
        for copy in loads:
            copy.wait()
        net.kept.clear()
        net.run(
            [
                wide_sum(net, *scratch[1:5], outs[1]),
                narrow_sum(net, ins[0], scratch[0], outs[0], 32),
                wide_sum(net, *scratch[5:9], outs[2]),
            ]
        )

    gn1_sum, grad_out_mine, grad_qkv_mine = exchange(
        "sum_attn",
        8,
        k8,
        [(gn1_part, vmem()), (grad_out, hbm()), (grad_qkv_full, hbm())],
        [mine, summed(384), summed(512)],
        [slots, *wide_sum_scratch(384), *wide_sum_scratch(512)],
    )
    inverse_one = lax.rsqrt(jnp.mean(x_mine * x_mine, axis=1, keepdims=True) + epsilon)
    through_one, gain_one_part = norm_back(x_mine, inverse_one, gain_one, gn1_sum)
    grad_input_mine = (grad_mid_mine + through_one).astype(BF)
    gain_parts = jnp.stack([gain_one_part.reshape(8, 320), gain_two_part.reshape(8, 320)], axis=1)
    gain_parts = jnp.pad(gain_parts, ((0, 0), (0, 6), (0, 64)))

    def k9(net, ins, outs, scratch):
        at = net.at
        everyone = [((at.w + k) % 16, at.n) for k in range(1, 16)]
        net.barrier(at.narrow_peers() + everyone, 22)
        me = at.n
        copies = [net.send(ins[1].at[p[1]], scratch[0].at[me], p) for p in at.narrow_peers()]
        task = narrow_swap(net, ins[0], outs[0])
        next(task)
        scratch[0][me] = ins[1][me]
        for copy in copies:
            copy.wait_recv()
        total = scratch[0][0]
        for k in range(1, 8):
            total += scratch[0][k]
        scratch[1][0] = total
        copies = [net.send(scratch[1].at[0], scratch[1].at[k + 1], p) for k, p in enumerate(everyone)]
        for copy in copies:
            copy.wait_recv()
        total = scratch[1][0]
        for k in range(1, 16):
            total += scratch[1][k]
        outs[1][...] = total
        net.run([task])

    grad_rows, gain_sums = exchange(
        "swap_grad_input",
        9,
        k9,
        [(by_feature(grad_input_mine), hbm()), (gain_parts, vmem())],
        [((8, OWN, 320), BF, hbm()), ((8, 384), F32, vmem())],
        [pltpu.VMEM((8, 8, 384), F32), pltpu.VMEM((16, 8, 384), F32)],
    )
    return (
        layer_output,
        grad_rows.reshape(TOK, 320).astype(F32),
        gain_sums[0, :320],
        grad_qkv_mine[:, :320],
        grad_qkv_mine[:, 320:400],
        grad_qkv_mine[:, 400:480],
        grad_out_mine[:, :320].T,
        gain_sums[1, :320],
        grad_g_mine,
        grad_u_mine,
        grad_d_mine.T,
    )


def solution(mesh):
    rows, columns = P("wide", "narrow"), P("narrow", "wide")
    return jax.shard_map(
        body,
        mesh=mesh,
        in_specs=(
            rows,
            P("narrow"),
            rows,
            rows,
            rows,
            columns,
            P("narrow"),
            rows,
            rows,
            columns,
            P(),
            rows,
        ),
        out_specs=(
            rows,
            rows,
            P("narrow"),
            rows,
            rows,
            rows,
            columns,
            P("narrow"),
            rows,
            rows,
            columns,
        ),
        check_vma=False,
    )
```

```python
import functools
import math

import jax
import jax.numpy as jnp
from jax import lax
from jax.experimental import pallas as pl
from jax.experimental.pallas import tpu as pltpu
from jax.sharding import PartitionSpec as P

D = 2560
HEADS = 32
KV_HEADS = 8
HEAD = 80
WINDOW = 1024
TOK = 512
OWN = 64
ROWS = 160
PANEL = 896
TILE = 128
REACH = WINDOW + TILE

epsilon = 1e-05
rope_base = 1000000.0
rope_factor = 8.0
long_wave = 8192.0
short_wave = 2048.0
masked = -1e30

MESH = pl.DeviceIdType.MESH
BF = jnp.bfloat16
F32 = jnp.float32


class Place:
    def __init__(self):
        self.w = lax.axis_index("wide")
        self.n = lax.axis_index("narrow")
        self.z, self.h, self.c = self.w // 4, (self.w // 2) % 2, self.w % 2
        self.x, self.l = self.n // 2, self.n % 2

    def wide(self, dz, dh, dc):
        return ((self.z + dz) % 4) * 4 + ((self.h + dh) % 2) * 2 + (self.c + dc) % 2

    def narrow(self, dx, dl):
        return ((self.x + dx) % 4) * 2 + (self.l + dl) % 2

    def narrow_peers(self):
        return [(self.w, self.narrow(k // 2, k % 2)) for k in (2, 6, 1, 3, 7, 4, 5)]

    def wide_peers(self):
        return [(self.wide(*d), self.n) for d in ((0, 1, 0), (1, 0, 0), (3, 0, 0), (2, 0, 0), (0, 0, 1))]


class Net:
    def __init__(self, place, send_sems, recv_sems, local_sems):
        self.at = place
        self.sems = (send_sems, recv_sems, local_sems)
        self.sent, self.kept, self.open = [], [], []

    def barrier(self, givers, takers):
        bar = pltpu.get_barrier_semaphore()
        for device in givers:
            pl.semaphore_signal(bar, inc=1, device_id=device, device_id_type=MESH)
        pl.semaphore_wait(bar, takers)

    def send(self, src, dst, device):
        i = len(self.sent)
        copy = pltpu.make_async_remote_copy(
            src_ref=src,
            dst_ref=dst,
            send_sem=self.sems[0].at[i],
            recv_sem=self.sems[1].at[i],
            device_id=device,
            device_id_type=MESH,
        )
        copy.start()
        self.sent.append(copy)
        return copy

    def keep(self, src, dst):
        copy = pltpu.make_async_copy(src, dst, self.sems[2].at[len(self.kept)])
        copy.start()
        self.kept.append(copy)
        self.open.append(copy)
        return copy

    def settle(self, *copies):
        for copy in copies:
            copy.wait()
            self.open = [c for c in self.open if c is not copy]

    def run(self, tasks):
        tasks = list(tasks)
        while tasks:
            left = []
            for task in tasks:
                try:
                    next(task)
                    left.append(task)
                except StopIteration:
                    pass
            tasks = left
        for copy in self.sent:
            copy.wait_send()
        for copy in self.open:
            copy.wait()


def block_of(ref, index, rows):
    return ref.at[pl.ds(pl.multiple_of(index * rows, 16), rows)]


def narrow_gather(net, src, dst, cut, stacked=False):
    at = net.at
    me, near = at.n, at.narrow(0, 1)
    rows = src.shape[0]

    def block(n):
        return dst.at[n] if stacked else block_of(dst, n, rows)

    kept = net.keep(src, block(me))
    late = net.send(src.at[cut:], block(me).at[cut:], (at.w, near))
    turns = [(d, net.send(src, block(me), (at.w, at.narrow(d, 0)))) for d in (1, 3, 2)]
    early = net.send(src.at[:cut], block(me).at[:cut], (at.w, near))
    yield
    late.wait_recv()
    rest = [
        net.send(block(near).at[cut:], block(near).at[cut:], (at.w, at.narrow(d, 0)))
        for d in (1, 3, 2)
    ]
    yield
    for d, copy in turns:
        copy.wait_recv()
        part = block(at.narrow(-d, 0)).at[:cut]
        rest.append(net.send(part, part, (at.w, near)))
    yield
    early.wait_recv()
    for copy in rest:
        copy.wait_recv()
    net.settle(kept)


def narrow_share(net, src, dst):
    me = net.at.n
    copies = [net.send(src, dst.at[me], peer) for peer in net.at.narrow_peers()]
    kept = net.keep(src, dst.at[me])
    yield
    yield
    for copy in copies:
        copy.wait_recv()
    net.settle(kept)


def narrow_swap(net, src, dst):
    me = net.at.n
    copies = [net.send(src.at[peer[1]], dst.at[me], peer) for peer in net.at.narrow_peers()]
    net.keep(src.at[me], dst.at[me])
    yield
    yield
    yield
    for copy in copies:
        copy.wait_recv()


def add_rows(rows, step, dst, terms):
    @pl.loop(0, rows // step)
    def _(i):
        part = pl.ds(pl.multiple_of(i * step, step), step)
        total = terms[0][part, :].astype(F32)
        for term in terms[1:]:
            total += term[part, :].astype(F32)
        dst[part, :] = total.astype(dst.dtype)


def narrow_sum(net, src, slots, out, cut):
    at = net.at
    me, near = at.n, at.narrow(0, 1)
    rows = out.shape[0]

    def block(n):
        return block_of(src, n, rows)

    over = {
        d: net.send(block(at.narrow(d, 1)).at[:cut], slots.at[d - 1, :cut], (at.w, near))
        for d in (1, 3, 2)
    }
    across = {
        d: net.send(block(at.narrow(d, 1)).at[cut:], slots.at[d - 1, cut:], (at.w, at.narrow(d, 0)))
        for d in (1, 3, 2)
    }
    late = [
        net.send(block(at.narrow(d, 0)).at[cut:], slots.at[2 + d, cut:], (at.w, at.narrow(d, 0)))
        for d in (1, 3, 2)
    ]
    final = [net.send(block(near).at[:cut], slots.at[6, :cut], (at.w, near))]
    yield
    early = []
    for d in (1, 3, 2):
        over[d].wait_recv()
        term = slots.at[d - 1, :cut]
        add_rows(cut, 16, term, [term, block(at.narrow(d, 0)).at[:cut]])
        early.append(net.send(term, slots.at[2 + d, :cut], (at.w, at.narrow(d, 0))))
    yield
    for d in (1, 3, 2):
        across[d].wait_recv()
    term = slots.at[0, cut:]
    add_rows(rows - cut, 16, term, [block(near).at[cut:], *(slots.at[k, cut:] for k in range(3))])
    final.append(net.send(term, slots.at[6, cut:], (at.w, near)))
    yield
    for copy in late + early + final:
        copy.wait_recv()
    add_rows(rows, 16, out, [block(me), *(slots.at[k] for k in range(3, 7))])


def wide_gather(net, src, dst):
    at = net.at
    half = ROWS // 2
    me, far = at.w, at.wide(0, 1, 0)
    up, down = (at.wide(1, 0, 0), at.n), (at.wide(3, 0, 0), at.n)
    other = (at.wide(0, 0, 1), at.n)

    def block(w):
        return block_of(dst, w, ROWS)

    kept = net.keep(src, block(me))
    from_far = net.send(src, block(me), (far, at.n))
    turns = [[net.send(src, block(me), up), net.send(src, block(me), down)]]
    over = [net.send(src, block(me), other)]
    yield
    from_far.wait_recv()
    turns.append([net.send(block(far), block(far), up), net.send(block(far), block(far), down)])
    over.append(net.send(block(far), block(far), other))
    yield
    further = []
    for e in (0, 1):
        for d, part, ahead, copy in (
            (3, slice(0, half), up, turns[e][0]),
            (1, slice(half, ROWS), down, turns[e][1]),
        ):
            copy.wait_recv()
            shard = block(at.wide(d, e, 0))
            further.append((e, part, net.send(shard.at[part], shard.at[part], ahead)))
            over.append(net.send(shard, shard, other))
        yield
    for e, part, copy in further:
        copy.wait_recv()
        shard = block(at.wide(2, e, 0)).at[part]
        over.append(net.send(shard, shard, other))
    yield
    for copy in over:
        copy.wait_recv()
    net.settle(kept)


def wide_sum(net, src, core, turned, last, out):
    at = net.at
    half = ROWS // 2
    up, down = (at.wide(1, 0, 0), at.n), (at.wide(3, 0, 0), at.n)
    other = (at.wide(0, 0, 1), at.n)
    order = [(d, e) for d in (2, 1, 3, 0) for e in (1, 0)]

    def block(w):
        return block_of(src, w, ROWS)

    over = {(d, e): net.send(block(at.wide(d, e, 1)), core.at[d, e], other) for d, e in order}
    yield
    further = []
    for d, e in order:
        over[d, e].wait_recv()
        part = core.at[d, e]
        add_rows(ROWS, 32, part, [part, block(at.wide(d, e, 0))])
        if d == 2:
            further.append(
                (
                    e,
                    net.send(part.at[:half], turned.at[2, e, :half], up),
                    net.send(part.at[half:], turned.at[2, e, half:], down),
                )
            )
    yield
    turns = []
    for e, first, second in further:
        first.wait_recv()
        part = core.at[1, e]
        add_rows(half, 16, part.at[:half], [part.at[:half], turned.at[2, e, :half]])
        turns.append((e, net.send(part, turned.at[0, e], up)))
        second.wait_recv()
        part = core.at[3, e]
        add_rows(half, 16, part.at[half:], [part.at[half:], turned.at[2, e, half:]])
        turns.append((e, net.send(part, turned.at[1, e], down)))
        yield
    for e, copy in turns:
        if e:
            copy.wait_recv()
    part = core.at[0, 1]
    add_rows(ROWS, 32, part, [part, turned.at[0, 1], turned.at[1, 1]])
    final = net.send(part, last, (at.wide(0, 1, 0), at.n))
    yield
    for e, copy in turns:
        if not e:
            copy.wait_recv()
    final.wait_recv()
    add_rows(ROWS, 32, out, [core.at[0, 0], last, turned.at[0, 0], turned.at[1, 0]])


def step(*tasks):
    for task in tasks:
        next(task, None)


def finish(*tasks):
    tasks = list(tasks)
    while tasks:
        tasks = [task for task in tasks if next(task, "end") != "end"]


def pieces_of(width, size, body):
    whole = width // size

    @pl.loop(0, whole)
    def _(i):
        body(pl.ds(pl.multiple_of(i * size, size), size))

    if width % size:
        body(pl.ds(whole * size, width % size))


def dot(a, b):
    return jnp.dot(a, b, preferred_element_type=F32)


def dot_t(a, b):
    return lax.dot_general(a, b, (((1,), (1,)), ((), ())), preferred_element_type=F32)


def t_dot(a, b):
    return lax.dot_general(a, b, (((0,), (0,)), ((), ())), preferred_element_type=F32)


def spread(dst, pieces):
    for j in range(8):
        for k in range(2):
            dst[pl.ds(k * 256, 256), pl.ds(j * 320, 320)] = pieces[j, :, pl.ds(k * 320, 320)]


def scores(keys, queries, low, first):
    raw = dot(keys, queries) * (1.0 / math.sqrt(HEAD))
    key = first + lax.broadcasted_iota(jnp.int32, raw.shape, 0)
    query = first + WINDOW + lax.broadcasted_iota(jnp.int32, raw.shape, 1) % TILE
    return jnp.where((key >= low) & (key <= query), raw, masked)


def attention(net, ins, outs, scratch):
    x_own, cot_own, gains_own, shard_a, shard_gu, shard_d, cosine, sine, low = ins
    normed, queries, kv, lse, attended, w_a, x_rows, mid, normed_mid, inverse, gains = outs[:11]
    cot_pieces, w_gu, w_d = outs[11:]
    x_pieces, gain_pieces, x, qkv, src, slots, total, values_t = scratch
    at = net.at
    later = [((at.w + k) % 16, at.n) for k in (1, 2)]
    earlier = [((at.w + 16 - k) % 16, at.n) for k in (1, 2)]
    net.barrier(at.narrow_peers() + at.wide_peers() + earlier, 14)
    panel = wide_gather(net, shard_a, w_a)
    stream = narrow_gather(net, x_own, x_pieces, 128, True)
    sizes = narrow_share(net, gains_own, gain_pieces)
    step(panel, stream, sizes)
    step(stream, panel, stream, panel, panel)
    finish(stream, sizes)
    cots = narrow_gather(net, cot_own, cot_pieces, 128, True)
    gate_up = wide_gather(net, shard_gu, w_gu)
    step(cots)
    spread(x, x_pieces)
    for j in range(8):
        gains[:, pl.ds(j * 320, 320)] = gain_pieces[j, :, :320]

    @pl.loop(0, TOK // 16)
    def _(i):
        rows = pl.ds(pl.multiple_of(i * 16, 16), 16)
        part = x[rows, :].astype(F32)
        inv = lax.rsqrt(jnp.mean(part * part, axis=1, keepdims=True) + epsilon)
        normed[rows, :] = (part * inv * gains[0:1, :]).astype(BF)

    own = x[pl.ds(pl.multiple_of(at.n * OWN, OWN), OWN), :].astype(F32)
    x_rows[...] = own
    finish(panel)
    step(gate_up)
    for k in range(2):
        part = pl.ds(k * 256, 256)
        qkv[part, :] = dot(normed[...], w_a[:, part]).T
    cos, sin = cosine[...], sine[...]
    zeros = jnp.zeros((48, TOK), F32)

    def turned(at_row):
        a, b = qkv[pl.ds(at_row, 40), :], qkv[pl.ds(at_row + 40, 40), :]
        return jnp.concatenate([a * cos - b * sin, b * cos + a * sin, zeros], axis=0)

    mine = pl.ds(2 * TOK, TOK)
    kv[mine, :128] = turned(320).T.astype(BF)
    kv[mine, 128:] = jnp.concatenate([qkv[pl.ds(400, 80), :], zeros], axis=0).T.astype(BF)
    arriving = [
        net.send(kv.at[mine], kv.at[pl.ds((2 - k) * TOK, TOK)], later[k - 1]) for k in (1, 2)
    ]
    for head in range(4):
        one = turned(head * HEAD).astype(BF)
        for tile in range(4):
            queries[tile, :, pl.ds(head * TILE, TILE)] = one[:, tile * TILE : (tile + 1) * TILE]
    step(cots, gate_up)
    for copy in arriving:
        copy.wait_recv()
    values_t[...] = kv[:, 128:].T

    @pl.loop(0, 4)
    def _(i):
        first = pl.multiple_of(i * TILE, TILE)
        seen = pl.ds(first, REACH)
        s = scores(kv[seen, :128], queries[i], low[i], first)
        largest = jnp.max(s, axis=0, keepdims=True)
        powers = jnp.exp(s - largest)
        totals = jnp.sum(powers, axis=0, keepdims=True)
        weights = (powers / totals).astype(BF)
        lse[i] = largest + jnp.log(totals)
        mixed = dot(values_t[:, seen], weights)
        attended[pl.ds(first, TILE), :] = (
            jnp.concatenate([mixed[:HEAD, h * TILE : (h + 1) * TILE] for h in range(4)], axis=0)
            .T.astype(BF)
        )

    @pl.loop(0, D // 256)
    def _(i):
        rows = pl.ds(pl.multiple_of(i * 256, 256), 256)
        src[:, rows] = dot_t(attended[...], w_a[rows, 512:832]).astype(BF)

    summed = narrow_sum(net, src, slots, total, 32)
    step(summed, cots, gate_up, gate_up, gate_up)
    down = wide_gather(net, shard_d, w_d)
    step(down)
    finish(summed)
    step(cots, down, gate_up)
    stream = x_rows[...] + total[...]
    mid[...] = stream
    inv = lax.rsqrt(jnp.mean(stream * stream, axis=1, keepdims=True) + epsilon)
    inverse[...] = jnp.broadcast_to(inv, inverse.shape)
    normed_mid[...] = (stream * inv * gains[1:2, :]).astype(BF)
    finish(cots, gate_up, down)
    net.run([])


def mlp(net, ins, outs, scratch):
    normed_own, d_hbm, gu_hbm, cot_hbm, mid, inverse, gains = ins
    grad_mid_full, grad_mid, down_part, grad_gu, grad_d, gain_part = outs
    w_gu, w_d, normed, cot_pieces, cot, gu, grad_hidden, hidden, grad_pre, src, slots, total = scratch[:12]
    core, turned, last, low = scratch[12:]
    at = net.at
    net.barrier(at.narrow_peers() + at.wide_peers(), 12)
    gather = narrow_gather(net, normed_own, normed, 32)
    step(gather)
    pieces = net.keep(cot_hbm, cot_pieces)
    weights = net.keep(gu_hbm, w_gu), net.keep(d_hbm, w_d)
    net.settle(pieces)
    spread(cot, cot_pieces)
    step(gather)
    net.settle(*weights)

    def back_down(columns):
        grad_hidden[:, columns] = dot(cot[...], w_d[:, columns])

    pieces_of(PANEL, 256, back_down)
    finish(gather)

    def gate_up(columns):
        gu[:, columns] = dot(normed[...], w_gu[:, columns])

    pieces_of(2 * PANEL, 256, gate_up)

    @pl.loop(0, TOK // 16)
    def _(i):
        rows = pl.ds(pl.multiple_of(i * 16, 16), 16)
        gate, up, grad = gu[rows, :PANEL], gu[rows, PANEL:], grad_hidden[rows, :]
        sigmoid = jax.nn.sigmoid(gate)
        active = gate * sigmoid
        hidden[rows, :] = (active * up).astype(BF)
        grad_pre[rows, :PANEL] = (grad * up * sigmoid * (1.0 + gate * (1.0 - sigmoid))).astype(BF)
        grad_pre[rows, PANEL:] = (grad * active).astype(BF)

    def back_normed(i):
        rows = pl.ds(pl.multiple_of(i * 256, 256), 256)
        src[:, rows] = dot_t(grad_pre[...], w_gu[rows, :]).astype(BF)

    pl.loop(0, D // 256)(back_normed)
    summed = narrow_sum(net, src, slots, total, 32)
    step(summed)

    def weight_grad(left, right, dst):
        def one(i):
            rows = pl.ds(pl.multiple_of(i * 256, 256), 256)
            dst[rows, :] = t_dot(left[:, rows], right[...]).astype(BF)

        pl.loop(0, D // 256)(one)

    weight_grad(normed, grad_pre, w_gu)
    sums = [wide_sum(net, w_gu, core, turned, last, grad_gu)]
    step(*sums)
    step(summed)

    def forward_down(i):
        rows = pl.ds(pl.multiple_of(i * 256, 256), 256)
        down_part[:, rows] = dot_t(hidden[...], w_d[rows, :]).astype(BF)

    pl.loop(0, D // 256)(forward_down)
    step(*sums)
    step(summed)
    weight_grad(cot, hidden, w_d)
    net.keep(w_d, grad_d)
    finish(summed)
    inv, scale = inverse[:, :1], gains[1:2, :]
    grad, stream = total[...], mid[...]
    weighted = grad * scale
    inner = jnp.sum(weighted * stream, axis=1, keepdims=True)
    through = inv * weighted - stream * (inv * inv * inv * inner / D)
    own = cot[pl.ds(pl.multiple_of(at.n * OWN, OWN), OWN), :].astype(F32) + through
    grad_mid[...] = own
    low[...] = own.astype(BF)
    gain_part[...] = jnp.broadcast_to(
        jnp.sum(grad * stream * inv, axis=0, keepdims=True), gain_part.shape
    )
    finish(narrow_gather(net, low, grad_mid_full, 32), *sums)
    net.run([])


def attention_back(net, ins, outs, scratch):
    grad_mid, grad_mid_own, attended, queries, kv, lse, low, w_a, normed = ins[:9]
    cosine, sine, down_part, d_hbm, mid, x_rows, gains, gain_two_part = ins[9:]
    output_rows, grad_rows, gain_sums, grad_out, grad_qkv, grad_d = outs
    w_d, upstream, keys_t, grad_kv, grad_q, src, slots_one, slots_two, total_one, total_two = scratch[:10]
    later_kv, turned_back, qkv_rows, w_out, w_qkv, rows_one, rows_two, parts, narrow_parts, wide_parts = scratch[10:20]
    sum_d, sum_out, sum_qkv = scratch[20:23], scratch[23:26], scratch[26:29]
    at = net.at
    everyone = [((at.w + k) % 16, at.n) for k in range(1, 16)]
    net.barrier(at.narrow_peers() + everyone, 22)
    loaded = net.keep(d_hbm, w_d)
    downs = narrow_sum(net, down_part, slots_one, total_one, 32)
    step(downs)
    for columns in (pl.ds(0, 256), pl.ds(256, 64)):
        qkv_rows[:, columns] = dot(
            grad_mid[...], w_a[:, pl.ds(512 + columns.start, columns.size)]
        )
    grads_t = qkv_rows[...].T
    zeros = jnp.zeros((48, TOK), F32)
    for head in range(4):
        one = jnp.concatenate([grads_t[head * HEAD : (head + 1) * HEAD], zeros], axis=0).astype(BF)
        for tile in range(4):
            upstream[tile, :, pl.ds(head * TILE, TILE)] = one[:, tile * TILE : (tile + 1) * TILE]
    keys_t[...] = kv[:, :128].T
    net.settle(loaded)
    wide_d = wide_sum(net, w_d, *sum_d, grad_d)
    step(wide_d, downs)
    fill = jnp.zeros((256, 64), F32)

    @pl.loop(0, D // 256)
    def _(i):
        rows = pl.ds(pl.multiple_of(i * 256, 256), 256)
        w_out[rows, :] = jnp.concatenate(
            [t_dot(grad_mid[:, rows], attended[...]), fill], axis=1
        ).astype(BF)

    wide_out = wide_sum(net, w_out, *sum_out, grad_out)
    step(wide_d, wide_out, downs)
    grad_kv[...] = jnp.zeros(grad_kv.shape, F32)
    factor = 1.0 / math.sqrt(HEAD)

    def one_tile(i):
        first = pl.multiple_of(i * TILE, TILE)
        seen = pl.ds(first, REACH)
        s = scores(kv[seen, :128], queries[i], low[i], first)
        weights = jnp.exp(s - lse[i])
        grad_weights = dot(kv[seen, 128:], upstream[i])
        inner = jnp.sum(weights * grad_weights, axis=0, keepdims=True)
        grad_scores = (weights * (grad_weights - inner)).astype(BF)
        grad_kv[seen, 128:] += dot_t(weights.astype(BF), upstream[i])
        grad_kv[seen, :128] += dot_t(grad_scores, queries[i]) * factor
        back = dot(keys_t[:, seen], grad_scores) * factor
        for head in range(4):
            grad_q[pl.ds(head * HEAD, HEAD), pl.ds(first, TILE)] = back[
                :HEAD, head * TILE : (head + 1) * TILE
            ]

    pl.loop(0, 2)(one_tile)
    step(wide_d, wide_out)
    pl.loop(2, 4)(one_tile)
    later_kv[...] = grad_kv[pl.ds(0, 2 * TOK), :].astype(BF)
    arriving = [
        net.send(
            later_kv.at[pl.ds((2 - k) * TOK, TOK)],
            turned_back.at[2 - k],
            ((at.w + 16 - k) % 16, at.n),
        )
        for k in (1, 2)
    ]
    step(wide_d, wide_out, downs)
    cos, sin = cosine[...], sine[...]

    def unturned(part):
        a, b = part[:40], part[40:80]
        return [a * cos + b * sin, b * cos - a * sin]

    rotated = []
    for head in range(4):
        rotated += unturned(grad_q[pl.ds(head * HEAD, HEAD), :])
    rows_one_of = narrow_swap(net, rows_one, output_rows)
    finish(downs)
    by_feature(rows_one, (mid[...] + total_one[...]).astype(BF))
    step(rows_one_of)
    for copy in arriving:
        copy.wait_recv()
    whole = (
        grad_kv[pl.ds(2 * TOK, TOK), :]
        + turned_back[0].astype(F32)
        + turned_back[1].astype(F32)
    )
    rotated += unturned(whole[:, :128].T)
    rotated += [whole[:, 128:].T[:HEAD], jnp.zeros((32, TOK), F32)]
    grads = jnp.concatenate(rotated, axis=0).T.astype(BF)
    grads_ref = scratch[29]
    grads_ref[...] = grads

    @pl.loop(0, D // 256)
    def _(i):
        rows = pl.ds(pl.multiple_of(i * 256, 256), 256)
        src[:, rows] = dot_t(grads_ref[...], w_a[rows, :512]).astype(BF)

    summed = narrow_sum(net, src, slots_two, total_two, 32)
    step(summed)

    @pl.loop(0, D // 256)
    def _(i):
        rows = pl.ds(pl.multiple_of(i * 256, 256), 256)
        w_qkv[rows, :] = t_dot(normed[:, rows], grads_ref[...]).astype(BF)

    wide_qkv = wide_sum(net, w_qkv, *sum_qkv, grad_qkv)
    step(wide_qkv, wide_d, wide_out, summed, wide_qkv, summed)
    finish(summed)
    step(wide_qkv, wide_d, wide_out)
    stream, grad = x_rows[...], total_two[...]
    inv = lax.rsqrt(jnp.mean(stream * stream, axis=1, keepdims=True) + epsilon)
    weighted = grad * gains[0:1, :]
    inner = jnp.sum(weighted * stream, axis=1, keepdims=True)
    through = inv * weighted - stream * (inv * inv * inv * inner / D)
    by_feature(rows_two, (grad_mid_own[...] + through).astype(BF))
    back = narrow_swap(net, rows_two, grad_rows)
    step(back)
    gain_one = jnp.sum(grad * stream * inv, axis=0, keepdims=True)
    both = jnp.concatenate([gain_one, gain_two_part[0:1, :], jnp.zeros((6, D), F32)], axis=0)
    for j in range(8):
        parts[j, :, :320] = both[:, j * 320 : (j + 1) * 320]
        parts[j, :, 320:] = jnp.zeros((8, 64), F32)
    me = at.n
    copies = [net.send(parts.at[p[1]], narrow_parts.at[me], p) for p in at.narrow_peers()]
    narrow_parts[me] = parts[me]
    step(wide_qkv, wide_d, wide_out)
    for copy in copies:
        copy.wait_recv()
    sum_parts = narrow_parts[0]
    for k in range(1, 8):
        sum_parts += narrow_parts[k]
    wide_parts[0] = sum_parts
    copies = [
        net.send(wide_parts.at[0], wide_parts.at[k + 1], p) for k, p in enumerate(everyone)
    ]
    step(wide_qkv, wide_d, wide_out)
    for copy in copies:
        copy.wait_recv()
    sum_parts = wide_parts[0]
    for k in range(1, 16):
        sum_parts += wide_parts[k]
    gain_sums[...] = sum_parts
    finish(wide_d, wide_out, wide_qkv, rows_one_of, back)
    net.run([])


def by_feature(dst, rows):
    for j in range(8):
        dst[j] = rows[:, j * 320 : (j + 1) * 320]


def wide_sum_scratch(columns):
    return [
        pltpu.VMEM((4, 2, ROWS, columns), BF),
        pltpu.VMEM((3, 2, ROWS, columns), BF),
        pltpu.VMEM((ROWS, columns), BF),
    ]


def vmem():
    return pl.BlockSpec(memory_space=pltpu.VMEM)


def hbm():
    return pl.BlockSpec(memory_space=pl.ANY)


def exchange(name, number, body, ins, outs, scratch=(), sends=160, keeps=16):
    def kernel(*refs):
        a, b = len(ins), len(ins) + len(outs)
        net = Net(Place(), *refs[-3:])
        body(net, refs[:a], refs[a:b], refs[b:-3])

    return pl.pallas_call(
        kernel,
        out_shape=[jax.ShapeDtypeStruct(shape, dtype) for shape, dtype, _ in outs],
        in_specs=[spec for _, spec in ins],
        out_specs=[spec for _, _, spec in outs],
        scratch_shapes=[
            *scratch,
            pltpu.SemaphoreType.DMA((sends,)),
            pltpu.SemaphoreType.DMA((sends,)),
            pltpu.SemaphoreType.DMA((keeps,)),
        ],
        compiler_params=pltpu.CompilerParams(
            collective_id=number, has_side_effects=True, vmem_limit_bytes=58 * 2**20
        ),
        name=name,
    )(*[array for array, _ in ins])


def documents(doc_lengths, places):
    ends_at = jnp.cumsum(doc_lengths)
    passed = places[:, None] >= ends_at[None, :]
    segment = jnp.sum(passed.astype(jnp.int32), axis=1)
    begins = jnp.sum(jnp.where(passed, doc_lengths[None, :], 0), axis=1)
    return (segment, places - begins)


def scaled_freqs():
    half_width = HEAD // 2
    freqs = rope_base ** (-2.0 * jnp.arange(half_width, dtype=jnp.float32) / HEAD)
    wavelen = 2.0 * math.pi / freqs
    smooth = (long_wave / wavelen - 1.0) / 3.0
    blended = (1.0 - smooth) * freqs / rope_factor + smooth * freqs
    return jnp.where(
        wavelen < short_wave, freqs, jnp.where(wavelen > long_wave, freqs / rope_factor, blended)
    )


def rope_tables(position):
    freqs = scaled_freqs()
    angles = freqs[:, None] * position.astype(jnp.float32)[None, :]
    return (jnp.cos(angles), jnp.sin(angles))


def packed(block):
    return jnp.concatenate([block[: TOK // 2], block[TOK // 2 :]], axis=1)


def body(
    layer_input,
    gain_attn,
    w_query,
    w_key,
    w_value,
    w_out,
    gain_mlp,
    w_gate,
    w_up,
    w_down,
    doc_lengths,
    cotangent,
):
    me_w = lax.axis_index("wide")
    shard_a = jnp.concatenate(
        [w_query, w_key, w_value, jnp.zeros((ROWS, 32), BF), w_out.T, jnp.zeros((ROWS, 64), BF)],
        axis=1,
    )
    shard_gu = jnp.concatenate([w_gate, w_up], axis=1)
    gains_own = jnp.zeros((8, 384), F32).at[0, :320].set(gain_attn).at[1, :320].set(gain_mlp)
    places = me_w * TOK + jnp.arange(TOK, dtype=jnp.int32)
    position = documents(doc_lengths, places)[1]
    cosine, sine = rope_tables(position)
    low = jnp.maximum(places - jnp.minimum(position, WINDOW - 1), 0) - (me_w - 2) * TOK
    low = jnp.broadcast_to(low.reshape(4, 1, 1, TILE), (4, 1, 4, TILE)).reshape(4, 1, 4 * TILE)

    def held(*shape, dtype=BF):
        return (shape, dtype, vmem())

    def far(*shape, dtype=BF):
        return (shape, dtype, hbm())

    def room(*shape, dtype=BF):
        return pltpu.VMEM(shape, dtype)

    def local(*arrays):
        return [(a, vmem()) for a in arrays]

    def remote(*arrays):
        return [(a, hbm()) for a in arrays]

    slots = room(7, OWN, D)
    (
        normed,
        queries,
        kv,
        lse,
        attended,
        w_a,
        x_rows,
        mid,
        normed_mid,
        inverse,
        gains,
        cot_pieces,
        full_gu,
        full_d,
    ) = exchange(
        "attention",
        1,
        attention,
        remote(packed(layer_input), packed(cotangent), gains_own, shard_a, shard_gu, w_down.T)
        + local(cosine, sine, low),
        [
            held(TOK, D),
            held(4, TILE, 4 * TILE),
            held(3 * TOK, 256),
            held(4, 1, 4 * TILE, dtype=F32),
            held(TOK, 320),
            held(D, PANEL),
            held(OWN, D, dtype=F32),
            held(OWN, D, dtype=F32),
            held(OWN, D),
            held(OWN, 128, dtype=F32),
            held(8, D, dtype=F32),
            far(8, TOK // 2, 640),
            far(D, 2 * PANEL),
            far(D, PANEL),
        ],
        [
            room(8, TOK // 2, 640),
            room(8, 8, 384, dtype=F32),
            room(TOK, D),
            room(512, TOK, dtype=F32),
            room(TOK, D),
            slots,
            room(OWN, D, dtype=F32),
            room(TILE, 3 * TOK),
        ],
    )
    grad_mid, grad_mid_own, down_part, grad_gu_sum, grad_d_part, gain_two_part = exchange(
        "mlp",
        2,
        mlp,
        local(normed_mid) + remote(full_d, full_gu, cot_pieces) + local(mid, inverse, gains),
        [
            held(TOK, D),
            held(OWN, D, dtype=F32),
            held(TOK, D),
            held(ROWS, 2 * PANEL, dtype=F32),
            far(D, PANEL),
            held(8, D, dtype=F32),
        ],
        [
            room(D, 2 * PANEL),
            room(D, PANEL),
            room(TOK, D),
            room(8, TOK // 2, 640),
            room(TOK, D),
            room(TOK, 2 * PANEL, dtype=F32),
            room(TOK, PANEL, dtype=F32),
            room(TOK, PANEL),
            room(TOK, 2 * PANEL),
            room(TOK, D),
            slots,
            room(OWN, D, dtype=F32),
            *wide_sum_scratch(2 * PANEL),
            room(OWN, D),
        ],
    )
    output_rows, grad_rows, gain_sums, grad_out, grad_qkv, grad_d = exchange(
        "attention_back",
        3,
        attention_back,
        local(grad_mid, grad_mid_own, attended, queries, kv, lse, low, w_a, normed)
        + local(cosine, sine, down_part)
        + remote(grad_d_part)
        + local(mid, x_rows, gains, gain_two_part),
        [
            far(8, OWN, 320),
            far(8, OWN, 320),
            held(8, 384, dtype=F32),
            held(ROWS, 384, dtype=F32),
            held(ROWS, 512, dtype=F32),
            held(ROWS, PANEL, dtype=F32),
        ],
        [
            room(D, PANEL),
            room(4, TILE, 4 * TILE),
            room(TILE, 3 * TOK),
            room(3 * TOK, 256, dtype=F32),
            room(320, TOK, dtype=F32),
            room(TOK, D),
            slots,
            slots,
            room(OWN, D, dtype=F32),
            room(OWN, D, dtype=F32),
            room(2 * TOK, 256),
            room(2, TOK, 256),
            room(TOK, 320, dtype=F32),
            room(D, 384),
            room(D, 512),
            room(8, OWN, 320),
            room(8, OWN, 320),
            room(8, 8, 384, dtype=F32),
            room(8, 8, 384, dtype=F32),
            room(16, 8, 384, dtype=F32),
            *wide_sum_scratch(PANEL),
            *wide_sum_scratch(384),
            *wide_sum_scratch(512),
            room(TOK, 512),
        ],
    )
    return (
        output_rows.reshape(TOK, 320),
        grad_rows.reshape(TOK, 320).astype(F32),
        gain_sums[0, :320],
        grad_qkv[:, :320],
        grad_qkv[:, 320:400],
        grad_qkv[:, 400:480],
        grad_out[:, :320].T,
        gain_sums[1, :320],
        grad_gu_sum[:, :PANEL],
        grad_gu_sum[:, PANEL:],
        grad_d.T,
    )


def solution(mesh):
    rows, columns = P("wide", "narrow"), P("narrow", "wide")
    return jax.shard_map(
        body,
        mesh=mesh,
        in_specs=(
            rows,
            P("narrow"),
            rows,
            rows,
            rows,
            columns,
            P("narrow"),
            rows,
            rows,
            columns,
            P(),
            rows,
        ),
        out_specs=(
            rows,
            rows,
            P("narrow"),
            rows,
            rows,
            rows,
            columns,
            P("narrow"),
            rows,
            rows,
            columns,
        ),
        check_vma=False,
    )
```

```python
import functools
import math

import jax
import jax.numpy as jnp
import numpy as np
from jax import lax
from jax.experimental import pallas as pl
from jax.experimental.pallas import tpu as pltpu
from jax.sharding import PartitionSpec as P

D = 2560
HEADS = 32
KV_HEADS = 8
HEAD = 80
WINDOW = 1024
TOK = 512
OWN = 64
ROWS = 160
PANEL = 896
TILE = 128
REACH = WINDOW + TILE

epsilon = 1e-05
rope_base = 1000000.0
rope_factor = 8.0
long_wave = 8192.0
short_wave = 2048.0
masked = -1e30

MESH = pl.DeviceIdType.MESH
BF = jnp.bfloat16
F32 = jnp.float32


class Place:
    def __init__(self):
        self.w = lax.axis_index("wide")
        self.n = lax.axis_index("narrow")
        self.z, self.h, self.c = self.w // 4, (self.w // 2) % 2, self.w % 2
        self.x, self.l = self.n // 2, self.n % 2

    def wide(self, dz, dh, dc):
        return ((self.z + dz) % 4) * 4 + ((self.h + dh) % 2) * 2 + (self.c + dc) % 2

    def narrow(self, dx, dl):
        return ((self.x + dx) % 4) * 2 + (self.l + dl) % 2

    def narrow_peers(self):
        return [(self.w, self.narrow(k // 2, k % 2)) for k in (2, 6, 1, 3, 7, 4, 5)]

    def wide_peers(self):
        return [(self.wide(*d), self.n) for d in ((0, 1, 0), (1, 0, 0), (3, 0, 0), (2, 0, 0), (0, 0, 1))]


class Net:
    def __init__(self, place, send_sems, recv_sems, local_sems):
        self.at = place
        self.sems = (send_sems, recv_sems, local_sems)
        self.sent, self.kept, self.open, self.done = [], [], [], 0

    def barrier(self, givers, takers):
        bar = pltpu.get_barrier_semaphore()
        for device in givers:
            pl.semaphore_signal(bar, inc=1, device_id=device, device_id_type=MESH)
        pl.semaphore_wait(bar, takers)

    def send(self, src, dst, device):
        i = len(self.sent)
        copy = pltpu.make_async_remote_copy(
            src_ref=src,
            dst_ref=dst,
            send_sem=self.sems[0].at[i],
            recv_sem=self.sems[1].at[i],
            device_id=device,
            device_id_type=MESH,
        )
        copy.start()
        self.sent.append(copy)
        return copy

    def keep(self, src, dst):
        copy = pltpu.make_async_copy(src, dst, self.sems[2].at[len(self.kept)])
        copy.start()
        self.kept.append(copy)
        self.open.append(copy)
        return copy

    def settle(self, *copies):
        for copy in copies:
            copy.wait()
            self.open = [c for c in self.open if c is not copy]

    def release(self, count):
        for copy in self.sent[self.done : count]:
            copy.wait_send()
        self.done = count

    def run(self, tasks):
        tasks = list(tasks)
        while tasks:
            left = []
            for task in tasks:
                try:
                    next(task)
                    left.append(task)
                except StopIteration:
                    pass
            tasks = left
        for copy in self.sent[self.done :]:
            copy.wait_send()
        for copy in self.open:
            copy.wait()


def block_of(ref, index, rows):
    return ref.at[pl.ds(pl.multiple_of(index * rows, 16), rows)]


def narrow_gather(net, src, dst, cut, stacked=False):
    at = net.at
    me, near = at.n, at.narrow(0, 1)
    rows = src.shape[0]

    def block(n):
        return dst.at[n] if stacked else block_of(dst, n, rows)

    kept = net.keep(src, block(me))
    late = net.send(src.at[cut:], block(me).at[cut:], (at.w, near))
    turns = [(d, net.send(src, block(me), (at.w, at.narrow(d, 0)))) for d in (1, 3, 2)]
    early = net.send(src.at[:cut], block(me).at[:cut], (at.w, near))
    yield
    late.wait_recv()
    rest = [
        net.send(block(near).at[cut:], block(near).at[cut:], (at.w, at.narrow(d, 0)))
        for d in (1, 3, 2)
    ]
    yield
    for d, copy in turns:
        copy.wait_recv()
        part = block(at.narrow(-d, 0)).at[:cut]
        rest.append(net.send(part, part, (at.w, near)))
    yield
    early.wait_recv()
    for copy in rest:
        copy.wait_recv()
    net.settle(kept)


def narrow_share(net, src, dst):
    me = net.at.n
    copies = [net.send(src, dst.at[me], peer) for peer in net.at.narrow_peers()]
    kept = net.keep(src, dst.at[me])
    yield
    yield
    for copy in copies:
        copy.wait_recv()
    net.settle(kept)


def narrow_swap(net, src, dst):
    me = net.at.n
    copies = [net.send(src.at[peer[1]], dst.at[me], peer) for peer in net.at.narrow_peers()]
    kept = net.keep(src.at[me], dst.at[me])
    yield
    for copy in copies:
        copy.wait_recv()
    net.settle(kept)


def add_rows(rows, step, dst, terms):
    @pl.loop(0, rows // step)
    def _(i):
        part = pl.ds(pl.multiple_of(i * step, step), step)
        total = terms[0][part, :].astype(F32)
        for term in terms[1:]:
            total += term[part, :].astype(F32)
        dst[part, :] = total.astype(dst.dtype)


def narrow_sum(net, src, slots, out, cut, held=None):
    at = net.at
    me, near = at.n, at.narrow(0, 1)
    rows = out.shape[0]

    def block(n):
        return block_of(src, n, rows)

    def term_of(n):
        return block_of(src if held is None else held, n, rows)

    over = {
        d: net.send(block(at.narrow(d, 1)).at[:cut], slots.at[d - 1, :cut], (at.w, near))
        for d in (1, 3, 2)
    }
    across = {
        d: net.send(block(at.narrow(d, 1)).at[cut:], slots.at[d - 1, cut:], (at.w, at.narrow(d, 0)))
        for d in (1, 3, 2)
    }
    late = [
        net.send(block(at.narrow(d, 0)).at[cut:], slots.at[2 + d, cut:], (at.w, at.narrow(d, 0)))
        for d in (1, 3, 2)
    ]
    final = [net.send(block(near).at[:cut], slots.at[6, :cut], (at.w, near))]
    yield
    early = []
    for d in (1, 3, 2):
        over[d].wait_recv()
        term = slots.at[d - 1, :cut]
        add_rows(cut, 16, term, [term, term_of(at.narrow(d, 0)).at[:cut]])
        early.append(net.send(term, slots.at[2 + d, :cut], (at.w, at.narrow(d, 0))))
    yield
    for d in (1, 3, 2):
        across[d].wait_recv()
    term = slots.at[0, cut:]
    add_rows(rows - cut, 16, term, [term_of(near).at[cut:], *(slots.at[k, cut:] for k in range(3))])
    final.append(net.send(term, slots.at[6, cut:], (at.w, near)))
    yield
    for copy in late + early + final:
        copy.wait_recv()
    add_rows(rows, 16, out, [term_of(me), *(slots.at[k] for k in range(3, 7))])


def wide_gather(net, src, dst):
    at = net.at
    half = ROWS // 2
    me, far = at.w, at.wide(0, 1, 0)
    up, down = (at.wide(1, 0, 0), at.n), (at.wide(3, 0, 0), at.n)
    other = (at.wide(0, 0, 1), at.n)

    def block(w):
        return block_of(dst, w, ROWS)

    kept = net.keep(src, block(me))
    turns = [[net.send(src, block(me), up), net.send(src, block(me), down)]]
    over = [net.send(src, block(me), other)]
    further = []

    def relay(e):
        for d, part, ahead, copy in (
            (3, slice(0, half), up, turns[e][0]),
            (1, slice(half, ROWS), down, turns[e][1]),
        ):
            copy.wait_recv()
            shard = block(at.wide(d, e, 0))
            further.append((e, part, net.send(shard.at[part], shard.at[part], ahead)))
            over.append(net.send(shard, shard, other))

    yield
    from_far = net.send(src, block(me), (far, at.n))
    yield
    relay(0)
    yield
    from_far.wait_recv()
    turns.append([net.send(block(far), block(far), up), net.send(block(far), block(far), down)])
    over.append(net.send(block(far), block(far), other))
    yield
    relay(1)
    yield
    for e, part, copy in further:
        copy.wait_recv()
        shard = block(at.wide(2, e, 0)).at[part]
        over.append(net.send(shard, shard, other))
    yield
    for copy in over:
        copy.wait_recv()
    net.settle(kept)


def wide_sum(net, src, core, turned, last, outs, held=None):
    at = net.at
    half = ROWS // 2
    up, down = (at.wide(1, 0, 0), at.n), (at.wide(3, 0, 0), at.n)
    other = (at.wide(0, 0, 1), at.n)
    order = [(d, e) for d in (2, 1, 3, 0) for e in (1, 0)]

    def block(w):
        return block_of(src, w, ROWS)

    over = {(d, e): net.send(block(at.wide(d, e, 1)), core.at[d, e], other) for d, e in order}
    yield
    further = []
    for d, e in order:
        over[d, e].wait_recv()
        part = core.at[d, e]
        add_rows(ROWS, 32, part, [part, block(at.wide(d, e, 0)) if held is None else held.at[d, e]])
        if d == 2:
            further.append(
                (
                    e,
                    net.send(part.at[:half], turned.at[2, e, :half], up),
                    net.send(part.at[half:], turned.at[2, e, half:], down),
                )
            )
    yield
    turns = []
    for e, first, second in further:
        first.wait_recv()
        part = core.at[1, e]
        add_rows(half, 16, part.at[:half], [part.at[:half], turned.at[2, e, :half]])
        turns.append((e, net.send(part, turned.at[0, e], up)))
        second.wait_recv()
        part = core.at[3, e]
        add_rows(half, 16, part.at[half:], [part.at[half:], turned.at[2, e, half:]])
        turns.append((e, net.send(part, turned.at[1, e], down)))
        yield
    for e, copy in turns:
        if e:
            copy.wait_recv()
    part = core.at[0, 1]
    add_rows(ROWS, 32, part, [part, turned.at[0, 1], turned.at[1, 1]])
    final = net.send(part, last, (at.wide(0, 1, 0), at.n))
    yield
    for e, copy in turns:
        if not e:
            copy.wait_recv()
    final.wait_recv()

    @pl.loop(0, ROWS // 32)
    def _(i):
        part = pl.ds(pl.multiple_of(i * 32, 32), 32)
        total = core[0, 0, part, :].astype(F32) + last[part, :].astype(F32)
        for d in range(2):
            total += turned[d, 0, part, :].astype(F32)
        for out, first, columns in outs:
            out[part, :] = total[:, first : first + columns]


def step(*tasks):
    for task in tasks:
        next(task, None)


def finish(*tasks):
    tasks = list(tasks)
    while tasks:
        tasks = [task for task in tasks if next(task, "end") != "end"]


def pieces_of(width, size, body):
    whole = width // size

    @pl.loop(0, whole)
    def _(i):
        body(pl.ds(pl.multiple_of(i * size, size), size))

    if width % size:
        body(pl.ds(whole * size, width % size))


def dot(a, b):
    return jnp.dot(a, b, preferred_element_type=F32)


def dot_t(a, b):
    return lax.dot_general(a, b, (((1,), (1,)), ((), ())), preferred_element_type=F32)


def t_dot(a, b):
    return lax.dot_general(a, b, (((0,), (0,)), ((), ())), preferred_element_type=F32)


def scores(keys, queries, low, first):
    raw = dot(keys, queries) * (1.0 / math.sqrt(HEAD))
    key = first + lax.broadcasted_iota(jnp.int32, raw.shape, 0)
    query = first + WINDOW + lax.broadcasted_iota(jnp.int32, raw.shape, 1) % TILE
    return jnp.where((key >= low) & (key <= query), raw, masked)


def by_feature(dst, rows):
    for j in range(8):
        dst[j] = rows[:, j * 320 : (j + 1) * 320]


def every(size, body):
    @pl.loop(0, D // size)
    def _(i):
        body(pl.ds(pl.multiple_of(i * size, size), size))


def attention(net, ins, outs, scratch):
    x_own, cot_own, w_query, w_key, w_value, w_out, w_gate, w_up, gain_one, gain_two, freqs, lengths = ins
    normed_far, w_qkv_far, w_out_far, cot, w_gu = outs[:5]
    queries, kv, lse, low, tables, attended, x_rows, mid, normed_mid, inverse, gains = outs[5:]
    (
        shard_qkv,
        shard_out,
        shard_gu,
        gains_own,
        gain_pieces,
        w_qkv,
        w_o,
        x_t,
        x,
        normed,
        qkv,
        src,
        slots,
        total,
        values_t,
    ) = scratch
    at = net.at
    later = [((at.w + k) % 16, at.n) for k in (1, 2)]
    earlier = [((at.w + 16 - k) % 16, at.n) for k in (1, 2)]
    shard_qkv[:, :320] = w_query[...]
    shard_qkv[:, 320:] = jnp.concatenate(
        [w_key[...], w_value[...], jnp.zeros((ROWS, 32), BF)], axis=1
    )
    gains_own[...] = jnp.zeros(gains_own.shape, F32)
    gains_own[0:1, :320] = gain_one[...].reshape(1, 320)
    gains_own[1:2, :320] = gain_two[...].reshape(1, 320)
    net.barrier(at.narrow_peers() + at.wide_peers() + earlier, 14)
    panel = wide_gather(net, shard_qkv, w_qkv)
    step(panel, panel)
    stream = narrow_gather(net, x_own, x_t, 160)
    sizes = narrow_share(net, gains_own, gain_pieces)
    step(stream, sizes)
    shard_out[...] = jnp.concatenate([w_out[...], jnp.zeros((ROWS, 64), BF)], axis=1)
    shard_gu[:, :PANEL] = w_gate[...]
    shard_gu[:, PANEL:] = w_up[...]

    place = at.w * TOK + lax.broadcasted_iota(jnp.int32, (1, TOK), 1)
    begins, end = jnp.zeros((1, TOK), jnp.int32), 0
    for k in range(8):
        end = end + lengths[k]
        begins = jnp.where(place >= end, end, begins)
    position = place - begins
    angles = freqs[:, 0:1] * position.astype(F32)
    cos, sin = jnp.cos(angles), jnp.sin(angles)
    tables[0], tables[1] = cos, sin
    first_key = jnp.maximum(begins, jnp.maximum(place - (WINDOW - 1), 0)) - (at.w - 2) * TOK
    for tile in range(4):
        one = first_key[:, tile * TILE : (tile + 1) * TILE]
        low[tile] = jnp.concatenate([one] * 4, axis=1)

    step(stream, panel, panel, panel)
    w_outs = wide_gather(net, shard_out, w_o)
    gate_up = wide_gather(net, shard_gu, w_gu)
    step(w_outs, w_outs, gate_up, stream, panel)
    finish(stream, sizes, panel)
    step(gate_up)
    for j in range(8):
        gains[:, pl.ds(j * 320, 320)] = gain_pieces[j, :, :320]
    every(256, lambda rows: turned_over(x, x_t, rows))

    @pl.loop(0, TOK // 16)
    def _(i):
        rows = pl.ds(pl.multiple_of(i * 16, 16), 16)
        part = x[rows, :].astype(F32)
        inv = lax.rsqrt(jnp.mean(part * part, axis=1, keepdims=True) + epsilon)
        normed[rows, :] = (part * inv * gains[0:1, :]).astype(BF)

    for h in range(2):
        x_rows[pl.ds(h * 32, 32), :] = x[own_rows(at, h), :].astype(F32)
    for k in range(2):
        part = pl.ds(k * 256, 256)
        qkv[part, :] = dot(normed[...], w_qkv[:, part]).T
    zeros = jnp.zeros((48, TOK), F32)

    def turned(at_row):
        a, b = qkv[pl.ds(at_row, 40), :], qkv[pl.ds(at_row + 40, 40), :]
        return jnp.concatenate([a * cos - b * sin, b * cos + a * sin, zeros], axis=0)

    mine = pl.ds(2 * TOK, TOK)
    kv[mine, :128] = turned(320).T.astype(BF)
    kv[mine, 128:] = jnp.concatenate([qkv[pl.ds(400, 80), :], zeros], axis=0).T.astype(BF)
    arriving = [
        net.send(kv.at[mine], kv.at[pl.ds((2 - k) * TOK, TOK)], later[k - 1]) for k in (1, 2)
    ]
    cots = narrow_gather(net, cot_own, cot, 160)
    step(cots)
    net.keep(normed, normed_far)
    net.keep(w_qkv, w_qkv_far)
    for head in range(4):
        one = turned(head * HEAD).astype(BF)
        for tile in range(4):
            queries[tile, :, pl.ds(head * TILE, TILE)] = one[:, tile * TILE : (tile + 1) * TILE]
    step(w_outs, w_outs)
    for copy in arriving:
        copy.wait_recv()
    step(w_outs)
    values_t[...] = kv[:, 128:].T

    def one_tile(i):
        first = pl.multiple_of(i * TILE, TILE)
        seen = pl.ds(first, REACH)
        s = scores(kv[seen, :128], queries[i], low[i], first)
        largest = jnp.max(s, axis=0, keepdims=True)
        powers = jnp.exp(s - largest)
        totals = jnp.sum(powers, axis=0, keepdims=True)
        weights = (powers / totals).astype(BF)
        lse[i] = largest + jnp.log(totals)
        mixed = dot(values_t[:, seen], weights)
        attended[pl.ds(first, TILE), :] = (
            jnp.concatenate([mixed[:HEAD, h * TILE : (h + 1) * TILE] for h in range(4)], axis=0)
            .T.astype(BF)
        )

    def out_part(h):
        tokens = pl.ds(h * 256, 256)

        def columns(rows):
            src[tokens, rows] = dot_t(attended[tokens, :], w_o[rows, :320]).astype(BF)

        every(256, columns)
        return narrow_sum(
            net, src.at[tokens], slots.at[h], total.at[pl.ds(h * 32, 32)], 16
        )

    def norm_part(h):
        rows = pl.ds(h * 32, 32)
        stream = x_rows[rows, :] + total[rows, :]
        mid[rows, :] = stream
        inv = lax.rsqrt(jnp.mean(stream * stream, axis=1, keepdims=True) + epsilon)
        inverse[rows, :] = jnp.broadcast_to(inv, (32, 128))
        normed_mid[rows, :] = (stream * inv * gains[1:2, :]).astype(BF)

    step(gate_up)
    pl.loop(0, 2)(one_tile)
    finish(w_outs)
    net.keep(w_o, w_out_far)
    early = out_part(0)
    step(early, gate_up, cots)
    pl.loop(2, 4)(one_tile)
    step(early)
    late = out_part(1)
    step(late, early, gate_up, late, cots)
    finish(early)
    norm_part(0)
    step(late, gate_up)
    finish(late)
    norm_part(1)
    finish(cots, gate_up)
    net.run([])


def own_rows(at, h):
    return pl.ds(pl.multiple_of(h * 256 + at.n * 32, 32), 32)


def turned_over(dst, src, rows):
    dst[:, rows] = src[rows, :].T


def mlp(net, ins, outs, scratch):
    normed_own, w_down, gu_far, cot_far, mid, inverse, gains = ins
    grad_mid_far, grad_mid, down_far, grad_gate, du_far, gain_part = outs
    shard_d, w_gu, w_d, normed, cot_t, cot, gu, grad_hidden, hidden, grad_pre, src = scratch[:11]
    down_part, slots, total, core, turned, last, low, grad_mid_full = scratch[11:]
    at = net.at
    shard_d[...] = w_down[...]
    net.barrier(at.narrow_peers() + at.wide_peers(), 12)
    tokens = [pl.ds(0, 256), pl.ds(256, 256)]
    own = [pl.ds(0, 32), pl.ds(32, 32)]
    gathers = [narrow_gather(net, normed_own.at[own[h]], normed.at[tokens[h]], 16) for h in (0, 1)]
    panel = wide_gather(net, shard_d, w_d)
    step(panel, gathers[0], panel)
    cots, weights = net.keep(cot_far, cot_t), net.keep(gu_far, w_gu)
    step(gathers[0], gathers[1])
    net.settle(cots)
    every(256, lambda rows: turned_over(cot, cot_t, rows))
    step(panel, gathers[1], panel, gathers[0], panel)
    net.settle(weights)
    finish(gathers[0])

    def gate_up(h):
        def part(columns):
            gu[tokens[h], columns] = dot(normed[tokens[h], :], w_gu[:, columns])

        pieces_of(2 * PANEL, 256, part)

    def back_down(h):
        def part(columns):
            grad_hidden[tokens[h], columns] = dot(cot[tokens[h], :], w_d[:, columns])

        pieces_of(PANEL, 256, part)

    def back_hidden(h):
        @pl.loop(h * 16, h * 16 + 16)
        def _(i):
            rows = pl.ds(pl.multiple_of(i * 16, 16), 16)
            gate, up, grad = gu[rows, :PANEL], gu[rows, PANEL:], grad_hidden[rows, :]
            sigmoid = jax.nn.sigmoid(gate)
            active = gate * sigmoid
            hidden[rows, :] = (active * up).astype(BF)
            grad_pre[rows, :PANEL] = (
                grad * up * sigmoid * (1.0 + gate * (1.0 - sigmoid))
            ).astype(BF)
            grad_pre[rows, PANEL:] = (grad * active).astype(BF)

    def back_normed(h):
        def part(rows):
            src[tokens[h], rows] = dot_t(grad_pre[tokens[h], :], w_gu[rows, :]).astype(BF)

        every(256, part)
        return narrow_sum(net, src.at[tokens[h]], slots.at[h], total.at[own[h]], 16)

    def back_norm(h):
        inv, scale = inverse[own[h], :1], gains[1:2, :]
        grad, stream = total[own[h], :], mid[own[h], :]
        weighted = grad * scale
        inner = jnp.sum(weighted * stream, axis=1, keepdims=True)
        through = inv * weighted - stream * (inv * inv * inv * inner / D)
        mine = cot[own_rows(at, h), :].astype(F32) + through
        grad_mid[own[h], :] = mine
        low[own[h], :] = mine.astype(BF)
        return narrow_gather(net, low.at[own[h]], grad_mid_full.at[tokens[h]], 16)

    gate_up(0)
    step(gathers[1], panel)
    finish(panel)
    gathered = len(net.sent)
    back_down(0)
    back_hidden(0)
    sums = [back_normed(0)]
    step(sums[0])
    finish(gathers[1])
    gate_up(1)
    step(sums[0])
    back_down(1)
    back_hidden(1)
    sums.append(back_normed(1))
    step(sums[1], sums[0])

    def grad_gate_rows(rows):
        w_gu[rows, :PANEL] = t_dot(normed[:, rows], grad_pre[:, :PANEL]).astype(BF)

    every(256, grad_gate_rows)
    wide = wide_sum(net, w_gu.at[:, pl.ds(0, PANEL)], core, turned, last, [(grad_gate, 0, PANEL)])
    step(wide, sums[1])
    finish(sums[0])
    back = [back_norm(0)]
    step(back[0], sums[1])

    def grad_up_rows(rows):
        w_gu[rows, PANEL:] = t_dot(normed[:, rows], grad_pre[:, PANEL:]).astype(BF)

    every(256, grad_up_rows)
    net.keep(w_gu.at[:, pl.ds(PANEL, PANEL)], du_far.at[:, pl.ds(PANEL, PANEL)])
    finish(sums[1])
    back.append(back_norm(1))
    step(back[0], back[1], wide)

    def forward_down(rows):
        down_part[:, rows] = dot_t(hidden[...], w_d[rows, :]).astype(BF)

    every(256, forward_down)
    net.keep(down_part, down_far)
    step(back[1], back[0], wide)
    net.release(gathered)

    def grad_d_rows(rows):
        w_d[rows, :] = dot(cot_t[rows, :], hidden[...]).astype(BF)

    every(256, grad_d_rows)
    net.keep(w_d, du_far.at[:, pl.ds(0, PANEL)])
    finish(back[0])
    step(back[1], wide)
    grad, stream = total[...], mid[...]
    gain_part[...] = jnp.broadcast_to(
        jnp.sum(grad * stream * inverse[:, :1], axis=0, keepdims=True), gain_part.shape
    )
    finish(back[1])
    net.keep(grad_mid_full, grad_mid_far)
    finish(wide)
    net.run([])


def attention_back(net, ins, outs, scratch):
    grad_mid_far, normed_far, w_qkv_far, w_out_far, down_far, du_far = ins[:6]
    grad_mid_own, attended, queries, kv, lse, low, tables, mid, x_rows, gains, gain_two_part = ins[6:]
    back_one, back_two, wide_parts, grad_out, grad_query, grad_key, grad_value, grad_d, grad_up = outs
    grad_mid, normed, w_qkv, w_o, down_part, held_du = scratch[:6]
    upstream, keys_t, grad_kv, grad_q, slots_one, slots_two, total_one, total_two = scratch[6:14]
    later_kv, turned_back, ga, rows_one, rows_two, parts, narrow_parts, grads_ref = scratch[14:22]
    sum_du, sum_out, sum_qkv = scratch[22:25], scratch[25:28], scratch[28:31]
    at = net.at
    tokens = [pl.ds(0, 256), pl.ds(256, 256)]
    own = [pl.ds(0, 32), pl.ds(32, 32)]
    loads = [net.keep(a, b) for a, b in zip(ins[:5], (grad_mid, normed, w_qkv, w_o, down_part))]
    held_loads = [
        net.keep(block_of(du_far, at.wide(d, e, 0), ROWS), held_du.at[d, e])
        for d in range(4)
        for e in range(2)
    ]
    everyone = [((at.w + k) % 16, at.n) for k in range(1, 16)]
    net.barrier(at.narrow_peers() + everyone, 22)
    wide_du = wide_sum(
        net, du_far, *sum_du, [(grad_d, 0, PANEL), (grad_up, PANEL, PANEL)], held_du
    )
    downs = [
        narrow_sum(
            net, down_far.at[tokens[h]], slots_one.at[h], total_one.at[own[h]], 16, down_part.at[tokens[h]]
        )
        for h in (0, 1)
    ]
    step(wide_du, *downs)
    net.settle(loads[0], loads[3])
    for first, columns in ((0, 256), (256, 64)):
        ga[:, pl.ds(first, columns)] = dot(grad_mid[...], w_o[:, pl.ds(first, columns)])
    grads_t = ga[...].T
    zeros = jnp.zeros((48, TOK), F32)
    for head in range(4):
        one = jnp.concatenate([grads_t[head * HEAD : (head + 1) * HEAD], zeros], axis=0).astype(BF)
        for tile in range(4):
            upstream[tile, :, pl.ds(head * TILE, TILE)] = one[:, tile * TILE : (tile + 1) * TILE]
    keys_t[...] = kv[:, :128].T
    net.settle(loads[4], *held_loads)
    step(wide_du, *downs)
    fill = jnp.zeros((256, 64), F32)

    def grad_out_rows(rows):
        w_o[rows, :] = jnp.concatenate(
            [t_dot(grad_mid[:, rows], attended[...]), fill], axis=1
        ).astype(BF)

    every(256, grad_out_rows)
    wide_out = wide_sum(net, w_o, *sum_out, [(grad_out, 0, 320)])
    step(wide_out)
    grad_kv[...] = jnp.zeros(grad_kv.shape, F32)
    factor = 1.0 / math.sqrt(HEAD)

    def one_tile(i):
        first = pl.multiple_of(i * TILE, TILE)
        seen = pl.ds(first, REACH)
        s = scores(kv[seen, :128], queries[i], low[i], first)
        weights = jnp.exp(s - lse[i])
        grad_weights = dot(kv[seen, 128:], upstream[i])
        inner = jnp.sum(weights * grad_weights, axis=0, keepdims=True)
        grad_scores = (weights * (grad_weights - inner)).astype(BF)
        grad_kv[seen, 128:] += dot_t(weights.astype(BF), upstream[i])
        grad_kv[seen, :128] += dot_t(grad_scores, queries[i]) * factor
        back = dot(keys_t[:, seen], grad_scores) * factor
        for head in range(4):
            grad_q[pl.ds(head * HEAD, HEAD), pl.ds(first, TILE)] = back[
                :HEAD, head * TILE : (head + 1) * TILE
            ]

    pl.loop(0, 2)(one_tile)
    step(*downs, wide_du)
    pl.loop(2, 4)(one_tile)
    later_kv[...] = grad_kv[pl.ds(0, 2 * TOK), :].astype(BF)
    arriving = [
        net.send(
            later_kv.at[pl.ds((2 - k) * TOK, TOK)],
            turned_back.at[2 - k],
            ((at.w + 16 - k) % 16, at.n),
        )
        for k in (1, 2)
    ]
    cos, sin = tables[0], tables[1]

    def unturned(part):
        a, b = part[:40], part[40:80]
        return [a * cos + b * sin, b * cos - a * sin]

    rotated = []
    for head in range(4):
        rotated += unturned(grad_q[pl.ds(head * HEAD, HEAD), :])
    step(wide_du, wide_out)
    finish(*downs)
    by_feature(rows_one, (mid[...] + total_one[...]).astype(BF))
    output_rows = narrow_swap(net, rows_one, back_one)
    step(output_rows)
    for copy in arriving:
        copy.wait_recv()
    whole = (
        grad_kv[pl.ds(2 * TOK, TOK), :]
        + turned_back[0].astype(F32)
        + turned_back[1].astype(F32)
    )
    rotated += unturned(whole[:, :128].T)
    rotated += [whole[:, 128:].T[:HEAD], jnp.zeros((32, TOK), F32)]
    grads_ref[...] = jnp.concatenate(rotated, axis=0).T.astype(BF)
    net.settle(loads[2])

    def back_normed(h):
        def part(rows):
            down_part[tokens[h], rows] = dot_t(grads_ref[tokens[h], :], w_qkv[rows, :]).astype(BF)

        every(256, part)
        return narrow_sum(net, down_part.at[tokens[h]], slots_two.at[h], total_two.at[own[h]], 16)

    sums = [back_normed(0)]
    step(sums[0])
    sums.append(back_normed(1))
    step(sums[1])
    net.settle(loads[1])

    def grad_qkv_rows(rows):
        w_qkv[rows, :] = t_dot(normed[:, rows], grads_ref[...]).astype(BF)

    step(sums[0])
    every(256, grad_qkv_rows)
    wide_qkv = wide_sum(
        net, w_qkv, *sum_qkv, [(grad_query, 0, 320), (grad_key, 320, 80), (grad_value, 400, 80)]
    )
    step(wide_qkv, sums[1], sums[0], wide_out, wide_qkv, sums[1], wide_du)
    finish(sums[0])
    finish(sums[1])
    stream, grad = x_rows[...], total_two[...]
    inv = lax.rsqrt(jnp.mean(stream * stream, axis=1, keepdims=True) + epsilon)
    weighted = grad * gains[0:1, :]
    inner = jnp.sum(weighted * stream, axis=1, keepdims=True)
    through = inv * weighted - stream * (inv * inv * inv * inner / D)
    by_feature(rows_two, (grad_mid_own[...] + through).astype(BF))
    back = narrow_swap(net, rows_two, back_two)
    step(back)
    gain_one = jnp.sum(grad * stream * inv, axis=0, keepdims=True)
    both = jnp.concatenate([gain_one, gain_two_part[0:1, :], jnp.zeros((6, D), F32)], axis=0)
    for j in range(8):
        parts[j, :, :320] = both[:, j * 320 : (j + 1) * 320]
        parts[j, :, 320:] = jnp.zeros((8, 64), F32)
    me = at.n
    copies = [net.send(parts.at[p[1]], narrow_parts.at[me], p) for p in at.narrow_peers()]
    narrow_parts[me] = parts[me]
    step(wide_out, wide_qkv, wide_du)
    for copy in copies:
        copy.wait_recv()
    sum_parts = narrow_parts[0]
    for k in range(1, 8):
        sum_parts += narrow_parts[k]
    wide_parts[0] = sum_parts
    copies = [
        net.send(wide_parts.at[0], wide_parts.at[k + 1], p) for k, p in enumerate(everyone)
    ]
    step(wide_out, wide_qkv, wide_du)
    finish(wide_out, wide_qkv, wide_du)
    for copy in copies:
        copy.wait_recv()
    finish(back, output_rows)
    net.run([])


def closing(*refs):
    ins, outs = refs[:10], refs[10:]
    for rows, out in ((ins[0], outs[0]), (ins[1], outs[1])):
        halves = [rows[:, pl.ds(h * 32, 32), :].reshape(256, 320) for h in (0, 1)]
        out[...] = jnp.concatenate(halves, axis=0).astype(F32).T.astype(out.dtype)
    total = ins[2][0]
    for k in range(1, 16):
        total += ins[2][k]
    outs[2][...] = total[0:1, :320].reshape(320)
    outs[3][...] = total[1:2, :320].reshape(320)
    for source, out in zip(ins[3:], outs[4:]):
        out[...] = source[...]


def wide_sum_scratch(columns):
    return [
        pltpu.VMEM((4, 2, ROWS, columns), BF),
        pltpu.VMEM((3, 2, ROWS, columns), BF),
        pltpu.VMEM((ROWS, columns), BF),
    ]


def vmem():
    return pl.BlockSpec(memory_space=pltpu.VMEM)


def hbm():
    return pl.BlockSpec(memory_space=pl.ANY)


def exchange(name, number, body, ins, outs, scratch=(), sends=200, keeps=24):
    def kernel(*refs):
        a, b = len(ins), len(ins) + len(outs)
        net = Net(Place(), *refs[-3:])
        body(net, refs[:a], refs[a:b], refs[b:-3])

    return pl.pallas_call(
        kernel,
        out_shape=[jax.ShapeDtypeStruct(shape, dtype) for shape, dtype, _ in outs],
        in_specs=[spec for _, spec in ins],
        out_specs=[spec for _, _, spec in outs],
        scratch_shapes=[
            *scratch,
            pltpu.SemaphoreType.DMA((sends,)),
            pltpu.SemaphoreType.DMA((sends,)),
            pltpu.SemaphoreType.DMA((keeps,)),
        ],
        compiler_params=pltpu.CompilerParams(
            collective_id=number, has_side_effects=True, vmem_limit_bytes=60 * 2**20
        ),
        name=name,
    )(*[array for array, _ in ins])


def scaled_freqs():
    freqs = (rope_base ** (-2.0 * np.arange(HEAD // 2) / HEAD)).astype(np.float32)
    wavelen = (2.0 * math.pi / freqs).astype(np.float32)
    smooth = (long_wave / wavelen - 1.0) / 3.0
    blended = (1.0 - smooth) * freqs / rope_factor + smooth * freqs
    return np.where(
        wavelen < short_wave, freqs, np.where(wavelen > long_wave, freqs / rope_factor, blended)
    ).astype(np.float32)


def body(
    layer_input,
    gain_attn,
    w_query,
    w_key,
    w_value,
    w_out,
    gain_mlp,
    w_gate,
    w_up,
    w_down,
    doc_lengths,
    cotangent,
):
    def held(*shape, dtype=BF):
        return (shape, dtype, vmem())

    def far(*shape, dtype=BF):
        return (shape, dtype, hbm())

    def room(*shape, dtype=BF):
        return pltpu.VMEM(shape, dtype)

    def local(*arrays):
        return [(a, vmem()) for a in arrays]

    def remote(*arrays):
        return [(a, hbm()) for a in arrays]

    freqs = jnp.asarray(np.repeat(scaled_freqs()[:, None], 128, axis=1))
    slots = room(2, 7, OWN // 2, D)
    own = room(OWN, D, dtype=F32)
    normed, w_qkv, w_o, cot, w_gu, queries, kv, lse, low, tables, attended, x_rows, mid, normed_mid, inverse, gains = exchange(
        "attention",
        1,
        attention,
        remote(layer_input.T, cotangent.T)
        + local(w_query, w_key, w_value, w_out.T, w_gate, w_up, gain_attn, gain_mlp, freqs)
        + [(doc_lengths, pl.BlockSpec(memory_space=pltpu.SMEM))],
        [
            far(TOK, D),
            far(D, 512),
            far(D, 384),
            far(D, TOK),
            far(D, 2 * PANEL),
            held(4, TILE, 4 * TILE),
            held(3 * TOK, 256),
            held(4, 1, 4 * TILE, dtype=F32),
            held(4, 1, 4 * TILE, dtype=jnp.int32),
            held(2, 40, TOK, dtype=F32),
            held(TOK, 320),
            held(OWN, D, dtype=F32),
            held(OWN, D, dtype=F32),
            held(OWN, D),
            held(OWN, 128, dtype=F32),
            held(8, D, dtype=F32),
        ],
        [
            room(ROWS, 512),
            room(ROWS, 384),
            room(ROWS, 2 * PANEL),
            room(8, 384, dtype=F32),
            room(8, 8, 384, dtype=F32),
            room(D, 512),
            room(D, 384),
            room(D, TOK),
            room(TOK, D),
            room(TOK, D),
            room(512, TOK, dtype=F32),
            room(TOK, D),
            slots,
            own,
            room(TILE, 3 * TOK),
        ],
    )
    grad_mid, grad_mid_own, down_part, grad_gate, grad_du, gain_two_part = exchange(
        "mlp",
        2,
        mlp,
        local(normed_mid, w_down.T) + remote(w_gu, cot) + local(mid, inverse, gains),
        [
            far(TOK, D),
            held(OWN, D, dtype=F32),
            far(TOK, D),
            held(ROWS, PANEL, dtype=F32),
            far(D, 2 * PANEL),
            held(8, D, dtype=F32),
        ],
        [
            room(ROWS, PANEL),
            room(D, 2 * PANEL),
            room(D, PANEL),
            room(TOK, D),
            room(D, TOK),
            room(TOK, D),
            room(TOK, 2 * PANEL, dtype=F32),
            room(TOK, PANEL, dtype=F32),
            room(TOK, PANEL),
            room(TOK, 2 * PANEL),
            room(TOK, D),
            room(TOK, D),
            slots,
            own,
            *wide_sum_scratch(PANEL),
            room(OWN, D),
            room(TOK, D),
        ],
    )
    output_rows, grad_rows, gain_parts, grad_out, grad_query, grad_key, grad_value, grad_d, grad_up = exchange(
        "attention_back",
        3,
        attention_back,
        remote(grad_mid, normed, w_qkv, w_o, down_part, grad_du)
        + local(grad_mid_own, attended, queries, kv, lse, low, tables, mid, x_rows, gains, gain_two_part),
        [
            held(8, OWN, 320),
            held(8, OWN, 320),
            held(16, 8, 384, dtype=F32),
            held(ROWS, 320, dtype=F32),
            held(ROWS, 320, dtype=F32),
            held(ROWS, 80, dtype=F32),
            held(ROWS, 80, dtype=F32),
            held(ROWS, PANEL, dtype=F32),
            held(ROWS, PANEL, dtype=F32),
        ],
        [
            room(TOK, D),
            room(TOK, D),
            room(D, 512),
            room(D, 384),
            room(TOK, D),
            room(4, 2, ROWS, 2 * PANEL),
            room(4, TILE, 4 * TILE),
            room(TILE, 3 * TOK),
            room(3 * TOK, 256, dtype=F32),
            room(320, TOK, dtype=F32),
            slots,
            slots,
            own,
            own,
            room(2 * TOK, 256),
            room(2, TOK, 256),
            room(TOK, 320, dtype=F32),
            room(8, OWN, 320),
            room(8, OWN, 320),
            room(8, 8, 384, dtype=F32),
            room(8, 8, 384, dtype=F32),
            room(TOK, 512),
            *wide_sum_scratch(2 * PANEL),
            *wide_sum_scratch(384),
            *wide_sum_scratch(512),
        ],
    )
    results = [
        ((320, TOK), BF),
        ((320, TOK), F32),
        ((320,), F32),
        ((320,), F32),
        ((ROWS, 320), F32),
        ((ROWS, 80), F32),
        ((ROWS, 80), F32),
        ((ROWS, 320), F32),
        ((ROWS, PANEL), F32),
        ((ROWS, PANEL), F32),
        ((ROWS, PANEL), F32),
    ]
    out = pl.pallas_call(
        closing,
        out_shape=[jax.ShapeDtypeStruct(shape, dtype) for shape, dtype in results],
        in_specs=[vmem()] * 10,
        out_specs=[vmem()] * 11,
        name="closing",
    )(output_rows, grad_rows, gain_parts, grad_query, grad_key, grad_value, grad_out, grad_gate, grad_up, grad_d)
    return (
        out[0].T,
        out[1].T,
        out[2],
        out[4],
        out[5],
        out[6],
        out[7].T,
        out[3],
        out[8],
        out[9],
        out[10].T,
    )


def solution(mesh):
    rows, columns = P("wide", "narrow"), P("narrow", "wide")
    return jax.shard_map(
        body,
        mesh=mesh,
        in_specs=(
            rows,
            P("narrow"),
            rows,
            rows,
            rows,
            columns,
            P("narrow"),
            rows,
            rows,
            columns,
            P(),
            rows,
        ),
        out_specs=(
            rows,
            rows,
            P("narrow"),
            rows,
            rows,
            rows,
            columns,
            P("narrow"),
            rows,
            rows,
            columns,
        ),
        check_vma=False,
    )
```

```python
import functools
import math

import jax
import jax.numpy as jnp
import numpy as np
from jax import lax
from jax.experimental import pallas as pl
from jax.experimental.pallas import tpu as pltpu
from jax.sharding import PartitionSpec as P

D = 2560
HEADS = 32
KV_HEADS = 8
HEAD = 80
WINDOW = 1024
TOK = 512
OWN = 64
ROWS = 160
PANEL = 896
TILE = 128
REACH = WINDOW + TILE
CUT = 1024

epsilon = 1e-05
rope_base = 1000000.0
rope_factor = 8.0
long_wave = 8192.0
short_wave = 2048.0
masked = -1e30

MESH = pl.DeviceIdType.MESH
BF = jnp.bfloat16
F32 = jnp.float32


class Place:
    def __init__(self):
        self.w = lax.axis_index("wide")
        self.n = lax.axis_index("narrow")
        self.z, self.h, self.c = self.w // 4, (self.w // 2) % 2, self.w % 2
        self.x, self.l = self.n // 2, self.n % 2

    def wide(self, dz, dh, dc):
        return ((self.z + dz) % 4) * 4 + ((self.h + dh) % 2) * 2 + (self.c + dc) % 2

    def narrow(self, dx, dl):
        return ((self.x + dx) % 4) * 2 + (self.l + dl) % 2

    def narrow_peers(self):
        return [(self.w, self.narrow(k // 2, k % 2)) for k in (2, 6, 1, 3, 7, 4, 5)]

    def wide_peers(self):
        return [(self.wide(*d), self.n) for d in ((0, 1, 0), (1, 0, 0), (3, 0, 0), (2, 0, 0), (0, 0, 1))]


class Net:
    def __init__(self, place, send_sems, recv_sems, local_sems):
        self.at = place
        self.sems = (send_sems, recv_sems, local_sems)
        self.sent, self.kept, self.open, self.done = [], [], [], 0

    def barrier(self, givers, takers):
        bar = pltpu.get_barrier_semaphore()
        for device in givers:
            pl.semaphore_signal(bar, inc=1, device_id=device, device_id_type=MESH)
        self.settle(*self.loads)
        pl.semaphore_wait(bar, takers)

    def send(self, src, dst, device):
        i = len(self.sent)
        copy = pltpu.make_async_remote_copy(
            src_ref=src,
            dst_ref=dst,
            send_sem=self.sems[0].at[i],
            recv_sem=self.sems[1].at[i],
            device_id=device,
            device_id_type=MESH,
        )
        copy.start()
        self.sent.append(copy)
        return copy

    def keep(self, src, dst):
        copy = pltpu.make_async_copy(src, dst, self.sems[2].at[len(self.kept)])
        copy.start()
        self.kept.append(copy)
        self.open.append(copy)
        return copy

    def settle(self, *copies):
        for copy in copies:
            copy.wait()
            self.open = [c for c in self.open if c is not copy]

    def release(self, count):
        for copy in self.sent[self.done : count]:
            copy.wait_send()
        self.done = count

    def run(self, tasks):
        tasks = list(tasks)
        while tasks:
            left = []
            for task in tasks:
                try:
                    next(task)
                    left.append(task)
                except StopIteration:
                    pass
            tasks = left
        for copy in self.sent[self.done :]:
            copy.wait_send()
        self.settle(*self.open)


def block_of(ref, index, rows):
    return ref.at[pl.ds(pl.multiple_of(index * rows, 16), rows)]


def narrow_gather(net, src, dst, cut):
    at = net.at
    me, near = at.n, at.narrow(0, 1)
    right, left, beside = (at.w, at.narrow(1, 0)), (at.w, at.narrow(3, 0)), (at.w, near)
    rows, columns = src.shape
    upper, lower = pl.ds(0, rows // 2), pl.ds(rows // 2, rows // 2)
    early, late = pl.ds(0, cut), pl.ds(cut, columns - cut)

    def block(n):
        return block_of(dst, n, rows)

    def on(part, device):
        return net.send(part, part, device)

    kept = net.keep(src, block(me))
    first = net.send(src.at[:, late], block(me).at[:, late], beside)
    to_right, to_left = net.send(src, block(me), right), net.send(src, block(me), left)
    over = [net.send(src.at[:, early], block(me).at[:, early], beside)]
    yield
    first.wait_recv()
    part = block(near).at[:, late]
    near_right, near_left = on(part, right), on(part, left)
    yield
    to_right.wait_recv()
    part = block(at.narrow(3, 0))
    from_left = on(part.at[upper], right)
    over.append(on(part.at[:, early], beside))
    to_left.wait_recv()
    part = block(at.narrow(1, 0))
    from_right = on(part.at[lower], left)
    over.append(on(part.at[:, early], beside))
    yield
    near_right.wait_recv()
    over.append(on(block(at.narrow(3, 1)).at[upper, late], right))
    near_left.wait_recv()
    over.append(on(block(at.narrow(1, 1)).at[lower, late], left))
    yield
    from_left.wait_recv()
    from_right.wait_recv()
    over.append(on(block(at.narrow(2, 0)).at[:, early], beside))
    yield
    for copy in over:
        copy.wait_recv()
    net.settle(kept)


def narrow_share(net, src, dst):
    me = net.at.n
    copies = [net.send(src, dst.at[me], peer) for peer in net.at.narrow_peers()]
    kept = net.keep(src, dst.at[me])
    yield
    yield
    for copy in copies:
        copy.wait_recv()
    net.settle(kept)


def narrow_swap(net, src, dst):
    me = net.at.n
    copies = [net.send(src.at[peer[1]], dst.at[me], peer) for peer in net.at.narrow_peers()]
    kept = net.keep(src.at[me], dst.at[me])
    yield
    for copy in copies:
        copy.wait_recv()
    net.settle(kept)


def add_rows(rows, step, dst, terms):
    @pl.loop(0, rows // step)
    def _(i):
        part = pl.ds(pl.multiple_of(i * step, step), step)
        total = terms[0][part, :].astype(F32)
        for term in terms[1:]:
            total += term[part, :].astype(F32)
        dst[part, :] = total.astype(dst.dtype)


def narrow_sum(net, src, slots, out, cut, held=None):
    at = net.at
    me, near = at.n, at.narrow(0, 1)
    right, left, beside = (at.w, at.narrow(1, 0)), (at.w, at.narrow(3, 0)), (at.w, near)
    rows, columns = out.shape
    upper, lower = pl.ds(0, rows // 2), pl.ds(rows // 2, rows // 2)
    early, late = pl.ds(0, cut), pl.ds(cut, columns - cut)

    def block(n):
        return block_of(src, n, rows)

    def term(n, *part):
        return block_of(src if held is None else held, n, rows)[part].astype(F32)

    def put(slot, value, *part):
        slots[slot, *part] = value.astype(BF)

    def at_slot(slot, *part):
        return slots[slot, *part].astype(F32)

    everything = slice(None)
    over = {
        d: net.send(block(at.narrow(d, 1)).at[:, early], slots.at[k, :, early], beside)
        for d, k in ((2, 2), (1, 0), (3, 1))
    }
    far = block(at.narrow(2, 1))
    pass_right = net.send(far.at[upper, late], slots.at[3, upper, late], right)
    pass_left = net.send(far.at[lower, late], slots.at[3, lower, late], left)
    final = [net.send(block(near).at[:, early], slots.at[7, :, early], beside)]
    yield
    over[2].wait_recv()
    n = at.narrow(2, 0)
    put(2, at_slot(2, everything, early) + term(n, everything, early), everything, early)
    put(2, term(n, everything, late), everything, late)
    far_right = net.send(slots.at[2, upper], slots.at[4, upper], right)
    far_left = net.send(slots.at[2, lower], slots.at[4, lower], left)
    yield
    pass_right.wait_recv()
    n = at.narrow(1, 1)
    put(10, term(n, upper, late) + at_slot(3, upper, late), upper, late)
    put(10, term(n, lower, late), lower, late)
    near_right = net.send(slots.at[10, :, late], slots.at[8, :, late], right)
    pass_left.wait_recv()
    n = at.narrow(3, 1)
    put(11, term(n, lower, late) + at_slot(3, lower, late), lower, late)
    put(11, term(n, upper, late), upper, late)
    near_left = net.send(slots.at[11, :, late], slots.at[9, :, late], left)
    yield
    for d, slot, copy, half, whole in (
        (1, 0, far_right, upper, lower),
        (3, 1, far_left, lower, upper),
    ):
        over[d].wait_recv()
        copy.wait_recv()
        n = at.narrow(d, 0)
        put(slot, at_slot(slot, half, early) + term(n, half, early) + at_slot(4, half, early), half, early)
        put(slot, at_slot(slot, whole, early) + term(n, whole, early), whole, early)
        put(slot, term(n, half, late) + at_slot(4, half, late), half, late)
        put(slot, term(n, whole, late), whole, late)
        final.append(
            net.send(slots.at[slot], slots.at[5 + slot], right if d == 1 else left)
        )
    yield
    near_right.wait_recv()
    near_left.wait_recv()
    value = term(near, everything, late) + at_slot(8, everything, late) + at_slot(9, everything, late)
    put(8, value, everything, late)
    final.append(net.send(slots.at[8, :, late], slots.at[7, :, late], beside))
    yield
    for copy in final:
        copy.wait_recv()
    out[...] = term(me, everything, everything) + at_slot(5) + at_slot(6) + at_slot(7)


def wide_gather(net, src, dst):
    at = net.at
    half = ROWS // 2
    me, far = at.w, at.wide(0, 1, 0)
    up, down = (at.wide(1, 0, 0), at.n), (at.wide(3, 0, 0), at.n)
    other = (at.wide(0, 0, 1), at.n)

    def block(w):
        return block_of(dst, w, ROWS)

    kept = net.keep(src, block(me))
    turns = [[net.send(src, block(me), up), net.send(src, block(me), down)]]
    over = [net.send(src, block(me), other)]
    further = []

    def relay(e):
        for d, part, ahead, copy in (
            (3, slice(0, half), up, turns[e][0]),
            (1, slice(half, ROWS), down, turns[e][1]),
        ):
            copy.wait_recv()
            shard = block(at.wide(d, e, 0))
            further.append((e, part, net.send(shard.at[part], shard.at[part], ahead)))
            over.append(net.send(shard, shard, other))

    yield
    from_far = net.send(src, block(me), (far, at.n))
    yield
    relay(0)
    yield
    from_far.wait_recv()
    turns.append([net.send(block(far), block(far), up), net.send(block(far), block(far), down)])
    over.append(net.send(block(far), block(far), other))
    yield
    relay(1)
    yield
    for e, part, copy in further:
        copy.wait_recv()
        shard = block(at.wide(2, e, 0)).at[part]
        over.append(net.send(shard, shard, other))
    yield
    for copy in over:
        copy.wait_recv()
    net.settle(kept)


def wide_sum(net, src, core, turned, last, outs, held=None):
    at = net.at
    half = ROWS // 2
    up, down = (at.wide(1, 0, 0), at.n), (at.wide(3, 0, 0), at.n)
    other = (at.wide(0, 0, 1), at.n)
    order = [(d, e) for d in (2, 1, 3, 0) for e in (1, 0)]

    def block(w):
        return block_of(src, w, ROWS)

    over = {(d, e): net.send(block(at.wide(d, e, 1)), core.at[d, e], other) for d, e in order}
    yield
    further = []
    for d, e in order:
        over[d, e].wait_recv()
        part = core.at[d, e]
        add_rows(ROWS, 32, part, [part, block(at.wide(d, e, 0)) if held is None else held.at[d, e]])
        if d == 2:
            further.append(
                (
                    e,
                    net.send(part.at[:half], turned.at[2, e, :half], up),
                    net.send(part.at[half:], turned.at[2, e, half:], down),
                )
            )
    yield
    turns = []
    for e, first, second in further:
        first.wait_recv()
        part = core.at[1, e]
        add_rows(half, 16, part.at[:half], [part.at[:half], turned.at[2, e, :half]])
        turns.append((e, net.send(part, turned.at[0, e], up)))
        second.wait_recv()
        part = core.at[3, e]
        add_rows(half, 16, part.at[half:], [part.at[half:], turned.at[2, e, half:]])
        turns.append((e, net.send(part, turned.at[1, e], down)))
        yield
    for e, copy in turns:
        if e:
            copy.wait_recv()
    part = core.at[0, 1]
    add_rows(ROWS, 32, part, [part, turned.at[0, 1], turned.at[1, 1]])
    final = net.send(part, last, (at.wide(0, 1, 0), at.n))
    yield
    for e, copy in turns:
        if not e:
            copy.wait_recv()
    final.wait_recv()

    @pl.loop(0, ROWS // 32)
    def _(i):
        part = pl.ds(pl.multiple_of(i * 32, 32), 32)
        total = core[0, 0, part, :].astype(F32) + last[part, :].astype(F32)
        for d in range(2):
            total += turned[d, 0, part, :].astype(F32)
        for out, first, columns in outs:
            out[part, :] = total[:, first : first + columns]


def step(*tasks):
    for task in tasks:
        next(task, None)


def finish(*tasks):
    tasks = list(tasks)
    while tasks:
        tasks = [task for task in tasks if next(task, "end") != "end"]


def pieces_of(width, size, body):
    whole = width // size

    @pl.loop(0, whole)
    def _(i):
        body(pl.ds(pl.multiple_of(i * size, size), size))

    if width % size:
        body(pl.ds(whole * size, width % size))


def dot(a, b):
    return jnp.dot(a, b, preferred_element_type=F32)


def dot_t(a, b):
    return lax.dot_general(a, b, (((1,), (1,)), ((), ())), preferred_element_type=F32)


def t_dot(a, b):
    return lax.dot_general(a, b, (((0,), (0,)), ((), ())), preferred_element_type=F32)


def scores(keys, queries, low, first):
    raw = dot(keys, queries) * (1.0 / math.sqrt(HEAD))
    key = first + lax.broadcasted_iota(jnp.int32, raw.shape, 0)
    query = first + WINDOW + lax.broadcasted_iota(jnp.int32, raw.shape, 1) % TILE
    return jnp.where((key >= low) & (key <= query), raw, masked)


def gain_terms(dst, grad, normed, gains, k):
    def part(columns):
        total = jnp.sum(
            grad[:, columns].astype(F32) * normed[:, columns].astype(F32), axis=0, keepdims=True
        )
        dst[:, columns] = jnp.broadcast_to(total / gains[k : k + 1, columns], (8, 256))

    every(256, part)


def by_feature(dst, rows):
    for j in range(8):
        dst[j] = rows[:, j * 320 : (j + 1) * 320]


def every(size, body, begin=0, end=D):
    @pl.loop(begin // size, end // size)
    def _(i):
        body(pl.ds(pl.multiple_of(i * size, size), size))


def attention(net, ins, outs, scratch):
    x_own, cot_own, w_query, w_key, w_value, w_out, w_gate, w_up, w_down = ins[:9]
    gain_one, gain_two, freqs, lengths = ins[9:]
    normed_far, w_qkv_far, w_out_far, cot, w_gu, w_d, normed_two = outs[:7]
    queries, kv, lse, low, tables, attended, x_rows, mid, inverse, gains = outs[7:]
    (
        shard_qkv,
        shard_out,
        shard_gu,
        gains_own,
        gain_pieces,
        w_qkv,
        w_o,
        x_t,
        x,
        normed,
        qkv,
        src,
        slots,
        total,
        values_t,
        normed_mid,
    ) = scratch
    at = net.at
    later = [((at.w + k) % 16, at.n) for k in (1, 2)]
    earlier = [((at.w + 16 - k) % 16, at.n) for k in (1, 2)]
    net.barrier(at.narrow_peers() + at.wide_peers() + earlier, 14)
    shard_qkv[:, :320] = w_query[...]
    shard_qkv[:, 320:] = jnp.concatenate(
        [w_key[...], w_value[...], jnp.zeros((ROWS, 32), BF)], axis=1
    )
    gains_own[...] = jnp.zeros(gains_own.shape, F32)
    gains_own[0:1, :320] = gain_one[...].reshape(1, 320)
    gains_own[1:2, :320] = gain_two[...].reshape(1, 320)
    panel = wide_gather(net, shard_qkv, w_qkv)
    step(panel, panel)
    stream = narrow_gather(net, x_own, x_t, 256)
    sizes = narrow_share(net, gains_own, gain_pieces)
    step(stream, sizes)
    shard_out[...] = jnp.concatenate([w_out[...], jnp.zeros((ROWS, 64), BF)], axis=1)
    shard_gu[:, :PANEL] = w_gate[...]
    shard_gu[:, PANEL:] = w_up[...]

    place = at.w * TOK + lax.broadcasted_iota(jnp.int32, (1, TOK), 1)
    begins, end = jnp.zeros((1, TOK), jnp.int32), 0
    for k in range(8):
        end = end + lengths[k]
        begins = jnp.where(place >= end, end, begins)
    position = place - begins
    angles = freqs[:, 0:1] * position.astype(F32)
    cos, sin = jnp.cos(angles), jnp.sin(angles)
    tables[0], tables[1] = cos, sin
    first_key = jnp.maximum(begins, jnp.maximum(place - (WINDOW - 1), 0)) - (at.w - 2) * TOK
    for tile in range(4):
        one = first_key[:, tile * TILE : (tile + 1) * TILE]
        low[tile] = jnp.concatenate([one] * 4, axis=1)

    step(panel, stream, panel, stream, panel)
    w_outs = wide_gather(net, shard_out, w_o)
    gate_up = wide_gather(net, shard_gu, w_gu)
    step(w_outs, w_outs, gate_up, panel, stream, stream, gate_up, w_outs, w_outs)
    finish(panel, sizes)
    step(w_outs)
    finish(stream)
    for j in range(8):
        gains[:, pl.ds(j * 320, 320)] = gain_pieces[j, :, :320]
    every(256, lambda rows: turned_over(x, x_t, rows))

    @pl.loop(0, TOK // 16)
    def _(i):
        rows = pl.ds(pl.multiple_of(i * 16, 16), 16)
        part = x[rows, :].astype(F32)
        inv = lax.rsqrt(jnp.mean(part * part, axis=1, keepdims=True) + epsilon)
        normed[rows, :] = (part * inv * gains[0:1, :]).astype(BF)

    for h in range(2):
        x_rows[pl.ds(h * 32, 32), :] = x[own_rows(at, h), :].astype(F32)
    for k in range(2):
        part = pl.ds(k * 256, 256)
        qkv[part, :] = dot(normed[...], w_qkv[:, part]).T
    zeros = jnp.zeros((48, TOK), F32)

    def turned(at_row):
        a, b = qkv[pl.ds(at_row, 40), :], qkv[pl.ds(at_row + 40, 40), :]
        return jnp.concatenate([a * cos - b * sin, b * cos + a * sin, zeros], axis=0)

    mine = pl.ds(2 * TOK, TOK)
    kv[mine, :128] = turned(320).T.astype(BF)
    kv[mine, 128:] = jnp.concatenate([qkv[pl.ds(400, 80), :], zeros], axis=0).T.astype(BF)
    arriving = [
        net.send(kv.at[mine], kv.at[pl.ds((2 - k) * TOK, TOK)], later[k - 1]) for k in (1, 2)
    ]
    cots = narrow_gather(net, cot_own, cot, 256)
    down = wide_gather(net, w_down, w_d)
    step(cots, down)
    for head in range(4):
        one = turned(head * HEAD).astype(BF)
        for tile in range(4):
            queries[tile, :, pl.ds(head * TILE, TILE)] = one[:, tile * TILE : (tile + 1) * TILE]
    step(w_outs, gate_up)
    for copy in arriving:
        copy.wait_recv()
    values_t[...] = kv[:, 128:].T

    def one_tile(i):
        first = pl.multiple_of(i * TILE, TILE)
        seen = pl.ds(first, REACH)
        s = scores(kv[seen, :128], queries[i], low[i], first)
        largest = jnp.max(s, axis=0, keepdims=True)
        powers = jnp.exp(s - largest)
        totals = jnp.sum(powers, axis=0, keepdims=True)
        weights = (powers / totals).astype(BF)
        lse[i] = largest + jnp.log(totals)
        mixed = dot(values_t[:, seen], weights)
        attended[pl.ds(first, TILE), :] = (
            jnp.concatenate([mixed[:HEAD, h * TILE : (h + 1) * TILE] for h in range(4)], axis=0)
            .T.astype(BF)
        )

    def out_part(h):
        tokens = pl.ds(h * 256, 256)

        def columns(rows):
            src[tokens, rows] = dot_t(attended[tokens, :], w_o[rows, :320]).astype(BF)

        every(512, columns)
        return narrow_sum(net, src.at[tokens], slots.at[h], total.at[pl.ds(h * 32, 32)], CUT)

    def norm_part(h):
        rows = pl.ds(h * 32, 32)
        stream = x_rows[rows, :] + total[rows, :]
        mid[rows, :] = stream
        inv = lax.rsqrt(jnp.mean(stream * stream, axis=1, keepdims=True) + epsilon)
        inverse[rows, :] = jnp.broadcast_to(inv, (32, 128))
        normed_mid[rows, :] = (stream * inv * gains[1:2, :]).astype(BF)
        return narrow_gather(
            net, normed_mid.at[rows], normed_two.at[pl.ds(h * 256, 256)], CUT
        )

    pl.loop(0, 2)(one_tile)
    finish(w_outs)
    early = out_part(0)
    step(early, gate_up, cots)
    pl.loop(2, 4)(one_tile)
    step(early, early)
    late = out_part(1)
    step(early, late, early, down, cots, late)
    net.keep(w_o, w_out_far)
    net.keep(normed, normed_far)
    step(late)
    net.keep(w_qkv, w_qkv_far)
    finish(early)
    ahead = norm_part(0)
    step(ahead, late, gate_up, ahead, late, down, ahead)
    step(cots, ahead, gate_up, ahead)
    finish(late)
    behind = norm_part(1)
    step(behind, down, cots, behind, down, behind)
    finish(ahead)
    step(behind, down, behind)
    finish(behind, gate_up, cots, down)
    net.run([])


def own_rows(at, h):
    return pl.ds(pl.multiple_of(h * 256 + at.n * 32, 32), 32)


def turned_over(dst, src, rows):
    dst[:, rows] = src[rows, :].T


def mlp(net, ins, outs, scratch):
    normed_far, d_far, gu_far, cot_far, mid, inverse, gains = ins
    grad_mid_far, grad_mid, down_far, grad_gate, du_far, gain_part = outs
    w_gu, w_d, normed, cot_t, cot, gu, grad_hidden, hidden, grad_pre, src = scratch[:10]
    down_part, slots, total, core, turned, last, low, grad_mid_full = scratch[10:]
    at = net.at
    sources, rooms = (normed_far, gu_far, cot_far, d_far), (normed, w_gu, cot_t, w_d)
    loads = [net.keep(a, b) for a, b in zip(sources, rooms)]
    net.barrier(at.narrow_peers() + at.wide_peers(), 12)
    tokens = [pl.ds(0, 256), pl.ds(256, 256)]
    own = [pl.ds(0, 32), pl.ds(32, 32)]
    def gate_up(h):
        def part(columns):
            gu[tokens[h], columns] = dot(normed[tokens[h], :], w_gu[:, columns])

        pieces_of(2 * PANEL, 256, part)

    def back_down(h):
        def part(columns):
            grad_hidden[tokens[h], columns] = dot(cot[tokens[h], :], w_d[:, columns])

        pieces_of(PANEL, 256, part)

    def back_hidden(h):
        @pl.loop(h * 16, h * 16 + 16)
        def _(i):
            rows = pl.ds(pl.multiple_of(i * 16, 16), 16)
            gate, up, grad = gu[rows, :PANEL], gu[rows, PANEL:], grad_hidden[rows, :]
            sigmoid = jax.nn.sigmoid(gate)
            active = gate * sigmoid
            hidden[rows, :] = (active * up).astype(BF)
            grad_pre[rows, :PANEL] = (
                grad * up * sigmoid * (1.0 + gate * (1.0 - sigmoid))
            ).astype(BF)
            grad_pre[rows, PANEL:] = (grad * active).astype(BF)

    def back_normed(h):
        def part(rows):
            src[tokens[h], rows] = dot_t(grad_pre[tokens[h], :], w_gu[rows, :]).astype(BF)

        every(256, part)
        return narrow_sum(net, src.at[tokens[h]], slots.at[h], total.at[own[h]], CUT)

    def back_norm(h):
        inv, scale = inverse[own[h], :1], gains[1:2, :]
        grad, stream = total[own[h], :], mid[own[h], :]
        weighted = grad * scale
        inner = jnp.sum(weighted * stream, axis=1, keepdims=True)
        through = inv * weighted - stream * (inv * inv * inv * inner / D)
        mine = cot[own_rows(at, h), :].astype(F32) + through
        grad_mid[own[h], :] = mine
        low[own[h], :] = mine.astype(BF)
        return narrow_gather(net, low.at[own[h]], grad_mid_full.at[tokens[h]], CUT)

    net.settle(*loads[:2])
    gate_up(0)
    net.settle(*loads[2:])
    every(256, lambda rows: turned_over(cot, cot_t, rows))
    back_down(0)
    back_hidden(0)
    sums = [back_normed(0)]
    step(sums[0])
    gate_up(1)
    step(sums[0])
    back_down(1)
    step(sums[0])
    back_hidden(1)
    step(sums[0])
    sums.append(back_normed(1))
    step(sums[0], sums[1])

    def grad_gate_rows(rows):
        w_gu[rows, :PANEL] = t_dot(normed[:, rows], grad_pre[:, :PANEL]).astype(BF)

    every(256, grad_gate_rows, 0, 1280)
    step(sums[1])
    finish(sums[0])
    back = [back_norm(0)]
    step(back[0], sums[1])
    every(256, grad_gate_rows, 1280, D)
    wide = wide_sum(net, w_gu.at[:, pl.ds(0, PANEL)], core, turned, last, [(grad_gate, 0, PANEL)])
    step(back[0], sums[1], wide, back[0])

    def grad_up_rows(rows):
        w_gu[rows, PANEL:] = t_dot(normed[:, rows], grad_pre[:, PANEL:]).astype(BF)

    every(256, grad_up_rows, 0, 1280)
    step(sums[1], back[0], wide)
    every(256, grad_up_rows, 1280, D)
    finish(sums[1])
    back.append(back_norm(1))
    step(back[1], back[0])
    net.keep(w_gu.at[:, pl.ds(PANEL, PANEL)], du_far.at[:, pl.ds(PANEL, PANEL)])

    def forward_down(rows):
        down_part[:, rows] = dot_t(hidden[...], w_d[rows, :]).astype(BF)

    every(256, forward_down, 0, 1280)
    step(back[1], wide)
    every(256, forward_down, 1280, D)
    net.keep(down_part, down_far)
    step(back[1], wide)

    def grad_d_rows(rows):
        w_d[rows, :] = dot(cot_t[rows, :], hidden[...]).astype(BF)

    every(256, grad_d_rows, 0, 1280)
    step(back[1], wide, back[1])
    every(256, grad_d_rows, 1280, D)
    net.keep(w_d, du_far.at[:, pl.ds(0, PANEL)])
    finish(back[0])
    step(wide)
    gain_terms(gain_part, src, normed, gains, 1)
    finish(back[1])
    net.keep(grad_mid_full, grad_mid_far)
    finish(wide)
    net.run([])


def attention_back(net, ins, outs, scratch):
    grad_mid_far, normed_far, w_qkv_far, w_out_far, down_far, du_far = ins[:6]
    grad_mid_own, attended, queries, kv, lse, low, tables, mid, x_rows, gains, gain_two_part = ins[6:]
    back_one, back_two, wide_parts, grad_out, grad_query, grad_key, grad_value, grad_d, grad_up = outs
    grad_mid, normed, w_qkv, w_o, down_part, held_du = scratch[:6]
    upstream, keys_t, grad_kv, grad_q, slots_one, slots_two, total_one, total_two = scratch[6:14]
    later_kv, turned_back, ga, rows_one, rows_two, parts, narrow_parts, grads_ref = scratch[14:22]
    sum_du, sum_out, sum_qkv, gain_one_part = scratch[22:25], scratch[25:28], scratch[28:31], scratch[31]
    at = net.at
    tokens = [pl.ds(0, 256), pl.ds(256, 256)]
    own = [pl.ds(0, 32), pl.ds(32, 32)]
    loads = [net.keep(a, b) for a, b in zip(ins[:5], (grad_mid, normed, w_qkv, w_o, down_part))]
    held_loads = [
        net.keep(block_of(du_far, at.wide(d, e, 0), ROWS), held_du.at[d, e])
        for d in range(4)
        for e in range(2)
    ]
    everyone = [((at.w + k) % 16, at.n) for k in range(1, 16)]
    net.barrier(at.narrow_peers() + everyone, 22)
    wide_du = wide_sum(
        net, du_far, *sum_du, [(grad_d, 0, PANEL), (grad_up, PANEL, PANEL)], held_du
    )
    downs = [
        narrow_sum(
            net, down_far.at[tokens[h]], slots_one.at[h], total_one.at[own[h]], CUT, down_part.at[tokens[h]]
        )
        for h in (0, 1)
    ]
    step(wide_du, *downs)
    net.settle(loads[0], loads[3])
    for first, columns in ((0, 256), (256, 64)):
        ga[:, pl.ds(first, columns)] = dot(grad_mid[...], w_o[:, pl.ds(first, columns)])
    grads_t = ga[...].T
    zeros = jnp.zeros((48, TOK), F32)
    for head in range(4):
        one = jnp.concatenate([grads_t[head * HEAD : (head + 1) * HEAD], zeros], axis=0).astype(BF)
        for tile in range(4):
            upstream[tile, :, pl.ds(head * TILE, TILE)] = one[:, tile * TILE : (tile + 1) * TILE]
    keys_t[...] = kv[:, :128].T
    net.settle(loads[4], *held_loads)
    step(downs[0], wide_du, downs[1], *downs)
    fill = jnp.zeros((512, 64), F32)

    def grad_out_rows(rows):
        w_o[rows, :] = jnp.concatenate(
            [t_dot(grad_mid[:, rows], attended[...]), fill], axis=1
        ).astype(BF)

    every(512, grad_out_rows)
    wide_out = wide_sum(net, w_o, *sum_out, [(grad_out, 0, 320)])
    step(wide_out)
    grad_kv[...] = jnp.zeros(grad_kv.shape, F32)
    factor = 1.0 / math.sqrt(HEAD)

    def one_tile(i):
        first = pl.multiple_of(i * TILE, TILE)
        seen = pl.ds(first, REACH)
        s = scores(kv[seen, :128], queries[i], low[i], first)
        weights = jnp.exp(s - lse[i])
        grad_weights = dot(kv[seen, 128:], upstream[i])
        inner = jnp.sum(weights * grad_weights, axis=0, keepdims=True)
        grad_scores = (weights * (grad_weights - inner)).astype(BF)
        grad_kv[seen, 128:] += dot_t(weights.astype(BF), upstream[i])
        grad_kv[seen, :128] += dot_t(grad_scores, queries[i]) * factor
        back = dot(keys_t[:, seen], grad_scores) * factor
        for head in range(4):
            grad_q[pl.ds(head * HEAD, HEAD), pl.ds(first, TILE)] = back[
                :HEAD, head * TILE : (head + 1) * TILE
            ]

    pl.loop(0, 2)(one_tile)
    step(*downs, wide_du, *downs, wide_out)
    pl.loop(2, 4)(one_tile)
    later_kv[...] = grad_kv[pl.ds(0, 2 * TOK), :].astype(BF)
    arriving = [
        net.send(
            later_kv.at[pl.ds((2 - k) * TOK, TOK)],
            turned_back.at[2 - k],
            ((at.w + 16 - k) % 16, at.n),
        )
        for k in (1, 2)
    ]
    cos, sin = tables[0], tables[1]

    def unturned(part):
        a, b = part[:40], part[40:80]
        return [a * cos + b * sin, b * cos - a * sin]

    rotated = []
    for head in range(4):
        rotated += unturned(grad_q[pl.ds(head * HEAD, HEAD), :])
    step(wide_du)
    finish(*downs)
    by_feature(rows_one, (mid[...] + total_one[...]).astype(BF))
    output_rows = narrow_swap(net, rows_one, back_one)
    step(output_rows)
    for copy in arriving:
        copy.wait_recv()
    whole = (
        grad_kv[pl.ds(2 * TOK, TOK), :]
        + turned_back[0].astype(F32)
        + turned_back[1].astype(F32)
    )
    rotated += unturned(whole[:, :128].T)
    rotated += [whole[:, 128:].T[:HEAD], jnp.zeros((32, TOK), F32)]
    grads_ref[...] = jnp.concatenate(rotated, axis=0).T.astype(BF)
    net.settle(loads[2])

    def back_normed(h):
        def part(rows):
            down_part[tokens[h], rows] = dot_t(grads_ref[tokens[h], :], w_qkv[rows, :]).astype(BF)

        every(256, part)
        return narrow_sum(net, down_part.at[tokens[h]], slots_two.at[h], total_two.at[own[h]], CUT)

    sums = [back_normed(0)]
    step(sums[0], wide_out)
    sums.append(back_normed(1))
    step(sums[0], sums[1], sums[0])
    net.settle(loads[1])

    def grad_qkv_rows(rows):
        w_qkv[rows, :] = t_dot(normed[:, rows], grads_ref[...]).astype(BF)

    every(512, grad_qkv_rows)
    wide_qkv = wide_sum(
        net, w_qkv, *sum_qkv, [(grad_query, 0, 320), (grad_key, 320, 80), (grad_value, 400, 80)]
    )
    step(wide_qkv, sums[1], sums[0])
    gain_terms(gain_one_part, down_part, normed, gains, 0)
    both = jnp.concatenate(
        [gain_one_part[0:1, :], gain_two_part[0:1, :], jnp.zeros((6, D), F32)], axis=0
    )
    for j in range(8):
        parts[j, :, :320] = both[:, j * 320 : (j + 1) * 320]
        parts[j, :, 320:] = jnp.zeros((8, 64), F32)
    me = at.n
    copies = [net.send(parts.at[p[1]], narrow_parts.at[me], p) for p in at.narrow_peers()]
    narrow_parts[me] = parts[me]
    step(sums[1], sums[0], wide_qkv, wide_out, sums[1], wide_du, wide_qkv)
    finish(sums[0])
    step(sums[1])
    for copy in copies:
        copy.wait_recv()
    sum_parts = narrow_parts[0]
    for k in range(1, 8):
        sum_parts += narrow_parts[k]
    wide_parts[0] = sum_parts
    copies = [
        net.send(wide_parts.at[0], wide_parts.at[k + 1], p) for k, p in enumerate(everyone)
    ]
    step(wide_out, wide_qkv)
    finish(sums[1])
    stream, grad = x_rows[...], total_two[...]
    inv = lax.rsqrt(jnp.mean(stream * stream, axis=1, keepdims=True) + epsilon)
    weighted = grad * gains[0:1, :]
    inner = jnp.sum(weighted * stream, axis=1, keepdims=True)
    through = inv * weighted - stream * (inv * inv * inv * inner / D)
    by_feature(rows_two, (grad_mid_own[...] + through).astype(BF))
    back = narrow_swap(net, rows_two, back_two)
    step(back, wide_out, wide_qkv, wide_du)
    finish(wide_out, wide_du, wide_qkv)
    for copy in copies:
        copy.wait_recv()
    finish(back, output_rows)
    net.run([])


def closing(*refs):
    ins, outs = refs[:10], refs[10:]
    for rows, out in ((ins[0], outs[0]), (ins[1], outs[1])):
        halves = [rows[:, pl.ds(h * 32, 32), :].reshape(256, 320) for h in (0, 1)]
        out[...] = jnp.concatenate(halves, axis=0).astype(F32).T.astype(out.dtype)
    total = ins[2][0]
    for k in range(1, 16):
        total += ins[2][k]
    outs[2][...] = total[0:1, :320].reshape(320)
    outs[3][...] = total[1:2, :320].reshape(320)
    for source, out in zip(ins[3:], outs[4:]):
        out[...] = source[...]


def wide_sum_scratch(columns):
    return [
        pltpu.VMEM((4, 2, ROWS, columns), BF),
        pltpu.VMEM((3, 2, ROWS, columns), BF),
        pltpu.VMEM((ROWS, columns), BF),
    ]


def vmem():
    return pl.BlockSpec(memory_space=pltpu.VMEM)


def hbm():
    return pl.BlockSpec(memory_space=pl.ANY)


def exchange(name, number, body, ins, outs, scratch=()):
    def room_for(where, shape, dtype):
        return [pltpu.VMEM(shape, dtype)] if where == "vmem" else []

    in_rooms = [room_for(where, a.shape, a.dtype) for a, where in ins]
    out_rooms = [room_for(where, shape, dtype) for shape, dtype, where in outs]
    rooms = [r for part in (*in_rooms, *out_rooms) for r in part]

    def kernel(*refs):
        a, b = len(ins), len(ins) + len(outs)
        c = b + len(rooms)
        spare = iter(refs[b:c])
        net = Net(Place(), *refs[-3:])
        in_refs = [next(spare) if room else ref for ref, room in zip(refs[:a], in_rooms)]
        out_refs = [next(spare) if room else ref for ref, room in zip(refs[a:b], out_rooms)]
        net.loads = [net.keep(far, near) for far, near in zip(refs[:a], in_refs) if far is not near]
        body(net, in_refs, out_refs, refs[c:-3])
        for far, near in zip(refs[a:b], out_refs):
            if far is not near:
                net.keep(near, far)
        net.settle(*net.open)

    def spec(where):
        return pl.BlockSpec(memory_space=pltpu.SMEM) if where == "smem" else hbm()

    return pl.pallas_call(
        kernel,
        out_shape=[jax.ShapeDtypeStruct(shape, dtype) for shape, dtype, _ in outs],
        in_specs=[spec(where) for _, where in ins],
        out_specs=[hbm() for _ in outs],
        scratch_shapes=[
            *rooms,
            *scratch,
            pltpu.SemaphoreType.DMA((200,)),
            pltpu.SemaphoreType.DMA((200,)),
            pltpu.SemaphoreType.DMA((56,)),
        ],
        compiler_params=pltpu.CompilerParams(
            collective_id=number, has_side_effects=True, vmem_limit_bytes=60 * 2**20
        ),
        name=name,
    )(*[array for array, _ in ins])


def scaled_freqs():
    freqs = (rope_base ** (-2.0 * np.arange(HEAD // 2) / HEAD)).astype(np.float32)
    wavelen = (2.0 * math.pi / freqs).astype(np.float32)
    smooth = (long_wave / wavelen - 1.0) / 3.0
    blended = (1.0 - smooth) * freqs / rope_factor + smooth * freqs
    return np.where(
        wavelen < short_wave, freqs, np.where(wavelen > long_wave, freqs / rope_factor, blended)
    ).astype(np.float32)


def body(
    layer_input,
    gain_attn,
    w_query,
    w_key,
    w_value,
    w_out,
    gain_mlp,
    w_gate,
    w_up,
    w_down,
    doc_lengths,
    cotangent,
):
    def held(*shape, dtype=BF):
        return (shape, dtype, "vmem")

    def far(*shape, dtype=BF):
        return (shape, dtype, "hbm")

    def room(*shape, dtype=BF):
        return pltpu.VMEM(shape, dtype)

    def local(*arrays):
        return [(a, "vmem") for a in arrays]

    def remote(*arrays):
        return [(a, "hbm") for a in arrays]

    freqs = jnp.asarray(np.repeat(scaled_freqs()[:, None], 128, axis=1))
    slots = room(2, 12, OWN // 2, D)
    own = room(OWN, D, dtype=F32)
    (
        normed,
        w_qkv,
        w_o,
        cot,
        w_gu,
        w_d,
        normed_two,
        queries,
        kv,
        lse,
        low,
        tables,
        attended,
        x_rows,
        mid,
        inverse,
        gains,
    ) = exchange(
        "attention",
        1,
        attention,
        remote(layer_input.T, cotangent.T)
        + local(w_query, w_key, w_value, w_out.T, w_gate, w_up, w_down.T, gain_attn, gain_mlp, freqs)
        + [(doc_lengths, "smem")],
        [
            far(TOK, D),
            far(D, 512),
            far(D, 384),
            far(D, TOK),
            far(D, 2 * PANEL),
            far(D, PANEL),
            far(TOK, D),
            held(4, TILE, 4 * TILE),
            held(3 * TOK, 256),
            held(4, 1, 4 * TILE, dtype=F32),
            held(4, 1, 4 * TILE, dtype=jnp.int32),
            held(2, 40, TOK, dtype=F32),
            held(TOK, 320),
            held(OWN, D, dtype=F32),
            held(OWN, D, dtype=F32),
            held(OWN, 128, dtype=F32),
            held(8, D, dtype=F32),
        ],
        [
            room(ROWS, 512),
            room(ROWS, 384),
            room(ROWS, 2 * PANEL),
            room(8, 384, dtype=F32),
            room(8, 8, 384, dtype=F32),
            room(D, 512),
            room(D, 384),
            room(D, TOK),
            room(TOK, D),
            room(TOK, D),
            room(512, TOK, dtype=F32),
            room(TOK, D),
            slots,
            own,
            room(TILE, 3 * TOK),
            room(OWN, D),
        ],
    )
    grad_mid, grad_mid_own, down_part, grad_gate, grad_du, gain_two_part = exchange(
        "mlp",
        2,
        mlp,
        remote(normed_two, w_d, w_gu, cot) + local(mid, inverse, gains),
        [
            far(TOK, D),
            held(OWN, D, dtype=F32),
            far(TOK, D),
            held(ROWS, PANEL, dtype=F32),
            far(D, 2 * PANEL),
            held(8, D, dtype=F32),
        ],
        [
            room(D, 2 * PANEL),
            room(D, PANEL),
            room(TOK, D),
            room(D, TOK),
            room(TOK, D),
            room(TOK, 2 * PANEL, dtype=F32),
            room(TOK, PANEL, dtype=F32),
            room(TOK, PANEL),
            room(TOK, 2 * PANEL),
            room(TOK, D),
            room(TOK, D),
            slots,
            own,
            *wide_sum_scratch(PANEL),
            room(OWN, D),
            room(TOK, D),
        ],
    )
    output_rows, grad_rows, gain_parts, grad_out, grad_query, grad_key, grad_value, grad_d, grad_up = exchange(
        "attention_back",
        3,
        attention_back,
        remote(grad_mid, normed, w_qkv, w_o, down_part, grad_du)
        + local(grad_mid_own, attended, queries, kv, lse, low, tables, mid, x_rows, gains, gain_two_part),
        [
            held(8, OWN, 320),
            held(8, OWN, 320),
            held(16, 8, 384, dtype=F32),
            held(ROWS, 320, dtype=F32),
            held(ROWS, 320, dtype=F32),
            held(ROWS, 80, dtype=F32),
            held(ROWS, 80, dtype=F32),
            held(ROWS, PANEL, dtype=F32),
            held(ROWS, PANEL, dtype=F32),
        ],
        [
            room(TOK, D),
            room(TOK, D),
            room(D, 512),
            room(D, 384),
            room(TOK, D),
            room(4, 2, ROWS, 2 * PANEL),
            room(4, TILE, 4 * TILE),
            room(TILE, 3 * TOK),
            room(3 * TOK, 256, dtype=F32),
            room(320, TOK, dtype=F32),
            slots,
            slots,
            own,
            own,
            room(2 * TOK, 256),
            room(2, TOK, 256),
            room(TOK, 320, dtype=F32),
            room(8, OWN, 320),
            room(8, OWN, 320),
            room(8, 8, 384, dtype=F32),
            room(8, 8, 384, dtype=F32),
            room(TOK, 512),
            *wide_sum_scratch(2 * PANEL),
            *wide_sum_scratch(384),
            *wide_sum_scratch(512),
            room(8, D, dtype=F32),
        ],
    )
    results = [
        ((320, TOK), BF),
        ((320, TOK), F32),
        ((320,), F32),
        ((320,), F32),
        ((ROWS, 320), F32),
        ((ROWS, 80), F32),
        ((ROWS, 80), F32),
        ((ROWS, 320), F32),
        ((ROWS, PANEL), F32),
        ((ROWS, PANEL), F32),
        ((ROWS, PANEL), F32),
    ]
    out = pl.pallas_call(
        closing,
        out_shape=[jax.ShapeDtypeStruct(shape, dtype) for shape, dtype in results],
        in_specs=[vmem()] * 10,
        out_specs=[vmem()] * 11,
        name="closing",
    )(output_rows, grad_rows, gain_parts, grad_query, grad_key, grad_value, grad_out, grad_gate, grad_up, grad_d)
    return (
        out[0].T,
        out[1].T,
        out[2],
        out[4],
        out[5],
        out[6],
        out[7].T,
        out[3],
        out[8],
        out[9],
        out[10].T,
    )


def solution(mesh):
    rows, columns = P("wide", "narrow"), P("narrow", "wide")
    return jax.shard_map(
        body,
        mesh=mesh,
        in_specs=(
            rows,
            P("narrow"),
            rows,
            rows,
            rows,
            columns,
            P("narrow"),
            rows,
            rows,
            columns,
            P(),
            rows,
        ),
        out_specs=(
            rows,
            rows,
            P("narrow"),
            rows,
            rows,
            rows,
            columns,
            P("narrow"),
            rows,
            rows,
            columns,
        ),
        check_vma=False,
    )
```

```python
import functools
import math

import jax
import jax.numpy as jnp
import numpy as np
from jax import lax
from jax.experimental import pallas as pl
from jax.experimental.pallas import tpu as pltpu
from jax.sharding import PartitionSpec as P

D = 2560
HEADS = 32
KV_HEADS = 8
HEAD = 80
WINDOW = 1024
TOK = 512
OWN = 64
ROWS = 160
PANEL = 896
TILE = 128
REACH = WINDOW + TILE
CUT = 768

epsilon = 1e-05
rope_base = 1000000.0
rope_factor = 8.0
long_wave = 8192.0
short_wave = 2048.0
masked = -1e30

MESH = pl.DeviceIdType.MESH
BF = jnp.bfloat16
F32 = jnp.float32


class Place:
    def __init__(self):
        self.w = lax.axis_index("wide")
        self.n = lax.axis_index("narrow")
        self.z, self.h, self.c = self.w // 4, (self.w // 2) % 2, self.w % 2
        self.x, self.l = self.n // 2, self.n % 2

    def wide(self, dz, dh, dc):
        return ((self.z + dz) % 4) * 4 + ((self.h + dh) % 2) * 2 + (self.c + dc) % 2

    def narrow(self, dx, dl):
        return ((self.x + dx) % 4) * 2 + (self.l + dl) % 2

    def narrow_peers(self):
        return [(self.w, self.narrow(k // 2, k % 2)) for k in (2, 6, 1, 3, 7, 4, 5)]

    def wide_peers(self):
        return [(self.wide(*d), self.n) for d in ((0, 1, 0), (1, 0, 0), (3, 0, 0), (2, 0, 0), (0, 0, 1))]


class Net:
    def __init__(self, place, send_sems, recv_sems, local_sems):
        self.at = place
        self.sems = (send_sems, recv_sems, local_sems)
        self.sent, self.kept, self.open, self.done = [], [], [], 0

    def barrier(self, givers, takers):
        bar = pltpu.get_barrier_semaphore()
        for device in givers:
            pl.semaphore_signal(bar, inc=1, device_id=device, device_id_type=MESH)
        self.settle(*self.loads)
        pl.semaphore_wait(bar, takers)

    def send(self, src, dst, device):
        i = len(self.sent)
        copy = pltpu.make_async_remote_copy(
            src_ref=src,
            dst_ref=dst,
            send_sem=self.sems[0].at[i],
            recv_sem=self.sems[1].at[i],
            device_id=device,
            device_id_type=MESH,
        )
        copy.start()
        self.sent.append(copy)
        return copy

    def keep(self, src, dst):
        copy = pltpu.make_async_copy(src, dst, self.sems[2].at[len(self.kept)])
        copy.start()
        self.kept.append(copy)
        self.open.append(copy)
        return copy

    def settle(self, *copies):
        for copy in copies:
            copy.wait()
            self.open = [c for c in self.open if c is not copy]

    def release(self, count):
        for copy in self.sent[self.done : count]:
            copy.wait_send()
        self.done = count

    def run(self, tasks):
        tasks = list(tasks)
        while tasks:
            left = []
            for task in tasks:
                try:
                    next(task)
                    left.append(task)
                except StopIteration:
                    pass
            tasks = left
        for copy in self.sent[self.done :]:
            copy.wait_send()
        self.settle(*self.open)


def block_of(ref, index, rows):
    return ref.at[pl.ds(pl.multiple_of(index * rows, 16), rows)]


def narrow_gather(net, src, dst, cut):
    at = net.at
    me, near = at.n, at.narrow(0, 1)
    right, left, beside = (at.w, at.narrow(1, 0)), (at.w, at.narrow(3, 0)), (at.w, near)
    rows, columns = src.shape
    upper, lower = pl.ds(0, rows // 2), pl.ds(rows // 2, rows // 2)
    early, late = pl.ds(0, cut), pl.ds(cut, columns - cut)

    def block(n):
        return block_of(dst, n, rows)

    def on(part, device):
        return net.send(part, part, device)

    kept = net.keep(src, block(me))
    first = net.send(src.at[:, late], block(me).at[:, late], beside)
    to_right, to_left = net.send(src, block(me), right), net.send(src, block(me), left)
    over = [net.send(src.at[:, early], block(me).at[:, early], beside)]
    yield
    first.wait_recv()
    part = block(near).at[:, late]
    near_right, near_left = on(part, right), on(part, left)
    yield
    to_right.wait_recv()
    part = block(at.narrow(3, 0))
    from_left = on(part.at[upper], right)
    over.append(on(part.at[:, early], beside))
    to_left.wait_recv()
    part = block(at.narrow(1, 0))
    from_right = on(part.at[lower], left)
    over.append(on(part.at[:, early], beside))
    yield
    near_right.wait_recv()
    over.append(on(block(at.narrow(3, 1)).at[upper, late], right))
    near_left.wait_recv()
    over.append(on(block(at.narrow(1, 1)).at[lower, late], left))
    yield
    from_left.wait_recv()
    from_right.wait_recv()
    over.append(on(block(at.narrow(2, 0)).at[:, early], beside))
    yield
    for copy in over:
        copy.wait_recv()
    net.settle(kept)


def narrow_share(net, src, dst):
    me = net.at.n
    copies = [net.send(src, dst.at[me], peer) for peer in net.at.narrow_peers()]
    kept = net.keep(src, dst.at[me])
    yield
    yield
    for copy in copies:
        copy.wait_recv()
    net.settle(kept)


def narrow_swap(net, src, dst):
    me = net.at.n
    copies = [net.send(src.at[peer[1]], dst.at[me], peer) for peer in net.at.narrow_peers()]
    kept = net.keep(src.at[me], dst.at[me])
    yield
    for copy in copies:
        copy.wait_recv()
    net.settle(kept)


def add_rows(rows, step, dst, terms):
    @pl.loop(0, rows // step)
    def _(i):
        part = pl.ds(pl.multiple_of(i * step, step), step)
        total = terms[0][part, :].astype(F32)
        for term in terms[1:]:
            total += term[part, :].astype(F32)
        dst[part, :] = total.astype(dst.dtype)


def narrow_sum(net, src, slots, out, cut, held=None):
    at = net.at
    me, near = at.n, at.narrow(0, 1)
    right, left, beside = (at.w, at.narrow(1, 0)), (at.w, at.narrow(3, 0)), (at.w, near)
    rows, columns = out.shape
    upper, lower = pl.ds(0, rows // 2), pl.ds(rows // 2, rows // 2)
    early, late = pl.ds(0, cut), pl.ds(cut, columns - cut)

    def block(n):
        return block_of(src, n, rows)

    def term(n, *part):
        return block_of(src if held is None else held, n, rows)[part].astype(F32)

    def put(slot, value, *part):
        slots[slot, *part] = value.astype(BF)

    def at_slot(slot, *part):
        return slots[slot, *part].astype(F32)

    everything = slice(None)
    over = {
        d: net.send(block(at.narrow(d, 1)).at[:, early], slots.at[k, :, early], beside)
        for d, k in ((2, 2), (1, 0), (3, 1))
    }
    far = block(at.narrow(2, 1))
    pass_right = net.send(far.at[upper, late], slots.at[3, upper, late], right)
    pass_left = net.send(far.at[lower, late], slots.at[3, lower, late], left)
    final = [net.send(block(near).at[:, early], slots.at[7, :, early], beside)]
    yield
    over[2].wait_recv()
    n = at.narrow(2, 0)
    put(2, at_slot(2, everything, early) + term(n, everything, early), everything, early)
    put(2, term(n, everything, late), everything, late)
    far_right = net.send(slots.at[2, upper], slots.at[4, upper], right)
    far_left = net.send(slots.at[2, lower], slots.at[4, lower], left)
    yield
    pass_right.wait_recv()
    n = at.narrow(1, 1)
    put(10, term(n, upper, late) + at_slot(3, upper, late), upper, late)
    put(10, term(n, lower, late), lower, late)
    near_right = net.send(slots.at[10, :, late], slots.at[8, :, late], right)
    pass_left.wait_recv()
    n = at.narrow(3, 1)
    put(11, term(n, lower, late) + at_slot(3, lower, late), lower, late)
    put(11, term(n, upper, late), upper, late)
    near_left = net.send(slots.at[11, :, late], slots.at[9, :, late], left)
    yield
    for d, slot, copy, half, whole in (
        (1, 0, far_right, upper, lower),
        (3, 1, far_left, lower, upper),
    ):
        over[d].wait_recv()
        copy.wait_recv()
        n = at.narrow(d, 0)
        put(slot, at_slot(slot, half, early) + term(n, half, early) + at_slot(4, half, early), half, early)
        put(slot, at_slot(slot, whole, early) + term(n, whole, early), whole, early)
        put(slot, term(n, half, late) + at_slot(4, half, late), half, late)
        put(slot, term(n, whole, late), whole, late)
        final.append(
            net.send(slots.at[slot], slots.at[5 + slot], right if d == 1 else left)
        )
    yield
    near_right.wait_recv()
    near_left.wait_recv()
    value = term(near, everything, late) + at_slot(8, everything, late) + at_slot(9, everything, late)
    put(8, value, everything, late)
    final.append(net.send(slots.at[8, :, late], slots.at[7, :, late], beside))
    yield
    for copy in final:
        copy.wait_recv()
    out[...] = term(me, everything, everything) + at_slot(5) + at_slot(6) + at_slot(7)


def wide_gather(net, src, dst):
    at = net.at
    half = ROWS // 2
    me, far = at.w, at.wide(0, 1, 0)
    up, down = (at.wide(1, 0, 0), at.n), (at.wide(3, 0, 0), at.n)
    other = (at.wide(0, 0, 1), at.n)

    def block(w):
        return block_of(dst, w, ROWS)

    kept = net.keep(src, block(me))
    turns = [[net.send(src, block(me), up), net.send(src, block(me), down)]]
    over = [net.send(src, block(me), other)]
    further = []

    def relay(e):
        for d, part, ahead, copy in (
            (3, slice(0, half), up, turns[e][0]),
            (1, slice(half, ROWS), down, turns[e][1]),
        ):
            copy.wait_recv()
            shard = block(at.wide(d, e, 0))
            further.append((e, part, net.send(shard.at[part], shard.at[part], ahead)))
            over.append(net.send(shard, shard, other))

    yield
    from_far = net.send(src, block(me), (far, at.n))
    yield
    relay(0)
    yield
    from_far.wait_recv()
    turns.append([net.send(block(far), block(far), up), net.send(block(far), block(far), down)])
    over.append(net.send(block(far), block(far), other))
    yield
    relay(1)
    yield
    for e, part, copy in further:
        copy.wait_recv()
        shard = block(at.wide(2, e, 0)).at[part]
        over.append(net.send(shard, shard, other))
    yield
    for copy in over:
        copy.wait_recv()
    net.settle(kept)


def wide_sum(net, src, core, turned, last, outs, held=None):
    at = net.at
    half = ROWS // 2
    up, down = (at.wide(1, 0, 0), at.n), (at.wide(3, 0, 0), at.n)
    other = (at.wide(0, 0, 1), at.n)
    order = [(d, e) for d in (2, 1, 3, 0) for e in (1, 0)]

    def block(w):
        return block_of(src, w, ROWS)

    over = {(d, e): net.send(block(at.wide(d, e, 1)), core.at[d, e], other) for d, e in order}
    yield
    further = []
    for d, e in order:
        over[d, e].wait_recv()
        part = core.at[d, e]
        add_rows(ROWS, 32, part, [part, block(at.wide(d, e, 0)) if held is None else held.at[d, e]])
        if d == 2:
            further.append(
                (
                    e,
                    net.send(part.at[:half], turned.at[2, e, :half], up),
                    net.send(part.at[half:], turned.at[2, e, half:], down),
                )
            )
    yield
    turns = []
    for e, first, second in further:
        first.wait_recv()
        part = core.at[1, e]
        add_rows(half, 16, part.at[:half], [part.at[:half], turned.at[2, e, :half]])
        turns.append((e, net.send(part, turned.at[0, e], up)))
        second.wait_recv()
        part = core.at[3, e]
        add_rows(half, 16, part.at[half:], [part.at[half:], turned.at[2, e, half:]])
        turns.append((e, net.send(part, turned.at[1, e], down)))
        yield
    for e, copy in turns:
        if e:
            copy.wait_recv()
    part = core.at[0, 1]
    add_rows(ROWS, 32, part, [part, turned.at[0, 1], turned.at[1, 1]])
    final = net.send(part, last, (at.wide(0, 1, 0), at.n))
    yield
    for e, copy in turns:
        if not e:
            copy.wait_recv()
    final.wait_recv()

    @pl.loop(0, ROWS // 32)
    def _(i):
        part = pl.ds(pl.multiple_of(i * 32, 32), 32)
        total = core[0, 0, part, :].astype(F32) + last[part, :].astype(F32)
        for d in range(2):
            total += turned[d, 0, part, :].astype(F32)
        for out, first, columns in outs:
            out[part, :] = total[:, first : first + columns]


def step(*tasks):
    for task in tasks:
        next(task, None)


def finish(*tasks):
    tasks = list(tasks)
    while tasks:
        tasks = [task for task in tasks if next(task, "end") != "end"]


def pieces_of(width, size, body):
    whole = width // size

    @pl.loop(0, whole)
    def _(i):
        body(pl.ds(pl.multiple_of(i * size, size), size))

    if width % size:
        body(pl.ds(whole * size, width % size))


def dot(a, b):
    return jnp.dot(a, b, preferred_element_type=F32)


def dot_t(a, b):
    return lax.dot_general(a, b, (((1,), (1,)), ((), ())), preferred_element_type=F32)


def t_dot(a, b):
    return lax.dot_general(a, b, (((0,), (0,)), ((), ())), preferred_element_type=F32)


def scores(keys, queries, low, first):
    raw = dot(keys, queries) * (1.0 / math.sqrt(HEAD))
    key = first + lax.broadcasted_iota(jnp.int32, raw.shape, 0)
    query = first + WINDOW + lax.broadcasted_iota(jnp.int32, raw.shape, 1) % TILE
    return jnp.where((key >= low) & (key <= query), raw, masked)


def gain_terms(dst, grad, normed, gains, k):
    def part(columns):
        total = jnp.sum(
            grad[:, columns].astype(F32) * normed[:, columns].astype(F32), axis=0, keepdims=True
        )
        dst[:, columns] = jnp.broadcast_to(total / gains[k : k + 1, columns], (8, 256))

    every(256, part)


def by_feature(dst, rows):
    for j in range(8):
        dst[j] = rows[:, j * 320 : (j + 1) * 320]


def every(size, body, begin=0, end=D):
    @pl.loop(begin // size, end // size)
    def _(i):
        body(pl.ds(pl.multiple_of(i * size, size), size))


def attention(net, ins, outs, scratch):
    x_own, cot_own, w_query, w_key, w_value, w_out, w_gate, w_up, w_down = ins[:9]
    gain_one, gain_two, freqs, lengths = ins[9:]
    normed_far, w_qkv_far, w_out_far, cot, w_g, w_u, w_d, normed_two = outs[:8]
    queries, kv, lse, low, tables, attended, x_rows, mid, inverse, gains = outs[8:]
    (
        shard_qkv,
        shard_out,
        gains_own,
        gain_pieces,
        w_qkv,
        w_o,
        x_t,
        x,
        normed,
        qkv,
        src,
        slots,
        total,
        values_t,
        normed_mid,
    ) = scratch
    at = net.at
    later = [((at.w + k) % 16, at.n) for k in (1, 2)]
    earlier = [((at.w + 16 - k) % 16, at.n) for k in (1, 2)]
    net.barrier(at.narrow_peers() + at.wide_peers() + earlier, 14)
    shard_qkv[:, :320] = w_query[...]
    shard_qkv[:, 320:] = jnp.concatenate(
        [w_key[...], w_value[...], jnp.zeros((ROWS, 32), BF)], axis=1
    )
    gains_own[...] = jnp.zeros(gains_own.shape, F32)
    gains_own[0:1, :320] = gain_one[...].reshape(1, 320)
    gains_own[1:2, :320] = gain_two[...].reshape(1, 320)
    panel = wide_gather(net, shard_qkv, w_qkv)
    step(panel, panel)
    lanes = [pl.ds(0, 256), pl.ds(256, 256)]
    streams = [
        narrow_gather(net, x_own.at[:, half], x_t.at[:, half], 128) for half in lanes
    ]
    sizes = narrow_share(net, gains_own, gain_pieces)
    step(streams[0], sizes)
    shard_out[...] = jnp.concatenate([w_out[...], jnp.zeros((ROWS, 64), BF)], axis=1)

    place = at.w * TOK + lax.broadcasted_iota(jnp.int32, (1, TOK), 1)
    begins, end = jnp.zeros((1, TOK), jnp.int32), 0
    for k in range(8):
        end = end + lengths[k]
        begins = jnp.where(place >= end, end, begins)
    position = place - begins
    angles = freqs[:, 0:1] * position.astype(F32)
    cos, sin = jnp.cos(angles), jnp.sin(angles)
    tables[0], tables[1] = cos, sin
    first_key = jnp.maximum(begins, jnp.maximum(place - (WINDOW - 1), 0)) - (at.w - 2) * TOK
    for tile in range(4):
        one = first_key[:, tile * TILE : (tile + 1) * TILE]
        low[tile] = jnp.concatenate([one] * 4, axis=1)

    step(streams[0], streams[1], panel, panel, streams[0], streams[1], panel)
    w_outs = wide_gather(net, shard_out, w_o)
    gate, up = wide_gather(net, w_gate, w_g), wide_gather(net, w_up, w_u)
    step(w_outs, w_outs, gate, streams[0], streams[1], streams[0], panel, streams[1])
    step(streams[1], gate, w_outs, w_outs, up)
    finish(panel, sizes)
    step(w_outs)
    finish(streams[0])
    for j in range(8):
        gains[:, pl.ds(j * 320, 320)] = gain_pieces[j, :, :320]

    def norm_in(h):
        every(256, lambda rows: turned_over(x.at[pl.ds(h * 256, 256)], x_t.at[:, lanes[h]], rows))

        @pl.loop(h * 16, h * 16 + 16)
        def _(i):
            rows = pl.ds(pl.multiple_of(i * 16, 16), 16)
            part = x[rows, :].astype(F32)
            inv = lax.rsqrt(jnp.mean(part * part, axis=1, keepdims=True) + epsilon)
            normed[rows, :] = (part * inv * gains[0:1, :]).astype(BF)

    norm_in(0)
    finish(streams[1])
    cots = narrow_gather(net, cot_own, cot, 256)
    down = wide_gather(net, w_down, w_d)
    step(cots, gate, down)
    norm_in(1)
    for h in range(2):
        x_rows[pl.ds(h * 32, 32), :] = x[own_rows(at, h), :].astype(F32)
    part = pl.ds(256, 256)
    qkv[part, :] = dot(normed[...], w_qkv[:, part]).T
    zeros = jnp.zeros((48, TOK), F32)

    def turned(at_row):
        a, b = qkv[pl.ds(at_row, 40), :], qkv[pl.ds(at_row + 40, 40), :]
        return jnp.concatenate([a * cos - b * sin, b * cos + a * sin, zeros], axis=0)

    mine = pl.ds(2 * TOK, TOK)
    kv[mine, :128] = turned(320).T.astype(BF)
    kv[mine, 128:] = jnp.concatenate([qkv[pl.ds(400, 80), :], zeros], axis=0).T.astype(BF)
    arriving = [
        net.send(kv.at[mine], kv.at[pl.ds((2 - k) * TOK, TOK)], later[k - 1]) for k in (1, 2)
    ]
    step(up, cots, down)
    part = pl.ds(0, 256)
    qkv[part, :] = dot(normed[...], w_qkv[:, part]).T
    for head in range(4):
        one = turned(head * HEAD).astype(BF)
        for tile in range(4):
            queries[tile, :, pl.ds(head * TILE, TILE)] = one[:, tile * TILE : (tile + 1) * TILE]
    step(w_outs, gate, up)
    for copy in arriving:
        copy.wait_recv()
    values_t[...] = kv[:, 128:].T

    def one_tile(i):
        first = pl.multiple_of(i * TILE, TILE)
        seen = pl.ds(first, REACH)
        s = scores(kv[seen, :128], queries[i], low[i], first)
        largest = jnp.max(s, axis=0, keepdims=True)
        powers = jnp.exp(s - largest)
        totals = jnp.sum(powers, axis=0, keepdims=True)
        weights = (powers / totals).astype(BF)
        lse[i] = largest + jnp.log(totals)
        mixed = dot(values_t[:, seen], weights)
        attended[pl.ds(first, TILE), :] = (
            jnp.concatenate([mixed[:HEAD, h * TILE : (h + 1) * TILE] for h in range(4)], axis=0)
            .T.astype(BF)
        )

    def out_part(h):
        tokens = pl.ds(h * 256, 256)

        def columns(rows):
            src[tokens, rows] = dot_t(attended[tokens, :], w_o[rows, :320]).astype(BF)

        every(512, columns)
        return narrow_sum(net, src.at[tokens], slots.at[h], total.at[pl.ds(h * 32, 32)], CUT)

    def norm_part(h):
        rows = pl.ds(h * 32, 32)
        stream = x_rows[rows, :] + total[rows, :]
        mid[rows, :] = stream
        inv = lax.rsqrt(jnp.mean(stream * stream, axis=1, keepdims=True) + epsilon)
        inverse[rows, :] = jnp.broadcast_to(inv, (32, 128))
        normed_mid[rows, :] = (stream * inv * gains[1:2, :]).astype(BF)
        return narrow_gather(
            net, normed_mid.at[rows], normed_two.at[pl.ds(h * 256, 256)], CUT
        )

    pl.loop(0, 2)(one_tile)
    finish(w_outs)
    early = out_part(0)
    step(early, cots, gate, up, cots)
    pl.loop(2, 4)(one_tile)
    step(early, early)
    late = out_part(1)
    step(early, late, early, down, late)
    net.keep(w_o, w_out_far)
    net.keep(normed, normed_far)
    step(late)
    net.keep(w_qkv, w_qkv_far)
    finish(early)
    ahead = norm_part(0)
    step(ahead, late, up, gate, ahead, late, down, ahead)
    step(cots, ahead, up, ahead, down)
    finish(late)
    behind = norm_part(1)
    step(behind, down, behind, behind, down)
    finish(ahead)
    step(behind, behind)
    finish(behind, gate, up, cots, down)
    net.run([])


def own_rows(at, h):
    return pl.ds(pl.multiple_of(h * 256 + at.n * 32, 32), 32)


def turned_over(dst, src, rows):
    dst[:, rows] = src[rows, :].T


def mlp(net, ins, outs, scratch):
    normed_far, d_far, g_far, u_far, cot_far, mid, inverse, gains = ins
    grad_mid_far, grad_mid, down_far, grad_gate, du_far, gain_part = outs
    w_gu, w_d, normed, cot_t, cot, gu, grad_hidden, hidden, grad_pre, src = scratch[:10]
    down_part, slots, total, core, turned, last, low = scratch[10:17]
    at = net.at
    sources = (normed_far, g_far, u_far, cot_far, d_far)
    rooms = (normed, w_gu.at[:, pl.ds(0, PANEL)], w_gu.at[:, pl.ds(PANEL, PANEL)], cot_t, w_d)
    loads = [net.keep(a, b) for a, b in zip(sources, rooms)]
    net.barrier(at.narrow_peers() + at.wide_peers(), 12)
    tokens = [pl.ds(0, 256), pl.ds(256, 256)]
    own = [pl.ds(0, 32), pl.ds(32, 32)]
    def gate_up(h):
        def part(columns):
            gu[tokens[h], columns] = dot(normed[tokens[h], :], w_gu[:, columns])

        pieces_of(2 * PANEL, 256, part)

    def back_down(h):
        def part(columns):
            grad_hidden[tokens[h], columns] = dot(cot[tokens[h], :], w_d[:, columns])

        pieces_of(PANEL, 256, part)

    def back_hidden(h):
        @pl.loop(h * 16, h * 16 + 16)
        def _(i):
            rows = pl.ds(pl.multiple_of(i * 16, 16), 16)
            gate, up, grad = gu[rows, :PANEL], gu[rows, PANEL:], grad_hidden[rows, :]
            sigmoid = jax.nn.sigmoid(gate)
            active = gate * sigmoid
            hidden[rows, :] = (active * up).astype(BF)
            grad_pre[rows, :PANEL] = (
                grad * up * sigmoid * (1.0 + gate * (1.0 - sigmoid))
            ).astype(BF)
            grad_pre[rows, PANEL:] = (grad * active).astype(BF)

    def back_normed(h):
        def part(rows):
            src[tokens[h], rows] = dot_t(grad_pre[tokens[h], :], w_gu[rows, :]).astype(BF)

        every(256, part)
        return narrow_sum(net, src.at[tokens[h]], slots.at[h], total.at[own[h]], CUT)

    def back_norm(h):
        inv, scale = inverse[own[h], :1], gains[1:2, :]
        grad, stream = total[own[h], :], mid[own[h], :]
        weighted = grad * scale
        inner = jnp.sum(weighted * stream, axis=1, keepdims=True)
        through = inv * weighted - stream * (inv * inv * inv * inner / D)
        mine = cot[own_rows(at, h), :].astype(F32) + through
        grad_mid[own[h], :] = mine
        low[own[h], :] = mine.astype(BF)
        return narrow_gather(net, low.at[own[h]], grad_mid_far.at[tokens[h]], CUT)

    net.settle(*loads[:3])
    gate_up(0)
    net.settle(*loads[3:])
    every(256, lambda rows: turned_over(cot, cot_t, rows))
    back_down(0)
    back_hidden(0)
    sums = [back_normed(0)]
    step(sums[0])
    gate_up(1)
    step(sums[0])
    back_down(1)
    step(sums[0])
    back_hidden(1)
    step(sums[0])
    sums.append(back_normed(1))
    step(sums[0], sums[1])

    def grad_gate_rows(rows):
        w_gu[rows, :PANEL] = t_dot(normed[:, rows], grad_pre[:, :PANEL]).astype(BF)

    every(256, grad_gate_rows, 0, 1280)
    step(sums[1])
    finish(sums[0])
    back = [back_norm(0)]
    step(back[0], sums[1])
    every(256, grad_gate_rows, 1280, D)
    wide = wide_sum(net, w_gu.at[:, pl.ds(0, PANEL)], core, turned, last, [(grad_gate, 0, PANEL)])
    step(back[0], sums[1], wide, back[0])

    def grad_up_rows(rows):
        w_gu[rows, PANEL:] = t_dot(normed[:, rows], grad_pre[:, PANEL:]).astype(BF)

    every(256, grad_up_rows, 0, 1280)
    step(sums[1], back[0], wide)
    every(256, grad_up_rows, 1280, D)
    finish(sums[1])
    back.append(back_norm(1))
    step(back[1], back[0])
    net.keep(w_gu.at[:, pl.ds(PANEL, PANEL)], du_far.at[:, pl.ds(PANEL, PANEL)])

    def forward_down(rows):
        down_part[:, rows] = dot_t(hidden[...], w_d[rows, :]).astype(BF)

    every(256, forward_down, 0, 1280)
    step(back[1], wide)
    every(256, forward_down, 1280, D)
    net.keep(down_part, down_far)
    step(back[1], wide)

    def grad_d_rows(rows):
        w_d[rows, :] = dot(cot_t[rows, :], hidden[...]).astype(BF)

    every(256, grad_d_rows, 0, 1280)
    step(back[1], wide, back[1])
    every(256, grad_d_rows, 1280, D)
    net.keep(w_d, du_far.at[:, pl.ds(0, PANEL)])
    finish(back[0])
    step(wide)
    gain_terms(gain_part, src, normed, gains, 1)
    finish(back[1])
    finish(wide)
    net.run([])


def attention_back(net, ins, outs, scratch):
    grad_mid_far, normed_far, w_qkv_far, w_out_far, down_far, du_far = ins[:6]
    grad_mid_own, attended, queries, kv, lse, low, tables, mid, x_rows, gains, gain_two_part = ins[6:]
    back_one, back_two, wide_parts, grad_out, grad_query, grad_key, grad_value, grad_d, grad_up = outs
    grad_mid, normed, w_qkv, w_o, down_part, held_du = scratch[:6]
    upstream, keys_t, grad_kv, grad_q, slots_one, slots_two, total_one, total_two = scratch[6:14]
    later_kv, turned_back, ga, rows_one, rows_two, parts, narrow_parts, grads_ref = scratch[14:22]
    sum_du, sum_out, sum_qkv, gain_one_part = scratch[22:25], scratch[25:28], scratch[28:31], scratch[31]
    at = net.at
    tokens = [pl.ds(0, 256), pl.ds(256, 256)]
    own = [pl.ds(0, 32), pl.ds(32, 32)]
    loads = [net.keep(a, b) for a, b in zip(ins[:5], (grad_mid, normed, w_qkv, w_o, down_part))]
    held_loads = [
        net.keep(block_of(du_far, at.wide(d, e, 0), ROWS), held_du.at[d, e])
        for d in range(4)
        for e in range(2)
    ]
    everyone = [((at.w + k) % 16, at.n) for k in range(1, 16)]
    net.barrier(at.narrow_peers() + everyone, 22)
    wide_du = wide_sum(
        net, du_far, *sum_du, [(grad_d, 0, PANEL), (grad_up, PANEL, PANEL)], held_du
    )
    downs = [
        narrow_sum(
            net, down_far.at[tokens[h]], slots_one.at[h], total_one.at[own[h]], CUT, down_part.at[tokens[h]]
        )
        for h in (0, 1)
    ]
    step(wide_du, *downs)
    net.settle(loads[0], loads[3])
    for first, columns in ((0, 256), (256, 64)):
        ga[:, pl.ds(first, columns)] = dot(grad_mid[...], w_o[:, pl.ds(first, columns)])
    grads_t = ga[...].T
    zeros = jnp.zeros((48, TOK), F32)
    for head in range(4):
        one = jnp.concatenate([grads_t[head * HEAD : (head + 1) * HEAD], zeros], axis=0).astype(BF)
        for tile in range(4):
            upstream[tile, :, pl.ds(head * TILE, TILE)] = one[:, tile * TILE : (tile + 1) * TILE]
    keys_t[...] = kv[:, :128].T
    net.settle(loads[4], *held_loads)
    step(downs[0], wide_du, downs[1], *downs)
    fill = jnp.zeros((512, 64), F32)

    def grad_out_rows(rows):
        w_o[rows, :] = jnp.concatenate(
            [t_dot(grad_mid[:, rows], attended[...]), fill], axis=1
        ).astype(BF)

    every(512, grad_out_rows)
    wide_out = wide_sum(net, w_o, *sum_out, [(grad_out, 0, 320)])
    step(wide_out)
    grad_kv[...] = jnp.zeros(grad_kv.shape, F32)
    factor = 1.0 / math.sqrt(HEAD)

    def one_tile(i):
        first = pl.multiple_of(i * TILE, TILE)
        seen = pl.ds(first, REACH)
        s = scores(kv[seen, :128], queries[i], low[i], first)
        weights = jnp.exp(s - lse[i])
        grad_weights = dot(kv[seen, 128:], upstream[i])
        inner = jnp.sum(weights * grad_weights, axis=0, keepdims=True)
        grad_scores = (weights * (grad_weights - inner)).astype(BF)
        grad_kv[seen, 128:] += dot_t(weights.astype(BF), upstream[i])
        grad_kv[seen, :128] += dot_t(grad_scores, queries[i]) * factor
        back = dot(keys_t[:, seen], grad_scores) * factor
        for head in range(4):
            grad_q[pl.ds(head * HEAD, HEAD), pl.ds(first, TILE)] = back[
                :HEAD, head * TILE : (head + 1) * TILE
            ]

    pl.loop(0, 2)(one_tile)
    step(*downs, wide_du, *downs, wide_out)
    pl.loop(2, 4)(one_tile)
    later_kv[...] = grad_kv[pl.ds(0, 2 * TOK), :].astype(BF)
    arriving = [
        net.send(
            later_kv.at[pl.ds((2 - k) * TOK, TOK)],
            turned_back.at[2 - k],
            ((at.w + 16 - k) % 16, at.n),
        )
        for k in (1, 2)
    ]
    cos, sin = tables[0], tables[1]

    def unturned(part):
        a, b = part[:40], part[40:80]
        return [a * cos + b * sin, b * cos - a * sin]

    rotated = []
    for head in range(4):
        rotated += unturned(grad_q[pl.ds(head * HEAD, HEAD), :])
    step(wide_du)
    finish(*downs)
    by_feature(rows_one, (mid[...] + total_one[...]).astype(BF))
    output_rows = narrow_swap(net, rows_one, back_one)
    step(output_rows)
    for copy in arriving:
        copy.wait_recv()
    whole = (
        grad_kv[pl.ds(2 * TOK, TOK), :]
        + turned_back[0].astype(F32)
        + turned_back[1].astype(F32)
    )
    rotated += unturned(whole[:, :128].T)
    rotated += [whole[:, 128:].T[:HEAD], jnp.zeros((32, TOK), F32)]
    grads_ref[...] = jnp.concatenate(rotated, axis=0).T.astype(BF)
    net.settle(loads[2])

    def back_normed(h):
        def part(rows):
            down_part[tokens[h], rows] = dot_t(grads_ref[tokens[h], :], w_qkv[rows, :]).astype(BF)

        every(256, part)
        return narrow_sum(net, down_part.at[tokens[h]], slots_two.at[h], total_two.at[own[h]], CUT)

    sums = [back_normed(0)]
    step(sums[0], wide_out)
    sums.append(back_normed(1))
    step(sums[0], sums[1], sums[0], wide_du)
    net.settle(loads[1])

    def grad_qkv_rows(rows):
        w_qkv[rows, :] = t_dot(normed[:, rows], grads_ref[...]).astype(BF)

    every(512, grad_qkv_rows)
    wide_qkv = wide_sum(
        net, w_qkv, *sum_qkv, [(grad_query, 0, 320), (grad_key, 320, 80), (grad_value, 400, 80)]
    )
    step(wide_qkv, sums[1], sums[0])
    gain_terms(gain_one_part, down_part, normed, gains, 0)
    both = jnp.concatenate(
        [gain_one_part[0:1, :], gain_two_part[0:1, :], jnp.zeros((6, D), F32)], axis=0
    )
    for j in range(8):
        parts[j, :, :320] = both[:, j * 320 : (j + 1) * 320]
        parts[j, :, 320:] = jnp.zeros((8, 64), F32)
    me = at.n
    copies = [net.send(parts.at[p[1]], narrow_parts.at[me], p) for p in at.narrow_peers()]
    narrow_parts[me] = parts[me]
    step(sums[1], sums[0], wide_qkv, sums[1], wide_out, wide_qkv)
    finish(sums[0])
    step(sums[1], wide_qkv)
    for copy in copies:
        copy.wait_recv()
    sum_parts = narrow_parts[0]
    for k in range(1, 8):
        sum_parts += narrow_parts[k]
    wide_parts[0] = sum_parts
    copies = [
        net.send(wide_parts.at[0], wide_parts.at[k + 1], p) for k, p in enumerate(everyone)
    ]
    step(wide_out, wide_qkv, wide_du)
    finish(sums[1])
    stream, grad = x_rows[...], total_two[...]
    inv = lax.rsqrt(jnp.mean(stream * stream, axis=1, keepdims=True) + epsilon)
    weighted = grad * gains[0:1, :]
    inner = jnp.sum(weighted * stream, axis=1, keepdims=True)
    through = inv * weighted - stream * (inv * inv * inv * inner / D)
    by_feature(rows_two, (grad_mid_own[...] + through).astype(BF))
    back = narrow_swap(net, rows_two, back_two)
    step(back, wide_out, wide_qkv, wide_du)
    finish(wide_out, wide_du, wide_qkv)
    for copy in copies:
        copy.wait_recv()
    finish(back, output_rows)
    net.run([])


def closing(*refs):
    ins, outs = refs[:10], refs[10:]
    for rows, out in ((ins[0], outs[0]), (ins[1], outs[1])):
        halves = [rows[:, pl.ds(h * 32, 32), :].reshape(256, 320) for h in (0, 1)]
        out[...] = jnp.concatenate(halves, axis=0).astype(F32).T.astype(out.dtype)
    total = ins[2][0]
    for k in range(1, 16):
        total += ins[2][k]
    outs[2][...] = total[0:1, :320].reshape(320)
    outs[3][...] = total[1:2, :320].reshape(320)
    for source, out in zip(ins[3:], outs[4:]):
        out[...] = source[...]


def wide_sum_scratch(columns):
    return [
        pltpu.VMEM((4, 2, ROWS, columns), BF),
        pltpu.VMEM((3, 2, ROWS, columns), BF),
        pltpu.VMEM((ROWS, columns), BF),
    ]


def vmem():
    return pl.BlockSpec(memory_space=pltpu.VMEM)


def hbm():
    return pl.BlockSpec(memory_space=pl.ANY)


def exchange(name, number, body, ins, outs, scratch=()):
    def room_for(where, shape, dtype):
        return [pltpu.VMEM(shape, dtype)] if where == "vmem" else []

    in_rooms = [room_for(where, a.shape, a.dtype) for a, where in ins]
    out_rooms = [room_for(where, shape, dtype) for shape, dtype, where in outs]
    rooms = [r for part in (*in_rooms, *out_rooms) for r in part]

    def kernel(*refs):
        a, b = len(ins), len(ins) + len(outs)
        c = b + len(rooms)
        spare = iter(refs[b:c])
        net = Net(Place(), *refs[-3:])
        in_refs = [next(spare) if room else ref for ref, room in zip(refs[:a], in_rooms)]
        out_refs = [next(spare) if room else ref for ref, room in zip(refs[a:b], out_rooms)]
        net.loads = [net.keep(far, near) for far, near in zip(refs[:a], in_refs) if far is not near]
        body(net, in_refs, out_refs, refs[c:-3])
        for far, near in zip(refs[a:b], out_refs):
            if far is not near:
                net.keep(near, far)
        net.settle(*net.open)

    def spec(where):
        return pl.BlockSpec(memory_space=pltpu.SMEM) if where == "smem" else hbm()

    return pl.pallas_call(
        kernel,
        out_shape=[jax.ShapeDtypeStruct(shape, dtype) for shape, dtype, _ in outs],
        in_specs=[spec(where) for _, where in ins],
        out_specs=[hbm() for _ in outs],
        scratch_shapes=[
            *rooms,
            *scratch,
            pltpu.SemaphoreType.DMA((200,)),
            pltpu.SemaphoreType.DMA((200,)),
            pltpu.SemaphoreType.DMA((56,)),
        ],
        compiler_params=pltpu.CompilerParams(
            collective_id=number, has_side_effects=True, vmem_limit_bytes=60 * 2**20
        ),
        name=name,
    )(*[array for array, _ in ins])


def scaled_freqs():
    freqs = (rope_base ** (-2.0 * np.arange(HEAD // 2) / HEAD)).astype(np.float32)
    wavelen = (2.0 * math.pi / freqs).astype(np.float32)
    smooth = (long_wave / wavelen - 1.0) / 3.0
    blended = (1.0 - smooth) * freqs / rope_factor + smooth * freqs
    return np.where(
        wavelen < short_wave, freqs, np.where(wavelen > long_wave, freqs / rope_factor, blended)
    ).astype(np.float32)


def body(
    layer_input,
    gain_attn,
    w_query,
    w_key,
    w_value,
    w_out,
    gain_mlp,
    w_gate,
    w_up,
    w_down,
    doc_lengths,
    cotangent,
):
    def held(*shape, dtype=BF):
        return (shape, dtype, "vmem")

    def far(*shape, dtype=BF):
        return (shape, dtype, "hbm")

    def room(*shape, dtype=BF):
        return pltpu.VMEM(shape, dtype)

    def local(*arrays):
        return [(a, "vmem") for a in arrays]

    def remote(*arrays):
        return [(a, "hbm") for a in arrays]

    freqs = jnp.asarray(np.repeat(scaled_freqs()[:, None], 128, axis=1))
    slots = room(2, 12, OWN // 2, D)
    own = room(OWN, D, dtype=F32)
    (
        normed,
        w_qkv,
        w_o,
        cot,
        w_g,
        w_u,
        w_d,
        normed_two,
        queries,
        kv,
        lse,
        low,
        tables,
        attended,
        x_rows,
        mid,
        inverse,
        gains,
    ) = exchange(
        "attention",
        1,
        attention,
        remote(layer_input.T, cotangent.T)
        + local(w_query, w_key, w_value, w_out.T, w_gate, w_up, w_down.T, gain_attn, gain_mlp, freqs)
        + [(doc_lengths, "smem")],
        [
            far(TOK, D),
            far(D, 512),
            far(D, 384),
            far(D, TOK),
            far(D, PANEL),
            far(D, PANEL),
            far(D, PANEL),
            far(TOK, D),
            held(4, TILE, 4 * TILE),
            held(3 * TOK, 256),
            held(4, 1, 4 * TILE, dtype=F32),
            held(4, 1, 4 * TILE, dtype=jnp.int32),
            held(2, 40, TOK, dtype=F32),
            held(TOK, 320),
            held(OWN, D, dtype=F32),
            held(OWN, D, dtype=F32),
            held(OWN, 128, dtype=F32),
            held(8, D, dtype=F32),
        ],
        [
            room(ROWS, 512),
            room(ROWS, 384),
            room(8, 384, dtype=F32),
            room(8, 8, 384, dtype=F32),
            room(D, 512),
            room(D, 384),
            room(D, TOK),
            room(TOK, D),
            room(TOK, D),
            room(512, TOK, dtype=F32),
            room(TOK, D),
            slots,
            own,
            room(TILE, 3 * TOK),
            room(OWN, D),
        ],
    )
    grad_mid, grad_mid_own, down_part, grad_gate, grad_du, gain_two_part = exchange(
        "mlp",
        2,
        mlp,
        remote(normed_two, w_d, w_g, w_u, cot) + local(mid, inverse, gains),
        [
            far(TOK, D),
            held(OWN, D, dtype=F32),
            far(TOK, D),
            held(ROWS, PANEL, dtype=F32),
            far(D, 2 * PANEL),
            held(8, D, dtype=F32),
        ],
        [
            room(D, 2 * PANEL),
            room(D, PANEL),
            room(TOK, D),
            room(D, TOK),
            room(TOK, D),
            room(TOK, 2 * PANEL, dtype=F32),
            room(TOK, PANEL, dtype=F32),
            room(TOK, PANEL),
            room(TOK, 2 * PANEL),
            room(TOK, D),
            room(TOK, D),
            slots,
            own,
            *wide_sum_scratch(PANEL),
            room(OWN, D),
        ],
    )
    output_rows, grad_rows, gain_parts, grad_out, grad_query, grad_key, grad_value, grad_d, grad_up = exchange(
        "attention_back",
        3,
        attention_back,
        remote(grad_mid, normed, w_qkv, w_o, down_part, grad_du)
        + local(grad_mid_own, attended, queries, kv, lse, low, tables, mid, x_rows, gains, gain_two_part),
        [
            held(8, OWN, 320),
            held(8, OWN, 320),
            held(16, 8, 384, dtype=F32),
            held(ROWS, 320, dtype=F32),
            held(ROWS, 320, dtype=F32),
            held(ROWS, 80, dtype=F32),
            held(ROWS, 80, dtype=F32),
            held(ROWS, PANEL, dtype=F32),
            held(ROWS, PANEL, dtype=F32),
        ],
        [
            room(TOK, D),
            room(TOK, D),
            room(D, 512),
            room(D, 384),
            room(TOK, D),
            room(4, 2, ROWS, 2 * PANEL),
            room(4, TILE, 4 * TILE),
            room(TILE, 3 * TOK),
            room(3 * TOK, 256, dtype=F32),
            room(320, TOK, dtype=F32),
            slots,
            slots,
            own,
            own,
            room(2 * TOK, 256),
            room(2, TOK, 256),
            room(TOK, 320, dtype=F32),
            room(8, OWN, 320),
            room(8, OWN, 320),
            room(8, 8, 384, dtype=F32),
            room(8, 8, 384, dtype=F32),
            room(TOK, 512),
            *wide_sum_scratch(2 * PANEL),
            *wide_sum_scratch(384),
            *wide_sum_scratch(512),
            room(8, D, dtype=F32),
        ],
    )
    results = [
        ((320, TOK), BF),
        ((320, TOK), F32),
        ((320,), F32),
        ((320,), F32),
        ((ROWS, 320), F32),
        ((ROWS, 80), F32),
        ((ROWS, 80), F32),
        ((ROWS, 320), F32),
        ((ROWS, PANEL), F32),
        ((ROWS, PANEL), F32),
        ((ROWS, PANEL), F32),
    ]
    out = pl.pallas_call(
        closing,
        out_shape=[jax.ShapeDtypeStruct(shape, dtype) for shape, dtype in results],
        in_specs=[vmem()] * 10,
        out_specs=[vmem()] * 11,
        name="closing",
    )(output_rows, grad_rows, gain_parts, grad_query, grad_key, grad_value, grad_out, grad_gate, grad_up, grad_d)
    return (
        out[0].T,
        out[1].T,
        out[2],
        out[4],
        out[5],
        out[6],
        out[7].T,
        out[3],
        out[8],
        out[9],
        out[10].T,
    )


def solution(mesh):
    rows, columns = P("wide", "narrow"), P("narrow", "wide")
    return jax.shard_map(
        body,
        mesh=mesh,
        in_specs=(
            rows,
            P("narrow"),
            rows,
            rows,
            rows,
            columns,
            P("narrow"),
            rows,
            rows,
            columns,
            P(),
            rows,
        ),
        out_specs=(
            rows,
            rows,
            P("narrow"),
            rows,
            rows,
            rows,
            columns,
            P("narrow"),
            rows,
            rows,
            columns,
        ),
        check_vma=False,
    )
```

```python
import functools
import math

import jax
import jax.numpy as jnp
import numpy as np
from jax import lax
from jax.experimental import pallas as pl
from jax.experimental.pallas import tpu as pltpu
from jax.sharding import PartitionSpec as P

D = 2560
HEADS = 32
KV_HEADS = 8
HEAD = 80
WINDOW = 1024
TOK = 512
OWN = 64
ROWS = 160
PANEL = 896
TILE = 128
REACH = WINDOW + TILE
CUT = 768

epsilon = 1e-05
rope_base = 1000000.0
rope_factor = 8.0
long_wave = 8192.0
short_wave = 2048.0
masked = -1e30

MESH = pl.DeviceIdType.MESH
BF = jnp.bfloat16
F32 = jnp.float32


class Place:
    def __init__(self):
        self.w = lax.axis_index("wide")
        self.n = lax.axis_index("narrow")
        self.z, self.h, self.c = self.w // 4, (self.w // 2) % 2, self.w % 2
        self.x, self.l = self.n // 2, self.n % 2

    def wide(self, dz, dh, dc):
        return ((self.z + dz) % 4) * 4 + ((self.h + dh) % 2) * 2 + (self.c + dc) % 2

    def narrow(self, dx, dl):
        return ((self.x + dx) % 4) * 2 + (self.l + dl) % 2

    def narrow_peers(self):
        return [(self.w, self.narrow(k // 2, k % 2)) for k in (2, 6, 1, 3, 7, 4, 5)]

    def wide_peers(self):
        return [(self.wide(*d), self.n) for d in ((0, 1, 0), (1, 0, 0), (3, 0, 0), (2, 0, 0), (0, 0, 1))]


class Net:
    def __init__(self, place, send_sems, recv_sems, local_sems):
        self.at = place
        self.sems = (send_sems, recv_sems, local_sems)
        self.sent, self.kept, self.open, self.done = [], [], [], 0

    def barrier(self, givers, takers):
        bar = pltpu.get_barrier_semaphore()
        for device in givers:
            pl.semaphore_signal(bar, inc=1, device_id=device, device_id_type=MESH)
        self.settle(*self.loads)
        pl.semaphore_wait(bar, takers)

    def send(self, src, dst, device):
        i = len(self.sent)
        copy = pltpu.make_async_remote_copy(
            src_ref=src,
            dst_ref=dst,
            send_sem=self.sems[0].at[i],
            recv_sem=self.sems[1].at[i],
            device_id=device,
            device_id_type=MESH,
        )
        copy.start()
        self.sent.append(copy)
        return copy

    def keep(self, src, dst):
        copy = pltpu.make_async_copy(src, dst, self.sems[2].at[len(self.kept)])
        copy.start()
        self.kept.append(copy)
        self.open.append(copy)
        return copy

    def settle(self, *copies):
        for copy in copies:
            copy.wait()
            self.open = [c for c in self.open if c is not copy]

    def release(self, count):
        for copy in self.sent[self.done : count]:
            copy.wait_send()
        self.done = count

    def run(self, tasks):
        tasks = list(tasks)
        while tasks:
            left = []
            for task in tasks:
                try:
                    next(task)
                    left.append(task)
                except StopIteration:
                    pass
            tasks = left
        for copy in self.sent[self.done :]:
            copy.wait_send()
        self.settle(*self.open)


def block_of(ref, index, rows):
    return ref.at[pl.ds(pl.multiple_of(index * rows, 16), rows)]


def narrow_gather(net, src, dst, cut):
    at = net.at
    me, near = at.n, at.narrow(0, 1)
    right, left, beside = (at.w, at.narrow(1, 0)), (at.w, at.narrow(3, 0)), (at.w, near)
    rows, columns = src.shape
    upper, lower = pl.ds(0, rows // 2), pl.ds(rows // 2, rows // 2)
    early, late = pl.ds(0, cut), pl.ds(cut, columns - cut)

    def block(n):
        return block_of(dst, n, rows)

    def on(part, device):
        return net.send(part, part, device)

    kept = net.keep(src, block(me))
    first = net.send(src.at[:, late], block(me).at[:, late], beside)
    to_right, to_left = net.send(src, block(me), right), net.send(src, block(me), left)
    over = [net.send(src.at[:, early], block(me).at[:, early], beside)]
    yield
    first.wait_recv()
    part = block(near).at[:, late]
    near_right, near_left = on(part, right), on(part, left)
    yield
    to_right.wait_recv()
    part = block(at.narrow(3, 0))
    from_left = on(part.at[upper], right)
    over.append(on(part.at[:, early], beside))
    to_left.wait_recv()
    part = block(at.narrow(1, 0))
    from_right = on(part.at[lower], left)
    over.append(on(part.at[:, early], beside))
    yield
    near_right.wait_recv()
    over.append(on(block(at.narrow(3, 1)).at[upper, late], right))
    near_left.wait_recv()
    over.append(on(block(at.narrow(1, 1)).at[lower, late], left))
    yield
    from_left.wait_recv()
    from_right.wait_recv()
    over.append(on(block(at.narrow(2, 0)).at[:, early], beside))
    yield
    for copy in over:
        copy.wait_recv()
    net.settle(kept)


def narrow_share(net, src, dst):
    me = net.at.n
    copies = [net.send(src, dst.at[me], peer) for peer in net.at.narrow_peers()]
    kept = net.keep(src, dst.at[me])
    yield
    yield
    for copy in copies:
        copy.wait_recv()
    net.settle(kept)


def narrow_swap(net, src, dst):
    me = net.at.n
    copies = [net.send(src.at[peer[1]], dst.at[me], peer) for peer in net.at.narrow_peers()]
    kept = net.keep(src.at[me], dst.at[me])
    yield
    for copy in copies:
        copy.wait_recv()
    net.settle(kept)


def add_rows(rows, step, dst, terms):
    @pl.loop(0, rows // step)
    def _(i):
        part = pl.ds(pl.multiple_of(i * step, step), step)
        total = terms[0][part, :].astype(F32)
        for term in terms[1:]:
            total += term[part, :].astype(F32)
        dst[part, :] = total.astype(dst.dtype)


def narrow_sum(net, src, slots, out, cut, held=None):
    at = net.at
    me, near = at.n, at.narrow(0, 1)
    right, left, beside = (at.w, at.narrow(1, 0)), (at.w, at.narrow(3, 0)), (at.w, near)
    rows, columns = out.shape
    upper, lower = pl.ds(0, rows // 2), pl.ds(rows // 2, rows // 2)
    early, late = pl.ds(0, cut), pl.ds(cut, columns - cut)

    def block(n):
        return block_of(src, n, rows)

    def term(n, *part):
        return block_of(src if held is None else held, n, rows)[part].astype(F32)

    def put(slot, value, *part):
        slots[slot, *part] = value.astype(BF)

    def at_slot(slot, *part):
        return slots[slot, *part].astype(F32)

    everything = slice(None)
    over = {
        d: net.send(block(at.narrow(d, 1)).at[:, early], slots.at[k, :, early], beside)
        for d, k in ((2, 2), (1, 0), (3, 1))
    }
    far = block(at.narrow(2, 1))
    pass_right = net.send(far.at[upper, late], slots.at[3, upper, late], right)
    pass_left = net.send(far.at[lower, late], slots.at[3, lower, late], left)
    final = [net.send(block(near).at[:, early], slots.at[7, :, early], beside)]
    yield
    over[2].wait_recv()
    n = at.narrow(2, 0)
    put(2, at_slot(2, everything, early) + term(n, everything, early), everything, early)
    put(2, term(n, everything, late), everything, late)
    far_right = net.send(slots.at[2, upper], slots.at[4, upper], right)
    far_left = net.send(slots.at[2, lower], slots.at[4, lower], left)
    yield
    pass_right.wait_recv()
    n = at.narrow(1, 1)
    put(10, term(n, upper, late) + at_slot(3, upper, late), upper, late)
    put(10, term(n, lower, late), lower, late)
    near_right = net.send(slots.at[10, :, late], slots.at[8, :, late], right)
    pass_left.wait_recv()
    n = at.narrow(3, 1)
    put(11, term(n, lower, late) + at_slot(3, lower, late), lower, late)
    put(11, term(n, upper, late), upper, late)
    near_left = net.send(slots.at[11, :, late], slots.at[9, :, late], left)
    yield
    for d, slot, copy, half, whole in (
        (1, 0, far_right, upper, lower),
        (3, 1, far_left, lower, upper),
    ):
        over[d].wait_recv()
        copy.wait_recv()
        n = at.narrow(d, 0)
        put(slot, at_slot(slot, half, early) + term(n, half, early) + at_slot(4, half, early), half, early)
        put(slot, at_slot(slot, whole, early) + term(n, whole, early), whole, early)
        put(slot, term(n, half, late) + at_slot(4, half, late), half, late)
        put(slot, term(n, whole, late), whole, late)
        final.append(
            net.send(slots.at[slot], slots.at[5 + slot], right if d == 1 else left)
        )
    yield
    near_right.wait_recv()
    near_left.wait_recv()
    value = term(near, everything, late) + at_slot(8, everything, late) + at_slot(9, everything, late)
    put(8, value, everything, late)
    final.append(net.send(slots.at[8, :, late], slots.at[7, :, late], beside))
    yield
    for copy in final:
        copy.wait_recv()
    out[...] = term(me, everything, everything) + at_slot(5) + at_slot(6) + at_slot(7)


def wide_gather(net, src, dst):
    at = net.at
    half = ROWS // 2
    me, far = at.w, at.wide(0, 1, 0)
    up, down = (at.wide(1, 0, 0), at.n), (at.wide(3, 0, 0), at.n)
    other = (at.wide(0, 0, 1), at.n)

    def block(w):
        return block_of(dst, w, ROWS)

    kept = net.keep(src, block(me))
    turns = [[net.send(src, block(me), up), net.send(src, block(me), down)]]
    over = [net.send(src, block(me), other)]
    further = []

    def relay(e):
        for d, part, ahead, copy in (
            (3, slice(0, half), up, turns[e][0]),
            (1, slice(half, ROWS), down, turns[e][1]),
        ):
            copy.wait_recv()
            shard = block(at.wide(d, e, 0))
            further.append((e, part, net.send(shard.at[part], shard.at[part], ahead)))
            over.append(net.send(shard, shard, other))

    yield
    from_far = net.send(src, block(me), (far, at.n))
    yield
    relay(0)
    yield
    from_far.wait_recv()
    turns.append([net.send(block(far), block(far), up), net.send(block(far), block(far), down)])
    over.append(net.send(block(far), block(far), other))
    yield
    relay(1)
    yield
    for e, part, copy in further:
        copy.wait_recv()
        shard = block(at.wide(2, e, 0)).at[part]
        over.append(net.send(shard, shard, other))
    yield
    for copy in over:
        copy.wait_recv()
    net.settle(kept)


def wide_sum(net, src, core, turned, last, outs, held=None):
    at = net.at
    half = ROWS // 2
    up, down = (at.wide(1, 0, 0), at.n), (at.wide(3, 0, 0), at.n)
    other = (at.wide(0, 0, 1), at.n)
    order = [(d, e) for d in (2, 1, 3, 0) for e in (1, 0)]

    def block(w):
        return block_of(src, w, ROWS)

    over = {(d, e): net.send(block(at.wide(d, e, 1)), core.at[d, e], other) for d, e in order}
    yield
    further = []
    for d, e in order:
        over[d, e].wait_recv()
        part = core.at[d, e]
        add_rows(ROWS, 32, part, [part, block(at.wide(d, e, 0)) if held is None else held.at[d, e]])
        if d == 2:
            further.append(
                (
                    e,
                    net.send(part.at[:half], turned.at[2, e, :half], up),
                    net.send(part.at[half:], turned.at[2, e, half:], down),
                )
            )
    yield
    turns = []
    for e, first, second in further:
        first.wait_recv()
        part = core.at[1, e]
        add_rows(half, 16, part.at[:half], [part.at[:half], turned.at[2, e, :half]])
        turns.append((e, net.send(part, turned.at[0, e], up)))
        second.wait_recv()
        part = core.at[3, e]
        add_rows(half, 16, part.at[half:], [part.at[half:], turned.at[2, e, half:]])
        turns.append((e, net.send(part, turned.at[1, e], down)))
        yield
    for e, copy in turns:
        if e:
            copy.wait_recv()
    part = core.at[0, 1]
    add_rows(ROWS, 32, part, [part, turned.at[0, 1], turned.at[1, 1]])
    final = net.send(part, last, (at.wide(0, 1, 0), at.n))
    yield
    for e, copy in turns:
        if not e:
            copy.wait_recv()
    final.wait_recv()

    @pl.loop(0, ROWS // 32)
    def _(i):
        part = pl.ds(pl.multiple_of(i * 32, 32), 32)
        total = core[0, 0, part, :].astype(F32) + last[part, :].astype(F32)
        for d in range(2):
            total += turned[d, 0, part, :].astype(F32)
        for out, first, columns in outs:
            out[part, :] = total[:, first : first + columns]


def step(*tasks):
    for task in tasks:
        next(task, None)


def finish(*tasks):
    tasks = list(tasks)
    while tasks:
        tasks = [task for task in tasks if next(task, "end") != "end"]


def pieces_of(width, size, body):
    whole = width // size

    @pl.loop(0, whole)
    def _(i):
        body(pl.ds(pl.multiple_of(i * size, size), size))

    if width % size:
        body(pl.ds(whole * size, width % size))


def dot(a, b):
    return jnp.dot(a, b, preferred_element_type=F32)


def dot_t(a, b):
    return lax.dot_general(a, b, (((1,), (1,)), ((), ())), preferred_element_type=F32)


def t_dot(a, b):
    return lax.dot_general(a, b, (((0,), (0,)), ((), ())), preferred_element_type=F32)


def scores(keys, queries, low, first):
    raw = dot(keys, queries) * (1.0 / math.sqrt(HEAD))
    key = first + lax.broadcasted_iota(jnp.int32, raw.shape, 0)
    query = first + WINDOW + lax.broadcasted_iota(jnp.int32, raw.shape, 1) % TILE
    return jnp.where((key >= low) & (key <= query), raw, masked)


def gain_terms(dst, grad, normed, gains, k):
    def part(columns):
        total = jnp.sum(
            grad[:, columns].astype(F32) * normed[:, columns].astype(F32), axis=0, keepdims=True
        )
        dst[:, columns] = jnp.broadcast_to(total / gains[k : k + 1, columns], (8, 256))

    every(256, part)


def by_feature(dst, rows):
    for j in range(8):
        dst[j] = rows[:, j * 320 : (j + 1) * 320]


def every(size, body, begin=0, end=D):
    @pl.loop(begin // size, end // size)
    def _(i):
        body(pl.ds(pl.multiple_of(i * size, size), size))


def attention(net, ins, outs, scratch):
    x_own, cot_own, w_query, w_key, w_value, w_out, w_gate, w_up, w_down = ins[:9]
    gain_one, gain_two, freqs, lengths = ins[9:]
    normed_far, w_qkv_far, w_out_far, cot, w_g, w_u, w_d, normed_two = outs[:8]
    queries, kv, lse, low, tables, attended, x_rows, mid, inverse, gains = outs[8:]
    (
        shard_qkv,
        shard_out,
        gains_own,
        gain_pieces,
        w_qkv,
        w_o,
        x_t,
        x,
        normed,
        qkv,
        src,
        slots,
        total,
        values_t,
        normed_mid,
    ) = scratch
    at = net.at
    later = [((at.w + k) % 16, at.n) for k in (1, 2)]
    earlier = [((at.w + 16 - k) % 16, at.n) for k in (1, 2)]
    net.barrier(at.narrow_peers() + at.wide_peers() + earlier, 14)
    shard_qkv[:, :320] = w_query[...]
    shard_qkv[:, 320:] = jnp.concatenate(
        [w_key[...], w_value[...], jnp.zeros((ROWS, 32), BF)], axis=1
    )
    gains_own[...] = jnp.zeros(gains_own.shape, F32)
    gains_own[0:1, :320] = gain_one[...].reshape(1, 320)
    gains_own[1:2, :320] = gain_two[...].reshape(1, 320)
    panel = wide_gather(net, shard_qkv, w_qkv)
    step(panel, panel)
    lanes = [pl.ds(0, 256), pl.ds(256, 256)]
    streams = [
        narrow_gather(net, x_own.at[:, half], x_t.at[:, half], 128) for half in lanes
    ]
    sizes = narrow_share(net, gains_own, gain_pieces)
    step(streams[0], sizes)
    shard_out[...] = jnp.concatenate([w_out[...], jnp.zeros((ROWS, 64), BF)], axis=1)

    place = at.w * TOK + lax.broadcasted_iota(jnp.int32, (1, TOK), 1)
    begins, end = jnp.zeros((1, TOK), jnp.int32), 0
    for k in range(8):
        end = end + lengths[k]
        begins = jnp.where(place >= end, end, begins)
    position = place - begins
    angles = freqs[:, 0:1] * position.astype(F32)
    cos, sin = jnp.cos(angles), jnp.sin(angles)
    tables[0], tables[1] = cos, sin
    first_key = jnp.maximum(begins, jnp.maximum(place - (WINDOW - 1), 0)) - (at.w - 2) * TOK
    for tile in range(4):
        one = first_key[:, tile * TILE : (tile + 1) * TILE]
        low[tile] = jnp.concatenate([one] * 4, axis=1)

    step(streams[0], streams[1], panel, panel, streams[0], streams[1], panel)
    w_outs = wide_gather(net, shard_out, w_o)
    gate, up = wide_gather(net, w_gate, w_g), wide_gather(net, w_up, w_u)
    step(w_outs, w_outs, gate, streams[0], streams[1], streams[0], panel, streams[1])
    step(streams[1], gate, w_outs, w_outs, up)
    finish(panel, sizes)
    step(w_outs)
    finish(streams[0])
    for j in range(8):
        gains[:, pl.ds(j * 320, 320)] = gain_pieces[j, :, :320]

    def norm_in(h):
        every(256, lambda rows: turned_over(x.at[pl.ds(h * 256, 256)], x_t.at[:, lanes[h]], rows))

        @pl.loop(h * 16, h * 16 + 16)
        def _(i):
            rows = pl.ds(pl.multiple_of(i * 16, 16), 16)
            part = x[rows, :].astype(F32)
            inv = lax.rsqrt(jnp.mean(part * part, axis=1, keepdims=True) + epsilon)
            normed[rows, :] = (part * inv * gains[0:1, :]).astype(BF)

    norm_in(0)
    finish(streams[1])
    cots = narrow_gather(net, cot_own, cot, 128)
    down = wide_gather(net, w_down, w_d)
    step(cots, gate, down)
    norm_in(1)
    for h in range(2):
        x_rows[pl.ds(h * 32, 32), :] = x[own_rows(at, h), :].astype(F32)
    part = pl.ds(256, 256)
    qkv[part, :] = dot(normed[...], w_qkv[:, part]).T
    zeros = jnp.zeros((48, TOK), F32)

    def turned(at_row):
        a, b = qkv[pl.ds(at_row, 40), :], qkv[pl.ds(at_row + 40, 40), :]
        return jnp.concatenate([a * cos - b * sin, b * cos + a * sin, zeros], axis=0)

    mine = pl.ds(2 * TOK, TOK)
    kv[mine, :128] = turned(320).T.astype(BF)
    kv[mine, 128:] = jnp.concatenate([qkv[pl.ds(400, 80), :], zeros], axis=0).T.astype(BF)
    arriving = [
        net.send(kv.at[mine], kv.at[pl.ds((2 - k) * TOK, TOK)], later[k - 1]) for k in (1, 2)
    ]
    step(up, cots, down)
    part = pl.ds(0, 256)
    qkv[part, :] = dot(normed[...], w_qkv[:, part]).T
    for head in range(4):
        one = turned(head * HEAD).astype(BF)
        for tile in range(4):
            queries[tile, :, pl.ds(head * TILE, TILE)] = one[:, tile * TILE : (tile + 1) * TILE]
    step(w_outs, gate, up)
    for copy in arriving:
        copy.wait_recv()
    values_t[...] = kv[:, 128:].T

    def one_tile(i):
        first = pl.multiple_of(i * TILE, TILE)
        seen = pl.ds(first, REACH)
        s = scores(kv[seen, :128], queries[i], low[i], first)
        largest = jnp.max(s, axis=0, keepdims=True)
        powers = jnp.exp(s - largest)
        totals = jnp.sum(powers, axis=0, keepdims=True)
        weights = (powers / totals).astype(BF)
        lse[i] = largest + jnp.log(totals)
        mixed = dot(values_t[:, seen], weights)
        attended[pl.ds(first, TILE), :] = (
            jnp.concatenate([mixed[:HEAD, h * TILE : (h + 1) * TILE] for h in range(4)], axis=0)
            .T.astype(BF)
        )

    def out_part(h):
        tokens = pl.ds(h * 256, 256)

        def columns(rows):
            src[tokens, rows] = dot_t(attended[tokens, :], w_o[rows, :320]).astype(BF)

        every(512, columns)
        return narrow_sum(net, src.at[tokens], slots.at[h], total.at[pl.ds(h * 32, 32)], CUT)

    def norm_part(h):
        rows = pl.ds(h * 32, 32)
        stream = x_rows[rows, :] + total[rows, :]
        mid[rows, :] = stream
        inv = lax.rsqrt(jnp.mean(stream * stream, axis=1, keepdims=True) + epsilon)
        inverse[rows, :] = jnp.broadcast_to(inv, (32, 128))
        normed_mid[rows, :] = (stream * inv * gains[1:2, :]).astype(BF)
        return narrow_gather(
            net, normed_mid.at[rows], normed_two.at[pl.ds(h * 256, 256)], CUT
        )

    pl.loop(0, 2)(one_tile)
    finish(w_outs)
    early = out_part(0)
    step(early, cots, gate, up, cots)
    pl.loop(2, 4)(one_tile)
    step(early, early)
    late = out_part(1)
    step(early, late, early, down, late)
    net.keep(w_o, w_out_far)
    net.keep(normed, normed_far)
    step(late)
    net.keep(w_qkv, w_qkv_far)
    finish(early)
    ahead = norm_part(0)
    step(ahead, late, up, gate, ahead, late, down, ahead)
    step(cots, ahead, up, ahead, down)
    finish(late)
    behind = norm_part(1)
    step(behind, down, behind, behind, down)
    finish(ahead)
    step(behind, behind)
    finish(behind, gate, up, cots, down)
    net.run([])


def own_rows(at, h):
    return pl.ds(pl.multiple_of(h * 256 + at.n * 32, 32), 32)


def turned_over(dst, src, rows):
    dst[:, rows] = src[rows, :].T


def mlp(net, ins, outs, scratch):
    normed_far, d_far, g_far, u_far, cot_far, mid, inverse, gains = ins
    grad_mid_far, grad_mid, down_far, grad_gate, du_far, gain_part = outs
    w_gu, w_d, normed, cot_t, cot, gu, grad_hidden, hidden, grad_pre, src = scratch[:10]
    down_part, slots, total, core, turned, last, low = scratch[10:17]
    at = net.at
    sources = (normed_far, g_far, u_far, cot_far, d_far)
    rooms = (normed, w_gu.at[:, pl.ds(0, PANEL)], w_gu.at[:, pl.ds(PANEL, PANEL)], cot_t, w_d)
    loads = [net.keep(a, b) for a, b in zip(sources, rooms)]
    net.barrier(at.narrow_peers() + at.wide_peers(), 12)
    tokens = [pl.ds(0, 256), pl.ds(256, 256)]
    own = [pl.ds(0, 32), pl.ds(32, 32)]
    def gate_up(h):
        def part(columns):
            gu[tokens[h], columns] = dot(normed[tokens[h], :], w_gu[:, columns])

        pieces_of(2 * PANEL, 256, part)

    def back_down(h):
        def part(columns):
            grad_hidden[tokens[h], columns] = dot(cot[tokens[h], :], w_d[:, columns])

        pieces_of(PANEL, 256, part)

    def back_hidden(h):
        @pl.loop(h * 16, h * 16 + 16)
        def _(i):
            rows = pl.ds(pl.multiple_of(i * 16, 16), 16)
            gate, up, grad = gu[rows, :PANEL], gu[rows, PANEL:], grad_hidden[rows, :]
            sigmoid = jax.nn.sigmoid(gate)
            active = gate * sigmoid
            hidden[rows, :] = (active * up).astype(BF)
            grad_pre[rows, :PANEL] = (
                grad * up * sigmoid * (1.0 + gate * (1.0 - sigmoid))
            ).astype(BF)
            grad_pre[rows, PANEL:] = (grad * active).astype(BF)

    def back_normed(h):
        def part(rows):
            src[tokens[h], rows] = dot_t(grad_pre[tokens[h], :], w_gu[rows, :]).astype(BF)

        every(256, part)
        return narrow_sum(net, src.at[tokens[h]], slots.at[h], total.at[own[h]], CUT)

    def back_norm(h):
        inv, scale = inverse[own[h], :1], gains[1:2, :]
        grad, stream = total[own[h], :], mid[own[h], :]
        weighted = grad * scale
        inner = jnp.sum(weighted * stream, axis=1, keepdims=True)
        through = inv * weighted - stream * (inv * inv * inv * inner / D)
        mine = cot[own_rows(at, h), :].astype(F32) + through
        grad_mid[own[h], :] = mine
        low[own[h], :] = mine.astype(BF)
        return narrow_gather(net, low.at[own[h]], grad_mid_far.at[tokens[h]], CUT)

    net.settle(*loads[:3])
    gate_up(0)
    net.settle(*loads[3:])
    every(256, lambda rows: turned_over(cot, cot_t, rows))
    back_down(0)
    back_hidden(0)
    sums = [back_normed(0)]
    step(sums[0])
    gate_up(1)
    step(sums[0])
    back_down(1)
    step(sums[0])
    back_hidden(1)
    step(sums[0])
    sums.append(back_normed(1))
    step(sums[0], sums[1])

    def grad_gate_rows(rows):
        w_gu[rows, :PANEL] = t_dot(normed[:, rows], grad_pre[:, :PANEL]).astype(BF)

    every(256, grad_gate_rows, 0, 1280)
    step(sums[1])
    finish(sums[0])
    back = [back_norm(0)]
    step(back[0], sums[1])
    every(256, grad_gate_rows, 1280, D)
    wide = wide_sum(net, w_gu.at[:, pl.ds(0, PANEL)], core, turned, last, [(grad_gate, 0, PANEL)])
    step(back[0], sums[1], wide, back[0])

    def grad_up_rows(rows):
        w_gu[rows, PANEL:] = t_dot(normed[:, rows], grad_pre[:, PANEL:]).astype(BF)

    every(256, grad_up_rows, 0, 1280)
    step(sums[1], back[0], wide)
    every(256, grad_up_rows, 1280, D)
    finish(sums[1])
    back.append(back_norm(1))
    step(back[1], back[0])
    net.keep(w_gu.at[:, pl.ds(PANEL, PANEL)], du_far.at[:, pl.ds(PANEL, PANEL)])

    def forward_down(rows):
        down_part[:, rows] = dot_t(hidden[...], w_d[rows, :]).astype(BF)

    every(256, forward_down, 0, 1280)
    step(back[1], wide)
    every(256, forward_down, 1280, D)
    net.keep(down_part, down_far)
    step(back[1], wide)

    def grad_d_rows(rows):
        w_d[rows, :] = dot(cot_t[rows, :], hidden[...]).astype(BF)

    every(256, grad_d_rows, 0, 1280)
    step(back[1], wide, back[1])
    every(256, grad_d_rows, 1280, D)
    net.keep(w_d, du_far.at[:, pl.ds(0, PANEL)])
    finish(back[0])
    step(wide)
    gain_terms(gain_part, src, normed, gains, 1)
    finish(back[1])
    finish(wide)
    net.run([])


def attention_back(net, ins, outs, scratch):
    grad_mid_far, normed_far, w_qkv_far, w_out_far, down_far, du_far = ins[:6]
    grad_mid_own, attended, queries, kv, lse, low, tables, mid, x_rows, gains, gain_two_part = ins[6:]
    back_one, back_two, wide_parts, grad_out, grad_query, grad_key, grad_value, grad_d, grad_up = outs
    grad_mid, normed, w_qkv, w_o, down_part, held_du = scratch[:6]
    upstream, keys_t, grad_kv, grad_q, slots_one, slots_two, total_one, total_two = scratch[6:14]
    later_kv, turned_back, ga, rows_one, rows_two, parts, narrow_parts, grads_ref = scratch[14:22]
    sum_du, sum_out, sum_qkv, gain_one_part = scratch[22:25], scratch[25:28], scratch[28:31], scratch[31]
    at = net.at
    tokens = [pl.ds(0, 256), pl.ds(256, 256)]
    own = [pl.ds(0, 32), pl.ds(32, 32)]
    loads = [net.keep(a, b) for a, b in zip(ins[:5], (grad_mid, normed, w_qkv, w_o, down_part))]
    held_loads = [
        net.keep(block_of(du_far, at.wide(d, e, 0), ROWS), held_du.at[d, e])
        for d in range(4)
        for e in range(2)
    ]
    everyone = [((at.w + k) % 16, at.n) for k in range(1, 16)]
    net.barrier(at.narrow_peers() + everyone, 22)
    wide_du = wide_sum(
        net, du_far, *sum_du, [(grad_d, 0, PANEL), (grad_up, PANEL, PANEL)], held_du
    )
    downs = [
        narrow_sum(
            net, down_far.at[tokens[h]], slots_one.at[h], total_one.at[own[h]], CUT, down_part.at[tokens[h]]
        )
        for h in (0, 1)
    ]
    step(wide_du, *downs)
    net.settle(loads[0], loads[3])
    for first, columns in ((0, 256), (256, 64)):
        ga[:, pl.ds(first, columns)] = dot(grad_mid[...], w_o[:, pl.ds(first, columns)])
    grads_t = ga[...].T
    zeros = jnp.zeros((48, TOK), F32)
    for head in range(4):
        one = jnp.concatenate([grads_t[head * HEAD : (head + 1) * HEAD], zeros], axis=0).astype(BF)
        for tile in range(4):
            upstream[tile, :, pl.ds(head * TILE, TILE)] = one[:, tile * TILE : (tile + 1) * TILE]
    keys_t[...] = kv[:, :128].T
    net.settle(loads[4], *held_loads)
    step(downs[0], wide_du, downs[1], *downs)
    fill = jnp.zeros((512, 64), F32)

    def grad_out_rows(rows):
        w_o[rows, :] = jnp.concatenate(
            [t_dot(grad_mid[:, rows], attended[...]), fill], axis=1
        ).astype(BF)

    every(512, grad_out_rows)
    wide_out = wide_sum(net, w_o, *sum_out, [(grad_out, 0, 320)])
    step(wide_out)
    grad_kv[...] = jnp.zeros(grad_kv.shape, F32)
    factor = 1.0 / math.sqrt(HEAD)

    def one_tile(i):
        first = pl.multiple_of(i * TILE, TILE)
        seen = pl.ds(first, REACH)
        s = scores(kv[seen, :128], queries[i], low[i], first)
        weights = jnp.exp(s - lse[i])
        grad_weights = dot(kv[seen, 128:], upstream[i])
        inner = jnp.sum(weights * grad_weights, axis=0, keepdims=True)
        grad_scores = (weights * (grad_weights - inner)).astype(BF)
        grad_kv[seen, 128:] += dot_t(weights.astype(BF), upstream[i])
        grad_kv[seen, :128] += dot_t(grad_scores, queries[i]) * factor
        back = dot(keys_t[:, seen], grad_scores) * factor
        for head in range(4):
            grad_q[pl.ds(head * HEAD, HEAD), pl.ds(first, TILE)] = back[
                :HEAD, head * TILE : (head + 1) * TILE
            ]

    pl.loop(0, 2)(one_tile)
    step(*downs, wide_du, *downs, wide_out)
    pl.loop(2, 4)(one_tile)
    later_kv[...] = grad_kv[pl.ds(0, 2 * TOK), :].astype(BF)
    arriving = [
        net.send(
            later_kv.at[pl.ds((2 - k) * TOK, TOK)],
            turned_back.at[2 - k],
            ((at.w + 16 - k) % 16, at.n),
        )
        for k in (1, 2)
    ]
    cos, sin = tables[0], tables[1]

    def unturned(part):
        a, b = part[:40], part[40:80]
        return [a * cos + b * sin, b * cos - a * sin]

    rotated = []
    for head in range(4):
        rotated += unturned(grad_q[pl.ds(head * HEAD, HEAD), :])
    step(wide_du)
    finish(*downs)
    by_feature(rows_one, (mid[...] + total_one[...]).astype(BF))
    output_rows = narrow_swap(net, rows_one, back_one)
    step(output_rows)
    for copy in arriving:
        copy.wait_recv()
    whole = (
        grad_kv[pl.ds(2 * TOK, TOK), :]
        + turned_back[0].astype(F32)
        + turned_back[1].astype(F32)
    )
    rotated += unturned(whole[:, :128].T)
    rotated += [whole[:, 128:].T[:HEAD], jnp.zeros((32, TOK), F32)]
    grads_ref[...] = jnp.concatenate(rotated, axis=0).T.astype(BF)
    net.settle(loads[2])

    def back_normed(h):
        def part(rows):
            down_part[tokens[h], rows] = dot_t(grads_ref[tokens[h], :], w_qkv[rows, :]).astype(BF)

        every(256, part)
        return narrow_sum(net, down_part.at[tokens[h]], slots_two.at[h], total_two.at[own[h]], CUT)

    sums = [back_normed(0)]
    step(sums[0], wide_out)
    sums.append(back_normed(1))
    step(sums[0], sums[1], sums[0], wide_du)
    net.settle(loads[1])

    def grad_qkv_rows(rows):
        w_qkv[rows, :] = t_dot(normed[:, rows], grads_ref[...]).astype(BF)

    every(512, grad_qkv_rows)
    wide_qkv = wide_sum(
        net, w_qkv, *sum_qkv, [(grad_query, 0, 320), (grad_key, 320, 80), (grad_value, 400, 80)]
    )
    step(wide_qkv, sums[1], sums[0])
    gain_terms(gain_one_part, down_part, normed, gains, 0)
    both = jnp.concatenate(
        [gain_one_part[0:1, :], gain_two_part[0:1, :], jnp.zeros((6, D), F32)], axis=0
    )
    for j in range(8):
        parts[j, :, :320] = both[:, j * 320 : (j + 1) * 320]
        parts[j, :, 320:] = jnp.zeros((8, 64), F32)
    me = at.n
    copies = [net.send(parts.at[p[1]], narrow_parts.at[me], p) for p in at.narrow_peers()]
    narrow_parts[me] = parts[me]
    step(sums[1], sums[0], wide_qkv, sums[1], wide_out, wide_qkv)
    finish(sums[0])
    step(sums[1], wide_qkv)
    for copy in copies:
        copy.wait_recv()
    sum_parts = narrow_parts[0]
    for k in range(1, 8):
        sum_parts += narrow_parts[k]
    wide_parts[0] = sum_parts
    copies = [
        net.send(wide_parts.at[0], wide_parts.at[k + 1], p) for k, p in enumerate(everyone)
    ]
    step(wide_out, wide_qkv, wide_du)
    finish(sums[1])
    stream, grad = x_rows[...], total_two[...]
    inv = lax.rsqrt(jnp.mean(stream * stream, axis=1, keepdims=True) + epsilon)
    weighted = grad * gains[0:1, :]
    inner = jnp.sum(weighted * stream, axis=1, keepdims=True)
    through = inv * weighted - stream * (inv * inv * inv * inner / D)
    by_feature(rows_two, (grad_mid_own[...] + through).astype(BF))
    back = narrow_swap(net, rows_two, back_two)
    step(back, wide_out, wide_qkv, wide_du)
    finish(wide_out, wide_du, wide_qkv)
    for copy in copies:
        copy.wait_recv()
    finish(back, output_rows)
    net.run([])


def closing(*refs):
    ins, outs = refs[:10], refs[10:]
    for rows, out in ((ins[0], outs[0]), (ins[1], outs[1])):
        halves = [rows[:, pl.ds(h * 32, 32), :].reshape(256, 320) for h in (0, 1)]
        out[...] = jnp.concatenate(halves, axis=0).astype(F32).T.astype(out.dtype)
    total = ins[2][0]
    for k in range(1, 16):
        total += ins[2][k]
    outs[2][...] = total[0:1, :320].reshape(320)
    outs[3][...] = total[1:2, :320].reshape(320)
    for source, out in zip(ins[3:], outs[4:]):
        out[...] = source[...]


def wide_sum_scratch(columns):
    return [
        pltpu.VMEM((4, 2, ROWS, columns), BF),
        pltpu.VMEM((3, 2, ROWS, columns), BF),
        pltpu.VMEM((ROWS, columns), BF),
    ]


def vmem():
    return pl.BlockSpec(memory_space=pltpu.VMEM)


def hbm():
    return pl.BlockSpec(memory_space=pl.ANY)


def exchange(name, number, body, ins, outs, scratch=()):
    def room_for(where, shape, dtype):
        return [pltpu.VMEM(shape, dtype)] if where == "vmem" else []

    in_rooms = [room_for(where, a.shape, a.dtype) for a, where in ins]
    out_rooms = [room_for(where, shape, dtype) for shape, dtype, where in outs]
    rooms = [r for part in (*in_rooms, *out_rooms) for r in part]

    def kernel(*refs):
        a, b = len(ins), len(ins) + len(outs)
        c = b + len(rooms)
        spare = iter(refs[b:c])
        net = Net(Place(), *refs[-3:])
        in_refs = [next(spare) if room else ref for ref, room in zip(refs[:a], in_rooms)]
        out_refs = [next(spare) if room else ref for ref, room in zip(refs[a:b], out_rooms)]
        net.loads = [net.keep(far, near) for far, near in zip(refs[:a], in_refs) if far is not near]
        body(net, in_refs, out_refs, refs[c:-3])
        for far, near in zip(refs[a:b], out_refs):
            if far is not near:
                net.keep(near, far)
        net.settle(*net.open)

    def spec(where):
        return pl.BlockSpec(memory_space=pltpu.SMEM) if where == "smem" else hbm()

    return pl.pallas_call(
        kernel,
        out_shape=[jax.ShapeDtypeStruct(shape, dtype) for shape, dtype, _ in outs],
        in_specs=[spec(where) for _, where in ins],
        out_specs=[hbm() for _ in outs],
        scratch_shapes=[
            *rooms,
            *scratch,
            pltpu.SemaphoreType.DMA((200,)),
            pltpu.SemaphoreType.DMA((200,)),
            pltpu.SemaphoreType.DMA((56,)),
        ],
        compiler_params=pltpu.CompilerParams(
            collective_id=number, has_side_effects=True, vmem_limit_bytes=60 * 2**20
        ),
        name=name,
    )(*[array for array, _ in ins])


def scaled_freqs():
    freqs = (rope_base ** (-2.0 * np.arange(HEAD // 2) / HEAD)).astype(np.float32)
    wavelen = (2.0 * math.pi / freqs).astype(np.float32)
    smooth = (long_wave / wavelen - 1.0) / 3.0
    blended = (1.0 - smooth) * freqs / rope_factor + smooth * freqs
    return np.where(
        wavelen < short_wave, freqs, np.where(wavelen > long_wave, freqs / rope_factor, blended)
    ).astype(np.float32)


def body(
    layer_input,
    gain_attn,
    w_query,
    w_key,
    w_value,
    w_out,
    gain_mlp,
    w_gate,
    w_up,
    w_down,
    doc_lengths,
    cotangent,
):
    def held(*shape, dtype=BF):
        return (shape, dtype, "vmem")

    def far(*shape, dtype=BF):
        return (shape, dtype, "hbm")

    def room(*shape, dtype=BF):
        return pltpu.VMEM(shape, dtype)

    def local(*arrays):
        return [(a, "vmem") for a in arrays]

    def remote(*arrays):
        return [(a, "hbm") for a in arrays]

    freqs = jnp.asarray(np.repeat(scaled_freqs()[:, None], 128, axis=1))
    slots = room(2, 12, OWN // 2, D)
    own = room(OWN, D, dtype=F32)
    (
        normed,
        w_qkv,
        w_o,
        cot,
        w_g,
        w_u,
        w_d,
        normed_two,
        queries,
        kv,
        lse,
        low,
        tables,
        attended,
        x_rows,
        mid,
        inverse,
        gains,
    ) = exchange(
        "attention",
        1,
        attention,
        remote(layer_input.T, cotangent.T)
        + local(w_query, w_key, w_value, w_out.T, w_gate, w_up, w_down.T, gain_attn, gain_mlp, freqs)
        + [(doc_lengths, "smem")],
        [
            far(TOK, D),
            far(D, 512),
            far(D, 384),
            far(D, TOK),
            far(D, PANEL),
            far(D, PANEL),
            far(D, PANEL),
            far(TOK, D),
            held(4, TILE, 4 * TILE),
            held(3 * TOK, 256),
            held(4, 1, 4 * TILE, dtype=F32),
            held(4, 1, 4 * TILE, dtype=jnp.int32),
            held(2, 40, TOK, dtype=F32),
            held(TOK, 320),
            held(OWN, D, dtype=F32),
            held(OWN, D, dtype=F32),
            held(OWN, 128, dtype=F32),
            held(8, D, dtype=F32),
        ],
        [
            room(ROWS, 512),
            room(ROWS, 384),
            room(8, 384, dtype=F32),
            room(8, 8, 384, dtype=F32),
            room(D, 512),
            room(D, 384),
            room(D, TOK),
            room(TOK, D),
            room(TOK, D),
            room(512, TOK, dtype=F32),
            room(TOK, D),
            slots,
            own,
            room(TILE, 3 * TOK),
            room(OWN, D),
        ],
    )
    grad_mid, grad_mid_own, down_part, grad_gate, grad_du, gain_two_part = exchange(
        "mlp",
        2,
        mlp,
        remote(normed_two, w_d, w_g, w_u, cot) + local(mid, inverse, gains),
        [
            far(TOK, D),
            held(OWN, D, dtype=F32),
            far(TOK, D),
            held(ROWS, PANEL, dtype=F32),
            far(D, 2 * PANEL),
            held(8, D, dtype=F32),
        ],
        [
            room(D, 2 * PANEL),
            room(D, PANEL),
            room(TOK, D),
            room(D, TOK),
            room(TOK, D),
            room(TOK, 2 * PANEL, dtype=F32),
            room(TOK, PANEL, dtype=F32),
            room(TOK, PANEL),
            room(TOK, 2 * PANEL),
            room(TOK, D),
            room(TOK, D),
            slots,
            own,
            *wide_sum_scratch(PANEL),
            room(OWN, D),
        ],
    )
    output_rows, grad_rows, gain_parts, grad_out, grad_query, grad_key, grad_value, grad_d, grad_up = exchange(
        "attention_back",
        3,
        attention_back,
        remote(grad_mid, normed, w_qkv, w_o, down_part, grad_du)
        + local(grad_mid_own, attended, queries, kv, lse, low, tables, mid, x_rows, gains, gain_two_part),
        [
            held(8, OWN, 320),
            held(8, OWN, 320),
            held(16, 8, 384, dtype=F32),
            held(ROWS, 320, dtype=F32),
            held(ROWS, 320, dtype=F32),
            held(ROWS, 80, dtype=F32),
            held(ROWS, 80, dtype=F32),
            held(ROWS, PANEL, dtype=F32),
            held(ROWS, PANEL, dtype=F32),
        ],
        [
            room(TOK, D),
            room(TOK, D),
            room(D, 512),
            room(D, 384),
            room(TOK, D),
            room(4, 2, ROWS, 2 * PANEL),
            room(4, TILE, 4 * TILE),
            room(TILE, 3 * TOK),
            room(3 * TOK, 256, dtype=F32),
            room(320, TOK, dtype=F32),
            slots,
            slots,
            own,
            own,
            room(2 * TOK, 256),
            room(2, TOK, 256),
            room(TOK, 320, dtype=F32),
            room(8, OWN, 320),
            room(8, OWN, 320),
            room(8, 8, 384, dtype=F32),
            room(8, 8, 384, dtype=F32),
            room(TOK, 512),
            *wide_sum_scratch(2 * PANEL),
            *wide_sum_scratch(384),
            *wide_sum_scratch(512),
            room(8, D, dtype=F32),
        ],
    )
    results = [
        ((320, TOK), BF),
        ((320, TOK), F32),
        ((320,), F32),
        ((320,), F32),
        ((ROWS, 320), F32),
        ((ROWS, 80), F32),
        ((ROWS, 80), F32),
        ((ROWS, 320), F32),
        ((ROWS, PANEL), F32),
        ((ROWS, PANEL), F32),
        ((ROWS, PANEL), F32),
    ]
    out = pl.pallas_call(
        closing,
        out_shape=[jax.ShapeDtypeStruct(shape, dtype) for shape, dtype in results],
        in_specs=[vmem()] * 10,
        out_specs=[vmem()] * 11,
        name="closing",
    )(output_rows, grad_rows, gain_parts, grad_query, grad_key, grad_value, grad_out, grad_gate, grad_up, grad_d)
    return (
        out[0].T,
        out[1].T,
        out[2],
        out[4],
        out[5],
        out[6],
        out[7].T,
        out[3],
        out[8],
        out[9],
        out[10].T,
    )


def solution(mesh):
    rows, columns = P("wide", "narrow"), P("narrow", "wide")
    return jax.shard_map(
        body,
        mesh=mesh,
        in_specs=(
            rows,
            P("narrow"),
            rows,
            rows,
            rows,
            columns,
            P("narrow"),
            rows,
            rows,
            columns,
            P(),
            rows,
        ),
        out_specs=(
            rows,
            rows,
            P("narrow"),
            rows,
            rows,
            rows,
            columns,
            P("narrow"),
            rows,
            rows,
            columns,
        ),
        check_vma=False,
    )
```
